32 devices in a mesh: rep: 4 (over z), exp: 8 (over y, x, core).
Axes of the slice: x: 2, y: 2, z: 4, core: 2. Of those that a mesh axis runs over, the one named last changes fastest.
Arguments:
- inputs: bfloat16 [32, 1024, 1024], P(('rep', 'exp')), may hold values from -6 to 6
- cotangent: bfloat16 [32, 1024, 1024], P(('rep', 'exp')), may hold values from -6 to 6
- token_ids: int32 [32, 1024], P(('rep', 'exp')), may hold values from 0 to 8007
- lengths: int32 [32], P(('rep', 'exp')), may hold values from 1 to 1024, 20480 in all
- hash_table: int32 [8008], replicated, may hold values from 0 to 7
- first_gain: float32 [1024], replicated, may hold values from 0.1 to 1.9
- first_shift: float32 [1024], replicated, may hold values from -3 to 3
- w_query: bfloat16 [1024, 1024], replicated, may hold values from -0.1875 to 0.1875
- w_key: bfloat16 [1024, 1024], replicated, may hold values from -0.1875 to 0.1875
- w_value: bfloat16 [1024, 1024], replicated, may hold values from -0.1875 to 0.1875
- w_output: bfloat16 [1024, 1024], replicated, may hold values from -0.75 to 0.75
- second_gain: float32 [1024], replicated, may hold values from 0.1 to 1.9
- second_shift: float32 [1024], replicated, may hold values from -3 to 3
- expert_in: bfloat16 [8, 4096, 1024], P('exp'), may hold values from -0.1875 to 0.1875
- expert_out: bfloat16 [8, 4096, 1024], P('exp'), may hold values from -0.09375 to 0.09375
Outputs:
- outputs: bfloat16 [32, 1024, 1024], P(('rep', 'exp'))
- grad_inputs: float32 [32, 1024, 1024], P(('rep', 'exp'))
- grad_first_gain: float32 [1024], P(('rep', 'exp'))
- grad_first_shift: float32 [1024], P(('rep', 'exp'))
- grad_query: float32 [1024, 1024], P(('rep', 'exp'))
- grad_key: float32 [1024, 1024], P(('rep', 'exp'))
- grad_value: float32 [1024, 1024], P(('rep', 'exp'))
- grad_output: float32 [1024, 1024], P(('rep', 'exp'))
- grad_second_gain: float32 [1024], P(('rep', 'exp'))
- grad_second_shift: float32 [1024], P(('rep', 'exp'))
- grad_expert_in: float32 [8, 4096, 1024], P('exp', 'rep')
- grad_expert_out: float32 [8, 4096, 1024], P('exp', 'rep')
The draws below stay inside these ranges and needn't reach their ends.
All inputs are finite; a program needn't handle non-finite values. No bound on the sum of `lengths` on one device may be relied on, other than what follows from the above.
Results may differ from the reference program's by a relative error of at most 0.012.
Values may be sent and summed in bfloat16 or wider, within the bound.
A program may use at most 448 MiB of HBM per device.

```python
import math
import jax
import jax.numpy as jnp
import numpy as np
from jax import lax

D = 1024
HEADS = 16
HEAD_DIM = 64
FF = 4096
VOCAB = 8008
SEQ_LEN = 1024
SEQ_DEV = 1
SEQS = 32
EXPERTS = 8
CAP = 128
DEVICES = 32


def set_ends(result, stream_key, smallest, high):
    index_at = [jax.random.randint(jax.random.fold_in(stream_key, axis), (), 0, length) for axis, length in enumerate(result.shape)]
    longest = result.shape.index(max(result.shape))
    neighbour = index_at[:longest] + [(index_at[longest] + 1) % result.shape[longest]] + index_at[longest + 1:]
    return result.at[tuple(index_at)].set(smallest).at[tuple(neighbour)].set(high)


def block_scale(own_key, extent, shards, low, top_value):
    def one(dim, shards_of):
        heights = jax.random.uniform(jax.random.fold_in(jax.random.fold_in(own_key, 6), dim), (shards_of,), jnp.float32, low / len(shards), top_value / len(shards))
        return jnp.repeat(jnp.exp(heights), extent[dim] // shards_of).reshape((-1,) + (1,) * (len(extent) - dim - 1))

    level = one(*shards[0])
    for cut in shards[1:]:
        level = level * one(*cut)
    return level


def rank_table(number_of, lean):
    loads = [(1 << 20) // math.isqrt(grade ** lean) + 1 for grade in range(1, number_of + 1)]
    deviation = 1 + sum(loads) // (1 << 30)
    return np.cumsum(np.array([max(1, weight // deviation) for weight in loads]))


def ranked_ids(stream_key, dims, number_of, lean):
    listing = rank_table(number_of, lean)
    pick = jax.random.randint(jax.random.fold_in(stream_key, 1), dims, 0, int(listing[number_of - 1]))
    standing = jnp.searchsorted(jnp.asarray(listing, jnp.int32), pick, side="right")
    return jax.random.permutation(jax.random.fold_in(stream_key, 2), number_of)[standing].astype(jnp.int32)


def profile(amount, total, limit, skew):
    loads = [(1 << 20) // math.isqrt(standing ** skew) + 1 for standing in range(2, amount + 1)]
    spare, holding = total - limit - (amount - 1), [1] * (amount - 1)
    while spare > 0:
        movable = [i for i in range(amount - 1) if holding[i] < limit]
        mass, remaining = sum([loads[i] for i in movable]), spare
        for i in movable:
            extra = min(limit - holding[i], max(1, remaining * loads[i] // mass), spare)
            holding[i] = holding[i] + extra
            spare = spare - extra
    return np.array([limit] + holding)


def uneven(rng, count, total, most, skew):
    if count == 2:
        one = jax.random.randint(rng, (), max(1, total - most), min(most, total - 1) + 1)
        return jnp.stack([one, total - one])
    sizes = jnp.asarray(profile(count, total, most, skew), jnp.int32)
    pairs = (count - 1) // 2
    donor, receiver = sizes[1:1 + 2 * pairs:2], sizes[2:2 + 2 * pairs:2]
    slack = jnp.minimum(donor - 1, most - receiver)
    shifted = jax.random.randint(jax.random.fold_in(rng, 1), (pairs,), 0, 1 << 20) % (slack + 1)
    sizes = sizes.at[1:1 + 2 * pairs:2].set(donor - shifted).at[2:2 + 2 * pairs:2].set(receiver + shifted)
    return sizes[jax.random.permutation(jax.random.fold_in(rng, 2), count)]


def centred(own_key, dims, scale, bound, cuts=(), kind=jnp.bfloat16):
    entries = jax.random.normal(own_key, dims, jnp.float32) * scale
    if len(cuts) > 0:
        entries = block_scale(own_key, dims, cuts, -0.22, 0.18) * entries
    return jnp.clip(entries, min=-bound, max=bound).astype(kind)


def setup_inputs(seed: int = 0) -> dict:
    key_of = jax.random.split(jax.random.key(seed), 16)
    inputs = centred(key_of[0], (SEQS, SEQ_LEN, D), 1.0, 6.0, ((0, 32),))
    cotangent = centred(key_of[1], (SEQS, SEQ_LEN, D), 1.0, 6.0, ((0, 32),))
    token_ids = set_ends(ranked_ids(key_of[2], (SEQS, SEQ_LEN), VOCAB, 2), jax.random.fold_in(key_of[2], 3), 0, VOCAB - 1).astype(jnp.int32)
    lengths = uneven(key_of[3], SEQS, SEQS * SEQ_LEN * 5 // 8, SEQ_LEN, 1).astype(jnp.int32)
    hash_table = set_ends(jax.random.randint(key_of[4], (VOCAB,), 0, EXPERTS), jax.random.fold_in(key_of[4], 1), 0, EXPERTS - 1).astype(jnp.int32)
    first_gain = jnp.clip(1.0 + 0.18 * jax.random.normal(key_of[5], (D,), jnp.float32), 0.1, 1.9)
    first_shift = centred(key_of[6], (D,), 0.5, 3.0, (), jnp.float32)
    w_query = centred(key_of[7], (D, D), D ** -0.5, 0.1875)
    w_key = centred(key_of[8], (D, D), D ** -0.5, 0.1875)
    w_value = centred(key_of[9], (D, D), D ** -0.5, 0.1875)
    w_output = centred(key_of[10], (D, D), (D // 16) ** -0.5, 0.75)
    second_gain = jnp.clip(1.0 + 0.18 * jax.random.normal(key_of[11], (D,), jnp.float32), 0.1, 1.9)
    second_shift = centred(key_of[12], (D,), 0.5, 3.0, (), jnp.float32)
    expert_in = centred(key_of[13], (EXPERTS, FF, D), D ** -0.5, 0.1875, ((0, 8),))
    expert_out = centred(key_of[14], (EXPERTS, FF, D), FF ** -0.5, 0.09375, ((0, 8),))
    return {"inputs": inputs, "cotangent": cotangent, "token_ids": token_ids, "lengths": lengths, "hash_table": hash_table, "first_gain": first_gain, "first_shift": first_shift, "w_query": w_query, "w_key": w_key, "w_value": w_value, "w_output": w_output, "second_gain": second_gain, "second_shift": second_shift, "expert_in": expert_in, "expert_out": expert_out}


@jax.custom_vjp
def low(v):
    return lax.optimization_barrier(v.astype(jnp.bfloat16)).astype(jnp.float32)

@jax.custom_vjp
def low_back(v):
    return v

def low_keep(v):
    return (low(v), None)

def low_pass(kept, grad):
    return (grad,)

def back_keep(v):
    return (v, None)

def back_low(kept, grad):
    return (low(grad),)
low.defvjp(low_keep, low_pass)
low_back.defvjp(back_keep, back_low)
PRECISE = lax.Precision.HIGHEST
epsilon = 1e-05

def high_dot(left, right):
    return jnp.dot(left, right, precision=PRECISE, preferred_element_type=jnp.float32)

def layer_norm(values_in, gain_vec, shift_vec):
    average = lax.optimization_barrier(jnp.mean(values_in, axis=-1, keepdims=True))
    centered = values_in - average
    spread = lax.optimization_barrier(jnp.mean(centered * centered, axis=-1, keepdims=True))
    return centered * lax.rsqrt(spread + epsilon) * gain_vec + shift_vec

def attention_seq(normed_seq, length, w_query, w_key, w_value):
    query_rows = low_back(low(high_dot(normed_seq, w_query))).reshape(SEQ_LEN, HEADS, HEAD_DIM)
    key_rows = low_back(low(high_dot(normed_seq, w_key))).reshape(SEQ_LEN, HEADS, HEAD_DIM)
    value_rows = low_back(low(high_dot(normed_seq, w_value))).reshape(SEQ_LEN, HEADS, HEAD_DIM)
    scores = low_back(HEAD_DIM ** (-0.5) * jnp.einsum('qhd,khd->hqk', query_rows, key_rows, precision=PRECISE))
    places = jnp.arange(SEQ_LEN, dtype=jnp.int32)
    allowed = (places[None, :] <= places[:, None]) & (places[None, :] < length.astype(jnp.int32))
    scores = jnp.where(allowed[None], scores, jnp.float32(-1e+30))
    highest = lax.optimization_barrier(jnp.max(scores, axis=2, keepdims=True))
    powers = jnp.exp(scores - highest)
    shares = powers / lax.optimization_barrier(jnp.sum(powers, axis=2, keepdims=True))
    mixed = jnp.einsum('hqk,khd->qhd', low(shares), value_rows, precision=PRECISE)
    return low_back(low(mixed.reshape(SEQ_LEN, D)))

def reference(inputs, cotangent, token_ids, lengths, hash_table, first_gain, first_shift, w_query, w_key, w_value, w_output, second_gain, second_shift, expert_in, expert_out):
    token_count = SEQS * SEQ_LEN
    dev_rows = SEQ_DEV * SEQ_LEN
    lengths_int = lengths.astype(jnp.int32)
    places = jnp.arange(SEQ_LEN, dtype=jnp.int32)
    valid = (places[None, :] < lengths_int[:, None]).reshape(token_count)
    expert_of = hash_table[token_ids.reshape(token_count).astype(jnp.int32)].astype(jnp.int32)
    expert_ids = jnp.arange(EXPERTS, dtype=jnp.int32)
    chosen = ((expert_of[:, None] == expert_ids[None, :]) & valid[:, None]).astype(jnp.int32)
    chosen_dev = chosen.reshape(DEVICES, dev_rows, EXPERTS)
    before = (jnp.cumsum(chosen_dev, axis=1).astype(jnp.int32) - chosen_dev).astype(jnp.int32)
    slot_of = lax.optimization_barrier(jnp.sum(before * chosen_dev, axis=2)).astype(jnp.int32).reshape(token_count)
    kept = valid & (slot_of < CAP)
    device_of = (jnp.arange(token_count, dtype=jnp.int32) // dev_rows).astype(jnp.int32)
    place = jnp.where(kept, (expert_of * DEVICES + device_of) * CAP + slot_of, EXPERTS * DEVICES * CAP).astype(jnp.int32)

    def forward(inputs_f, gain_one, shift_one, query_w, key_w, value_w, output_w, gain_two, shift_two, first_w, second_w):
        normed = low(layer_norm(inputs_f, gain_one, shift_one))

        def seq_step(carry, packed):
            normed_seq, length = packed
            return (carry, jax.checkpoint(attention_seq)(normed_seq, length, query_w, key_w, value_w))
        carry, mixed = lax.scan(seq_step, jnp.zeros((), jnp.float32), (normed.reshape(SEQS, SEQ_LEN, D), lengths_int))
        branch = low_back(high_dot(mixed.reshape(token_count, D), output_w))
        middle = inputs_f + branch
        sent = low_back(low(layer_norm(middle, gain_two, shift_two)))
        buffer = jnp.zeros((EXPERTS * DEVICES * CAP, D), jnp.float32).at[place].set(sent, mode='drop')

        def expert_step(packed):
            rows_in, weight_in, weight_out = packed
            hidden = low_back(jnp.einsum('rd,fd->rf', rows_in, weight_in, precision=PRECISE))
            activated = low(jax.nn.gelu(hidden, approximate=False))
            return low_back(low(high_dot(activated, weight_out)))
        results = lax.map(jax.checkpoint(expert_step), (buffer.reshape(EXPERTS, DEVICES * CAP, D), first_w, second_w))
        combined = results.reshape(EXPERTS * DEVICES * CAP, D).at[place].get(mode='fill', fill_value=0.0)
        return middle + combined
    primals = (inputs.reshape(token_count, D).astype(jnp.float32), first_gain.astype(jnp.float32), first_shift.astype(jnp.float32), w_query.astype(jnp.float32), w_key.astype(jnp.float32), w_value.astype(jnp.float32), w_output.astype(jnp.float32), second_gain.astype(jnp.float32), second_shift.astype(jnp.float32), expert_in.astype(jnp.float32), expert_out.astype(jnp.float32))
    outputs, pullback = jax.vjp(forward, *primals)
    grad_seed = cotangent.reshape(token_count, D).astype(jnp.float32) * valid[:, None].astype(jnp.float32)
    grads = pullback(grad_seed)
    return (outputs.reshape(SEQS, SEQ_LEN, D).astype(jnp.bfloat16), grads[0].reshape(SEQS, SEQ_LEN, D), grads[1], grads[2], grads[3], grads[4], grads[5], grads[6], grads[7], grads[8], grads[9], grads[10])
```

```python
import functools
import math

import jax
import jax.numpy as jnp
from jax import lax
from jax.experimental import pallas as pl
from jax.experimental.pallas import tpu as pltpu
from jax.sharding import PartitionSpec as P

HEAD_DIM = 64
PAIR = 2 * HEAD_DIM
MASKED = -1e30
epsilon = 1e-05
bf16, f32 = jnp.bfloat16, jnp.float32
VMEM_BYTES = 56 * 1024 * 1024


def params():
    return pltpu.CompilerParams(vmem_limit_bytes=VMEM_BYTES)


def shape(dims, kind):
    return jax.ShapeDtypeStruct(dims, kind)


def nn(left, right):
    return lax.dot_general(left, right, (((1,), (0,)), ((), ())), preferred_element_type=f32)


def nt(left, right):
    return lax.dot_general(left, right, (((1,), (1,)), ((), ())), preferred_element_type=f32)


def tn(left, right):
    return lax.dot_general(left, right, (((0,), (0,)), ((), ())), preferred_element_type=f32)


def whole(array):
    return pl.BlockSpec(array.shape, lambda *_: (0,) * array.ndim)


def row_spec(rows, width):
    return pl.BlockSpec((rows, width), lambda i: (i, 0))


def normalize(values):
    average = jnp.mean(values, axis=1, keepdims=True)
    centered = values - average
    spread = jnp.mean(centered * centered, axis=1, keepdims=True)
    inverse = lax.rsqrt(spread + epsilon)
    return centered * inverse, inverse


def norm_backward(grad_out, normal, inverse, gain):
    grad_normal = grad_out * gain
    inner = (
        grad_normal
        - jnp.mean(grad_normal, axis=1, keepdims=True)
        - normal * jnp.mean(grad_normal * normal, axis=1, keepdims=True)
    )
    return inner * inverse


def gelu_parts(hidden):
    share = 0.5 * (1.0 + lax.erf(hidden * (1.0 / math.sqrt(2.0))))
    slope = share + hidden * jnp.exp(-0.5 * hidden * hidden) * (1.0 / math.sqrt(2.0 * math.pi))
    return hidden * share, slope


def route_kernel(len_ref, ids_ref, table_ref, cot_ref, place_ref, send_ref, *, groups, capacity):
    seq_len = ids_ref.shape[1]
    slot_total = groups * capacity
    high_count, low_count = table_ref.shape
    ids = ids_ref[...]
    high, low = ids // low_count, ids % low_count
    high_pick = (
        lax.broadcasted_iota(jnp.int32, (high_count, seq_len), 0) == high
    ).astype(f32).astype(bf16)
    picked = tn(table_ref[...].astype(bf16), high_pick)
    low_pick = lax.broadcasted_iota(jnp.int32, (low_count, seq_len), 0) == low
    expert = jnp.sum(jnp.where(low_pick, picked, 0.0), axis=0, keepdims=True)
    valid = lax.broadcasted_iota(jnp.int32, (1, seq_len), 1) < len_ref[0]
    own = lax.broadcasted_iota(jnp.int32, (groups, seq_len), 0).astype(f32)
    chosen = jnp.where((own == expert) & valid, 1.0, 0.0)
    earlier = (
        lax.broadcasted_iota(jnp.int32, (seq_len, seq_len), 0)
        < lax.broadcasted_iota(jnp.int32, (seq_len, seq_len), 1)
    ).astype(f32).astype(bf16)
    before = nn(chosen.astype(bf16), earlier)
    slot = jnp.sum(before * chosen, axis=0, keepdims=True)
    place = jnp.where(valid & (slot < capacity), expert * capacity + slot, float(slot_total))
    place_ref[...] = jnp.broadcast_to(place, place_ref.shape)
    send_ref[...] = nn(slot_pick(place, slot_total), cot_ref[...]).astype(bf16)


def slot_pick(place_row, slot_total):
    slots = lax.broadcasted_iota(jnp.int32, (slot_total, place_row.shape[1]), 0).astype(f32)
    return jnp.where(slots == place_row, 1.0, 0.0).astype(bf16)


def row_pick(place_rows, slot_total):
    column = place_rows.T[:, :1]
    slots = lax.broadcasted_iota(jnp.int32, (column.shape[0], slot_total), 1).astype(f32)
    return jnp.where(slots == column, 1.0, 0.0).astype(bf16)


def route(lengths, ids, table, cotangent, groups, capacity):
    rows, width = cotangent.shape
    return pl.pallas_call(
        functools.partial(route_kernel, groups=groups, capacity=capacity),
        in_specs=[
            pl.BlockSpec(memory_space=pltpu.SMEM),
            whole(ids),
            whole(table),
            whole(cotangent),
        ],
        out_specs=[
            pl.BlockSpec((8, rows), lambda: (0, 0)),
            pl.BlockSpec((groups * capacity, width), lambda: (0, 0)),
        ],
        out_shape=[shape((8, rows), f32), shape((groups * capacity, width), bf16)],
        compiler_params=params(),
    )(lengths, ids, table, cotangent)


def project_kernel(x_ref, gain_ref, shift_ref, wq_ref, wk_ref, wv_ref, n_ref, q_ref, k_ref, v_ref):
    normal, _ = normalize(x_ref[...].astype(f32))
    normed = (normal * gain_ref[...] + shift_ref[...]).astype(bf16)
    n_ref[...] = normed
    q_ref[...] = nn(normed, wq_ref[...]).astype(bf16)
    k_ref[...] = nn(normed, wk_ref[...]).astype(bf16)
    v_ref[...] = nn(normed, wv_ref[...]).astype(bf16)


def project(x, gain, shift, wq, wk, wv, block=256):
    rows, width = x.shape
    return pl.pallas_call(
        project_kernel,
        grid=(rows // block,),
        in_specs=[row_spec(block, width)] + [whole(a) for a in (gain, shift, wq, wk, wv)],
        out_specs=[row_spec(block, width)] * 4,
        out_shape=[shape((rows, width), bf16)] * 4,
        compiler_params=params(),
    )(x, gain, shift, wq, wk, wv)


def head_parts(length, block, seq_len):
    lane = lax.broadcasted_iota(jnp.int32, (1, PAIR), 1)
    position = lax.broadcasted_iota(jnp.int32, (seq_len, 1), 0)
    bias = jnp.where(position < length, 0.0, MASKED).astype(bf16)
    down = lax.broadcasted_iota(jnp.int32, (block, block), 0)
    across = lax.broadcasted_iota(jnp.int32, (block, block), 1)
    return lane // HEAD_DIM, lane % HEAD_DIM == 0, bias, down <= across


def attend_kernel(len_ref, q_ref, k_ref, v_ref, o_ref, log_ref, *, block, pairs):
    seq_len = q_ref.shape[0]
    factor = HEAD_DIM**-0.5 * math.log2(math.e)
    half, first_lane, bias, causal = head_parts(len_ref[0], block, seq_len)
    zero = jnp.zeros_like(bias)
    keys, queries, values = [], [], []
    for pair in range(pairs):
        lanes = slice(pair * PAIR, (pair + 1) * PAIR)
        q, k = q_ref[:, lanes], k_ref[:, lanes]
        value_t = v_ref[:, lanes].T
        for h in range(2):
            spare = jnp.where(first_lane & (half != h), 1.0, 0.0).astype(bf16)
            keys.append(jnp.where(half == h, k, bias * spare))
            queries.append(jnp.where(half == h, q, spare))
            values.append(
                jnp.concatenate(
                    [value_t[h * HEAD_DIM : (h + 1) * HEAD_DIM], jnp.ones((16, seq_len), bf16)],
                    axis=0,
                )
            )
    order = [(h, j) for j in range(seq_len // block) for h in range(2 * pairs)]

    def score(h, j):
        end = (j + 1) * block
        return nt(keys[h][:end], queries[h][j * block : end])

    def soften(scores, j):
        last = jnp.where(causal, scores[j * block :], MASKED)
        scores = last if j == 0 else jnp.concatenate([scores[: j * block], last], axis=0)
        highest = jnp.max(scores, axis=0, keepdims=True) * factor
        return jnp.exp2(scores * factor - highest).astype(bf16), highest

    def finish(powers, highest, h, j):
        rows = slice(j * block, (j + 1) * block)
        total = nn(values[h][:, : (j + 1) * block], powers)
        summed = total[HEAD_DIM : HEAD_DIM + 1]
        mixed = total[:HEAD_DIM] * (1.0 / summed)
        o_ref[rows, h * HEAD_DIM : (h + 1) * HEAD_DIM] = mixed.T.astype(bf16)
        log_ref[h // 2, h % 2 : h % 2 + 1, rows] = highest + jnp.log2(summed)

    ahead = score(*order[0])
    behind = None
    for step, (h, j) in enumerate(order):
        scores = ahead
        if step + 1 < len(order):
            ahead = score(*order[step + 1])
        if behind is not None:
            finish(*behind, *order[step - 1])
        behind = soften(scores, j)
    finish(*behind, *order[-1])


def attend(lengths, q, k, v, block=256, pairs=2):
    rows, width = q.shape
    lanes = pl.BlockSpec((rows, pairs * PAIR), lambda i: (0, i))
    return pl.pallas_call(
        functools.partial(attend_kernel, block=block, pairs=pairs),
        grid=(width // (pairs * PAIR),),
        in_specs=[pl.BlockSpec(memory_space=pltpu.SMEM)] + [lanes] * 3,
        out_specs=[lanes, pl.BlockSpec((pairs, 2, rows), lambda i: (i, 0, 0))],
        out_shape=[shape((rows, width), bf16), shape((width // PAIR, 2, rows), f32)],
        compiler_params=params(),
    )(lengths, q, k, v)


def attend_back_kernel(
    len_ref, q_ref, k_ref, v_ref, o_ref, g_ref, log_ref, dq_ref, dk_ref, dv_ref, *, block, pairs
):
    seq_len = q_ref.shape[0]
    blocks = seq_len // block
    scale = HEAD_DIM**-0.5
    factor = scale * math.log2(math.e)
    half, first_lane, bias, causal = head_parts(len_ref[0], block, seq_len)
    zero = jnp.zeros_like(bias)
    keys, queries, values, keys_t, logs, deltas = [], [], [], [], [], []
    for pair in range(pairs):
        lanes = slice(pair * PAIR, (pair + 1) * PAIR)
        q, k, v = q_ref[:, lanes], k_ref[:, lanes], v_ref[:, lanes]
        key_t = k.T
        product = (g_ref[:, lanes].astype(f32) * o_ref[:, lanes].astype(f32)).T
        for h in range(2):
            rows = slice(h * HEAD_DIM, (h + 1) * HEAD_DIM)
            spare = jnp.where(first_lane & (half != h), 1.0, 0.0).astype(bf16)
            keys.append(jnp.where(half == h, k, bias * spare))
            queries.append(jnp.where(half == h, q, spare))
            values.append(jnp.where(half == h, v, zero))
            keys_t.append(key_t[rows])
            logs.append(log_ref[pair, h : h + 1, :])
            deltas.append(jnp.sum(product[rows], axis=0, keepdims=True))
    order = [(h, i) for i in range(blocks) for h in range(2 * pairs)]
    query_sums = [[None] * blocks for _ in range(2 * pairs)]
    kept = {}

    def lanes_of(h):
        return slice((h // 2) * PAIR, (h // 2 + 1) * PAIR)

    def products(h, i):
        rows = slice(i * block, (i + 1) * block)
        return (
            nt(keys[h][rows], queries[h][i * block :]),
            nt(values[h][rows], g_ref[i * block :, lanes_of(h)]),
        )

    def shares_of(scores, grad_shares, h, i):
        shares = jnp.exp2(scores * factor - logs[h][:, i * block :])
        first = jnp.where(causal, shares[:, :block], 0.0)
        if i + 1 < blocks:
            first = jnp.concatenate([first, shares[:, block:]], axis=1)
        grad_scores = first * (grad_shares - deltas[h][:, i * block :])
        return first.astype(bf16), grad_scores.astype(bf16)

    def finish(shares, grad_scores, h, i):
        rows, lanes = slice(i * block, (i + 1) * block), lanes_of(h)
        grad_v = nn(shares, g_ref[i * block :, lanes])
        grad_k = nn(grad_scores, q_ref[i * block :, lanes])
        part = nn(keys_t[h][:, rows], grad_scores)
        for j in range(i, blocks):
            term = part[:, (j - i) * block : (j - i + 1) * block]
            held = query_sums[h][j]
            query_sums[h][j] = term if held is None else held + term
        dq_ref[rows, h * HEAD_DIM : (h + 1) * HEAD_DIM] = (
            (query_sums[h][i] * scale).T.astype(bf16)
        )
        kept[h] = (grad_k, grad_v)
        if h % 2:
            other_k, other_v = kept[h - 1]
            dk_ref[rows, lanes] = (jnp.where(half == 0, other_k, grad_k) * scale).astype(bf16)
            dv_ref[rows, lanes] = jnp.where(half == 0, other_v, grad_v).astype(bf16)

    ahead = products(*order[0])
    behind = None
    for step, (h, i) in enumerate(order):
        now = ahead
        if step + 1 < len(order):
            ahead = products(*order[step + 1])
        if behind is not None:
            finish(*behind, *order[step - 1])
        behind = shares_of(*now, h, i)
    finish(*behind, *order[-1])


def attend_back(lengths, q, k, v, mixed, grad_mixed, logs, block=256, pairs=2):
    rows, width = q.shape
    lanes = pl.BlockSpec((rows, pairs * PAIR), lambda i: (0, i))
    return pl.pallas_call(
        functools.partial(attend_back_kernel, block=block, pairs=pairs),
        grid=(width // (pairs * PAIR),),
        in_specs=[pl.BlockSpec(memory_space=pltpu.SMEM)]
        + [lanes] * 5
        + [pl.BlockSpec((pairs, 2, rows), lambda i: (i, 0, 0))],
        out_specs=[lanes] * 3,
        out_shape=[shape((rows, width), bf16)] * 3,
        compiler_params=params(),
    )(lengths, q, k, v, mixed, grad_mixed, logs)


def middle_kernel(x_ref, m_ref, w_ref, gain_ref, shift_ref, place_ref, mid_ref, send_ref, sent):
    step = pl.program_id(0)
    block = x_ref.shape[0]
    middle = x_ref[...].astype(f32) + nn(m_ref[...], w_ref[...])
    mid_ref[...] = middle
    normal, _ = normalize(middle)
    sent[pl.ds(step * block, block)] = (normal * gain_ref[...] + shift_ref[...]).astype(bf16)

    @pl.when(step == pl.num_programs(0) - 1)
    def _():
        pick = slot_pick(place_ref[:1], send_ref.shape[0])
        send_ref[...] = nn(pick, sent[...]).astype(bf16)


def middle_and_send(x, mixed, w_output, gain, shift, place, slot_total, block=256):
    rows, width = x.shape
    blocked = row_spec(block, width)
    return pl.pallas_call(
        middle_kernel,
        grid=(rows // block,),
        in_specs=[blocked, blocked] + [whole(a) for a in (w_output, gain, shift, place)],
        out_specs=[blocked, pl.BlockSpec((slot_total, width), lambda i: (0, 0))],
        out_shape=[shape((rows, width), f32), shape((slot_total, width), bf16)],
        scratch_shapes=[pltpu.VMEM((rows, width), bf16)],
        compiler_params=params(),
    )(x, mixed, w_output, gain, shift, place)


def expert_kernel(x_ref, g_ref, in_ref, out_ref, slots_ref, act_ref, total, *, chunk):
    step = pl.program_id(0)
    count = x_ref.shape[0] // chunk

    @pl.when(step == 0)
    def _():
        total[...] = jnp.zeros_like(total)

    def rows(r):
        return slice(r * chunk, (r + 1) * chunk)

    def first(r):
        return nt(x_ref[rows(r)], in_ref[...]), nt(g_ref[rows(r)], out_ref[...])

    def second(hidden, grad_activated, r):
        activated, slope = gelu_parts(hidden)
        act_ref[rows(r)] = activated.astype(bf16)
        return (grad_activated * slope).astype(bf16)

    def third(grad_hidden, r):
        total[rows(r)] += nn(grad_hidden, in_ref[...])

    ahead, behind = first(0), None
    for r in range(count):
        now = ahead
        if r + 1 < count:
            ahead = first(r + 1)
        if behind is not None:
            third(behind, r - 1)
        behind = second(*now, r)
    third(behind, count - 1)

    @pl.when(step == pl.num_programs(0) - 1)
    def _():
        slots_ref[...] = total[...].astype(bf16)


def expert_main(x, g, w_in, w_out, block=1024, chunk=256):
    rows, width = x.shape
    units = w_in.shape[0]
    return pl.pallas_call(
        functools.partial(expert_kernel, chunk=chunk),
        grid=(units // block,),
        in_specs=[whole(x), whole(g), row_spec(block, width), row_spec(block, width)],
        out_specs=[whole(x), pl.BlockSpec((rows, block), lambda i: (0, i))],
        out_shape=[shape((rows, width), bf16), shape((rows, units), bf16)],
        scratch_shapes=[pltpu.VMEM((rows, width), f32)],
        compiler_params=params(),
    )(x, g, w_in, w_out)


def result_kernel(a_ref, w_ref, o_ref):
    o_ref[...] = nn(a_ref[...], w_ref[...]).astype(bf16)


def expert_result(activated, w_out, block=256):
    rows, units = activated.shape
    width = w_out.shape[1]
    return pl.pallas_call(
        result_kernel,
        grid=(rows // block,),
        in_specs=[row_spec(block, units), whole(w_out)],
        out_specs=row_spec(block, width),
        out_shape=shape((rows, width), bf16),
        compiler_params=params(),
    )(activated, w_out)


def expert_grad_kernel(*refs, count, sub):
    x_refs, g_refs = refs[:count], refs[count : 2 * count]
    in_ref, out_ref, gin_ref, gout_ref = refs[2 * count :]
    order = [(r, p) for r in range(in_ref.shape[0] // sub) for p in range(count)]
    sums = [None]

    def rows(r):
        return slice(r * sub, (r + 1) * sub)

    def first(r, p):
        return nt(in_ref[rows(r)], x_refs[p][...]), nt(out_ref[rows(r)], g_refs[p][...])

    def second(hidden, grad_activated):
        activated, slope = gelu_parts(hidden)
        return activated.astype(bf16), (grad_activated * slope).astype(bf16)

    def third(activated, grad_hidden, r, p):
        grad_out = nn(activated, g_refs[p][...])
        grad_in = nn(grad_hidden, x_refs[p][...])
        if p:
            grad_out += gout_ref[rows(r)]
            grad_in += gin_ref[rows(r)]
        gout_ref[rows(r)] = grad_out
        gin_ref[rows(r)] = grad_in

    ahead, behind = first(*order[0]), None
    for step in range(len(order)):
        now = ahead
        if step + 1 < len(order):
            ahead = first(*order[step + 1])
        if behind is not None:
            third(*behind, *order[step - 1])
        behind = second(*now)
    third(*behind, *order[-1])


def expert_grads(xs, gs, w_in, w_out, block=256, sub=256):
    units, width = w_in.shape
    blocked = row_spec(block, width)
    return pl.pallas_call(
        functools.partial(expert_grad_kernel, count=len(xs), sub=sub),
        grid=(units // block,),
        in_specs=[whole(a) for a in (*xs, *gs)] + [blocked, blocked],
        out_specs=[blocked, blocked],
        out_shape=[shape((units, width), f32)] * 2,
        compiler_params=params(),
    )(*xs, *gs, w_in, w_out)


def back_kernel(
    back_ref, place_ref, mid_ref, cot_ref, len_ref, gain_ref, w_ref,
    gmid_ref, branch_ref, gmix_ref, ggain_ref, gshift_ref,
):
    step = pl.program_id(0)
    block = mid_ref.shape[0]
    grad_sent = nn(row_pick(place_ref[...], back_ref.shape[0]), back_ref[...])
    normal, inverse = normalize(mid_ref[...])
    position = step * block + lax.broadcasted_iota(jnp.int32, (block, 1), 0)
    grad_final = jnp.where(position < len_ref[0], cot_ref[...].astype(f32), 0.0)
    grad_middle = grad_final + norm_backward(grad_sent, normal, inverse, gain_ref[...])
    gmid_ref[...] = grad_middle
    branch = grad_middle.astype(bf16)
    branch_ref[...] = branch
    gmix_ref[...] = nt(branch, w_ref[...]).astype(bf16)

    @pl.when(step == 0)
    def _():
        ggain_ref[...] = jnp.zeros_like(ggain_ref)
        gshift_ref[...] = jnp.zeros_like(gshift_ref)

    ggain_ref[...] += jnp.sum(grad_sent * normal, axis=0, keepdims=True)
    gshift_ref[...] += jnp.sum(grad_sent, axis=0, keepdims=True)


def middle_back(back, place, middle, cotangent, lengths, gain, w_output, block=256):
    rows, width = middle.shape
    blocked = row_spec(block, width)
    vector = pl.BlockSpec((1, width), lambda i: (0, 0))
    return pl.pallas_call(
        back_kernel,
        grid=(rows // block,),
        in_specs=[
            whole(back),
            pl.BlockSpec((8, block), lambda i: (0, i)),
            blocked,
            blocked,
            pl.BlockSpec(memory_space=pltpu.SMEM),
            whole(gain),
            whole(w_output),
        ],
        out_specs=[blocked, blocked, blocked, vector, vector],
        out_shape=[shape((rows, width), f32)]
        + [shape((rows, width), bf16)] * 2
        + [shape((1, width), f32)] * 2,
        compiler_params=params(),
    )(back, place, middle, cotangent, lengths, gain, w_output)


def weight_grad_kernel(a_ref, *refs, kind):
    count = len(refs) // 2
    left = a_ref[...].T
    for b_ref, o_ref in zip(refs[:count], refs[count:]):
        o_ref[...] = nn(left, b_ref[...]).astype(kind)


def weight_grads(a, bs, block=256, kind=bf16):
    rows, width = a.shape
    out_width = bs[0].shape[1]
    return pl.pallas_call(
        functools.partial(weight_grad_kernel, kind=kind),
        grid=(width // block,),
        in_specs=[pl.BlockSpec((rows, block), lambda i: (0, i))] + [whole(b) for b in bs],
        out_specs=[row_spec(block, out_width)] * len(bs),
        out_shape=[shape((width, out_width), kind)] * len(bs),
        compiler_params=params(),
    )(a, *bs)


def input_back_kernel(
    gq_ref, gk_ref, gv_ref, wq_ref, wk_ref, wv_ref, x_ref, gmid_ref, gain_ref,
    gin_ref, ggain_ref, gshift_ref,
):
    grad_normed = (
        nt(gq_ref[...], wq_ref[...]) + nt(gk_ref[...], wk_ref[...]) + nt(gv_ref[...], wv_ref[...])
    )
    normal, inverse = normalize(x_ref[...].astype(f32))
    gin_ref[...] = gmid_ref[...] + norm_backward(grad_normed, normal, inverse, gain_ref[...])

    @pl.when(pl.program_id(0) == 0)
    def _():
        ggain_ref[...] = jnp.zeros_like(ggain_ref)
        gshift_ref[...] = jnp.zeros_like(gshift_ref)

    ggain_ref[...] += jnp.sum(grad_normed * normal, axis=0, keepdims=True)
    gshift_ref[...] += jnp.sum(grad_normed, axis=0, keepdims=True)


def input_back(gq, gk, gv, wq, wk, wv, x, grad_middle, gain, block=256):
    rows, width = x.shape
    blocked = row_spec(block, width)
    vector = pl.BlockSpec((1, width), lambda i: (0, 0))
    return pl.pallas_call(
        input_back_kernel,
        grid=(rows // block,),
        in_specs=[blocked] * 3 + [whole(w) for w in (wq, wk, wv)] + [blocked, blocked, whole(gain)],
        out_specs=[blocked, vector, vector],
        out_shape=[shape((rows, width), f32)] + [shape((1, width), f32)] * 2,
        compiler_params=params(),
    )(gq, gk, gv, wq, wk, wv, x, grad_middle, gain)


def output_kernel(back_ref, place_ref, mid_ref, o_ref):
    combined = nn(row_pick(place_ref[...], back_ref.shape[0]), back_ref[...])
    o_ref[...] = (mid_ref[...] + combined).astype(bf16)


def combine(back, place, middle, block=256):
    rows, width = middle.shape
    return pl.pallas_call(
        output_kernel,
        grid=(rows // block,),
        in_specs=[
            whole(back),
            pl.BlockSpec((8, block), lambda i: (0, i)),
            row_spec(block, width),
        ],
        out_specs=row_spec(block, width),
        out_shape=shape((rows, width), bf16),
        compiler_params=params(),
    )(back, place, middle)


def body(
    inputs,
    cotangent,
    token_ids,
    lengths,
    hash_table,
    first_gain,
    first_shift,
    w_query,
    w_key,
    w_value,
    w_output,
    second_gain,
    second_shift,
    expert_in,
    expert_out,
):
    seq_count, seq_len, width = inputs.shape
    rows = seq_count * seq_len
    groups = lax.axis_size("exp")
    copies = lax.axis_size("rep")
    place_z = lax.axis_index("rep")
    capacity = rows // groups
    slot_total = groups * capacity
    x = inputs.reshape(rows, width)
    cot = cotangent.reshape(rows, width)
    gain_one, shift_one, gain_two, shift_two = (
        v.reshape(1, width) for v in (first_gain, first_shift, second_gain, second_shift)
    )
    table_rows = -(-hash_table.shape[0] // (8 * 128)) * 8
    table = jnp.pad(hash_table, (0, table_rows * 128 - hash_table.shape[0]))
    table = table.reshape(table_rows, 128)

    def exchange(array):
        return lax.all_to_all(
            array.reshape(groups, capacity, width), "exp", split_axis=0, concat_axis=0, tiled=True
        ).reshape(slot_total, width)

    def spread(array):
        up, down = [array], [array]
        for _ in range(copies - 1):
            up.append(lax.ppermute(up[-1], "rep", [(i, i + 1) for i in range(copies - 1)]))
            down.append(lax.ppermute(down[-1], "rep", [(i + 1, i) for i in range(copies - 1)]))
        return [
            jnp.where(place_z >= step, up[step], down[copies - step]) for step in range(1, copies)
        ]

    place, grad_send = route(
        lengths, token_ids.reshape(1, rows), table, cot, groups, capacity
    )
    grad_arrived = exchange(grad_send)
    normed, q, k, v = project(x, gain_one, shift_one, w_query, w_key, w_value)
    mixed, logs = attend(lengths, q, k, v)
    middle, send_rows = middle_and_send(x, mixed, w_output, gain_two, shift_two, place, slot_total)
    arrived = exchange(send_rows)
    grad_slots, activated = expert_main(arrived, grad_arrived, expert_in[0], expert_out[0])
    grad_back = exchange(grad_slots)
    returned = exchange(expert_result(activated, expert_out[0]))
    grad_middle, branch, grad_mixed, grad_second_gain, grad_second_shift = middle_back(
        grad_back, place, middle, cot, lengths, gain_two, w_output
    )
    (grad_w_output,) = weight_grads(mixed, [branch])
    gq, gk, gv = attend_back(lengths, q, k, v, mixed, grad_mixed, logs)
    grad_qkv = weight_grads(normed, [gq, gk, gv])
    grad_inputs, grad_first_gain, grad_first_shift = input_back(
        gq, gk, gv, w_query, w_key, w_value, x, grad_middle, gain_one
    )
    outputs = combine(returned, place, middle)

    share = expert_in.shape[1] // copies
    shares = [
        lax.dynamic_slice_in_dim(w[0], place_z * share, share, axis=0)
        for w in (expert_in, expert_out)
    ]
    grad_expert_in, grad_expert_out = expert_grads(
        [arrived, *spread(arrived)], [grad_arrived, *spread(grad_arrived)], *shares
    )

    def scatter(arrays):
        devices = groups * copies
        parts = [a.reshape(copies, groups, width // devices, width) for a in arrays]
        joined = jnp.concatenate(parts, axis=2)
        joined = lax.psum_scatter(
            joined.transpose(1, 0, 2, 3), "exp", scatter_dimension=0, tiled=True
        )
        joined = lax.psum_scatter(joined[0], "rep", scatter_dimension=0, tiled=True)[0]
        return [part.astype(f32) for part in jnp.split(joined, len(arrays), axis=0)]

    (dense_output,) = scatter([grad_w_output])
    dense_query, dense_key, dense_value = scatter(grad_qkv)
    vectors = jnp.concatenate(
        [grad_first_gain, grad_first_shift, grad_second_gain, grad_second_shift], axis=0
    )
    vectors = lax.psum(vectors, ("rep", "exp"))
    part = width // (groups * copies)
    mine = (place_z * groups + lax.axis_index("exp")) * part
    vectors = lax.dynamic_slice_in_dim(vectors, mine, part, axis=1)
    return (
        outputs.reshape(seq_count, seq_len, width),
        grad_inputs.reshape(seq_count, seq_len, width),
        vectors[0],
        vectors[1],
        dense_query,
        dense_key,
        dense_value,
        dense_output,
        vectors[2],
        vectors[3],
        grad_expert_in[None],
        grad_expert_out[None],
    )


def solution(mesh):
    both = ("rep", "exp")
    placed = (
        P(both, None, None),
        P(both, None, None),
        P(both, None),
        P(both),
    ) + (P(),) * 9 + (P("exp", None, None),) * 2
    return jax.shard_map(
        body,
        mesh=mesh,
        in_specs=placed,
        out_specs=(
            P(both, None, None),
            P(both, None, None),
            P(both),
            P(both),
            P(both, None),
            P(both, None),
            P(both, None),
            P(both, None),
            P(both),
            P(both),
            P("exp", "rep", None),
            P("exp", "rep", None),
        ),
        check_vma=False,
    )
```

```python
import functools
import math

import jax
import jax.numpy as jnp
from jax import lax
from jax.experimental import pallas as pl
from jax.experimental.pallas import tpu as pltpu
from jax.sharding import PartitionSpec as P

HEAD_DIM = 64
PAIR = 2 * HEAD_DIM
MASKED = -1e30
epsilon = 1e-05
bf16, f32 = jnp.bfloat16, jnp.float32
MESH = pl.DeviceIdType.MESH
ANY = pl.BlockSpec(memory_space=pl.ANY)
VMEM_BYTES = 56 * 1024 * 1024
PARTS = 4


def params(collective_id=None):
    if collective_id is None:
        return pltpu.CompilerParams(vmem_limit_bytes=VMEM_BYTES)
    return pltpu.CompilerParams(
        vmem_limit_bytes=VMEM_BYTES, collective_id=collective_id, has_side_effects=True
    )


def launch(kernel, operands, in_specs, micros, after=(), collective_id=None, **options):
    count = len(operands)

    def run(*refs):
        kernel(*refs[:count], *refs[count + len(after) :])

    return pl.pallas_call(
        run,
        in_specs=list(in_specs) + [pl.BlockSpec(memory_space=pl.ANY)] * len(after),
        compiler_params=params(collective_id),
        cost_estimate=pl.CostEstimate(
            flops=int(micros * 1.1e9), bytes_accessed=int(micros * 3.5e6), transcendentals=0
        ),
        **options,
    )(*operands, *after)


def greet(groups):
    me = lax.axis_index("exp")
    barrier = pltpu.get_barrier_semaphore()

    def tell(step, carry):
        peer = lax.rem(me + step, groups)
        pl.semaphore_signal(barrier, inc=1, device_id={"exp": peer}, device_id_type=MESH)
        return carry

    lax.fori_loop(1, groups, tell, 0)
    pl.semaphore_wait(barrier, groups - 1)


def remote(source, target, send_sem, recv_sem, peer):
    return pltpu.make_async_remote_copy(
        src_ref=source,
        dst_ref=target,
        send_sem=send_sem,
        recv_sem=recv_sem,
        device_id={"exp": peer},
        device_id_type=MESH,
    )


def start_exchange(send_ref, recv_ref, send_sems, recv_sems):
    groups = send_ref.shape[0]
    me = lax.axis_index("exp")
    greet(groups)
    pltpu.make_async_copy(send_ref.at[me], recv_ref.at[me], recv_sems.at[me]).start()

    def send(step, carry):
        peer = lax.rem(me + step, groups)
        remote(send_ref.at[peer], recv_ref.at[me], send_sems.at[peer], recv_sems.at[me], peer).start()
        return carry

    lax.fori_loop(1, groups, send, 0)


def finish_exchange(send_ref, recv_ref, send_sems, recv_sems):
    groups = send_ref.shape[0]
    me = lax.axis_index("exp")
    pltpu.make_async_copy(send_ref.at[me], recv_ref.at[me], recv_sems.at[me]).wait()

    def wait(step, carry):
        peer = lax.rem(me + step, groups)
        copy = remote(send_ref.at[peer], recv_ref.at[peer], send_sems.at[peer], recv_sems.at[peer], peer)
        copy.wait_send()
        copy.wait_recv()
        return carry

    lax.fori_loop(1, groups, wait, 0)


def exchange_scratch(send):
    return [pltpu.SemaphoreType.DMA((send.shape[0],))] * 2


def shape(dims, kind):
    return jax.ShapeDtypeStruct(dims, kind)


def nn(left, right):
    return lax.dot_general(left, right, (((1,), (0,)), ((), ())), preferred_element_type=f32)


def nt(left, right):
    return lax.dot_general(left, right, (((1,), (1,)), ((), ())), preferred_element_type=f32)


def tn(left, right):
    return lax.dot_general(left, right, (((0,), (0,)), ((), ())), preferred_element_type=f32)


def whole(array):
    return pl.BlockSpec(array.shape, lambda *_: (0,) * array.ndim)


def row_spec(rows, width):
    return pl.BlockSpec((rows, width), lambda i: (i, 0))


def normalize(values):
    average = jnp.mean(values, axis=1, keepdims=True)
    centered = values - average
    spread = jnp.mean(centered * centered, axis=1, keepdims=True)
    inverse = lax.rsqrt(spread + epsilon)
    return centered * inverse, inverse


def norm_backward(grad_out, normal, inverse, gain):
    grad_normal = grad_out * gain
    inner = (
        grad_normal
        - jnp.mean(grad_normal, axis=1, keepdims=True)
        - normal * jnp.mean(grad_normal * normal, axis=1, keepdims=True)
    )
    return inner * inverse


def gelu_parts(hidden):
    share = 0.5 * (1.0 + lax.erf(hidden * (1.0 / math.sqrt(2.0))))
    slope = share + hidden * jnp.exp(-0.5 * hidden * hidden) * (1.0 / math.sqrt(2.0 * math.pi))
    return hidden * share, slope


def route_kernel(
    len_ref, ids_ref, table_ref, cot_ref, place_ref, send_a_ref, send_b_ref, *, groups, capacity
):
    seq_len = ids_ref.shape[1]
    slot_total = groups * capacity
    high_count, low_count = table_ref.shape
    ids = ids_ref[...]
    high, low = ids // low_count, ids % low_count
    high_pick = (
        lax.broadcasted_iota(jnp.int32, (high_count, seq_len), 0) == high
    ).astype(f32).astype(bf16)
    picked = tn(table_ref[...].astype(bf16), high_pick)
    low_pick = lax.broadcasted_iota(jnp.int32, (low_count, seq_len), 0) == low
    expert = jnp.sum(jnp.where(low_pick, picked, 0.0), axis=0, keepdims=True)
    valid = lax.broadcasted_iota(jnp.int32, (1, seq_len), 1) < len_ref[0]
    own = lax.broadcasted_iota(jnp.int32, (groups, seq_len), 0).astype(f32)
    chosen = jnp.where((own == expert) & valid, 1.0, 0.0)
    earlier = (
        lax.broadcasted_iota(jnp.int32, (seq_len, seq_len), 0)
        < lax.broadcasted_iota(jnp.int32, (seq_len, seq_len), 1)
    ).astype(f32).astype(bf16)
    before = nn(chosen.astype(bf16), earlier)
    slot = jnp.sum(before * chosen, axis=0, keepdims=True)
    place = jnp.where(valid & (slot < capacity), expert * capacity + slot, float(slot_total))
    place_ref[...] = jnp.broadcast_to(place, place_ref.shape)
    sent = nn(slot_pick(place, slot_total), cot_ref[...]).astype(bf16)
    sent = sent.reshape(groups, capacity, sent.shape[1])
    half = capacity // 2
    send_a_ref[...] = sent[:, :half]
    send_b_ref[...] = sent[:, half:]


def slot_pick(place_row, slot_total):
    slots = lax.broadcasted_iota(jnp.int32, (slot_total, place_row.shape[1]), 0).astype(f32)
    return jnp.where(slots == place_row, 1.0, 0.0).astype(bf16)


def row_pick(place_rows, slot_total):
    column = place_rows.T[:, :1]
    slots = lax.broadcasted_iota(jnp.int32, (column.shape[0], slot_total), 1).astype(f32)
    return jnp.where(slots == column, 1.0, 0.0).astype(bf16)


def route(lengths, ids, table, cotangent, groups, capacity, after=()):
    rows, width = cotangent.shape
    return launch(
        functools.partial(route_kernel, groups=groups, capacity=capacity),
        (lengths, ids, table, cotangent,),
        [
            pl.BlockSpec(memory_space=pltpu.SMEM),
            whole(ids),
            whole(table),
            whole(cotangent),
        ],
        10,
        after,
        out_specs=[pl.BlockSpec((8, rows), lambda: (0, 0))]
        + [pl.BlockSpec((groups, capacity // 2, width), lambda: (0, 0, 0))] * 2,
        out_shape=[shape((8, rows), f32)] + [shape((groups, capacity // 2, width), bf16)] * 2,
    )


def project_kernel(
    x_ref, gain_ref, shift_ref, wq_ref, wk_ref, wv_ref, send_ref,
    n_ref, q_ref, k_ref, v_ref, recv_ref, send_sems, recv_sems,
):
    @pl.when(pl.program_id(0) == 0)
    def _():
        start_exchange(send_ref, recv_ref, send_sems, recv_sems)

    normal, _ = normalize(x_ref[...].astype(f32))
    normed = (normal * gain_ref[...] + shift_ref[...]).astype(bf16)
    n_ref[...] = normed
    q_ref[...] = nn(normed, wq_ref[...]).astype(bf16)
    k_ref[...] = nn(normed, wk_ref[...]).astype(bf16)
    v_ref[...] = nn(normed, wv_ref[...]).astype(bf16)

    @pl.when(pl.program_id(0) == pl.num_programs(0) - 1)
    def _():
        finish_exchange(send_ref, recv_ref, send_sems, recv_sems)


def project(x, gain, shift, wq, wk, wv, send, block=256, after=()):
    rows, width = x.shape
    return launch(
        project_kernel,
        (x, gain, shift, wq, wk, wv, send),
        [row_spec(block, width)] + [whole(a) for a in (gain, shift, wq, wk, wv)] + [ANY],
        16,
        after,
        collective_id=2,
        grid=(rows // block,),
        out_specs=[row_spec(block, width)] * 4 + [ANY],
        out_shape=[shape((rows, width), bf16)] * 4 + [shape(send.shape, bf16)],
        scratch_shapes=exchange_scratch(send),
    )


def head_parts(length, block, seq_len):
    lane = lax.broadcasted_iota(jnp.int32, (1, PAIR), 1)
    position = lax.broadcasted_iota(jnp.int32, (seq_len, 1), 0)
    bias = jnp.where(position < length, 0.0, MASKED).astype(bf16)
    down = lax.broadcasted_iota(jnp.int32, (block, block), 0)
    across = lax.broadcasted_iota(jnp.int32, (block, block), 1)
    return lane // HEAD_DIM, lane % HEAD_DIM == 0, bias, down <= across


def attend_kernel(
    len_ref, q_ref, k_ref, v_ref, send_ref, o_ref, log_ref, recv_ref, send_sems, recv_sems,
    *, block, pairs,
):
    @pl.when(pl.program_id(0) == 0)
    def _():
        start_exchange(send_ref, recv_ref, send_sems, recv_sems)

    seq_len = q_ref.shape[0]
    factor = HEAD_DIM**-0.5 * math.log2(math.e)
    half, first_lane, bias, causal = head_parts(len_ref[0], block, seq_len)
    zero = jnp.zeros_like(bias)
    keys, queries, values = [], [], []
    for pair in range(pairs):
        lanes = slice(pair * PAIR, (pair + 1) * PAIR)
        q, k = q_ref[:, lanes], k_ref[:, lanes]
        value_t = v_ref[:, lanes].T
        for h in range(2):
            spare = jnp.where(first_lane & (half != h), 1.0, 0.0).astype(bf16)
            keys.append(jnp.where(half == h, k, bias * spare))
            queries.append(jnp.where(half == h, q, spare))
            values.append(
                jnp.concatenate(
                    [value_t[h * HEAD_DIM : (h + 1) * HEAD_DIM], jnp.ones((16, seq_len), bf16)],
                    axis=0,
                )
            )
    order = [(h, j) for j in range(seq_len // block) for h in range(2 * pairs)]

    def score(h, j):
        end = (j + 1) * block
        return nt(keys[h][:end], queries[h][j * block : end])

    def soften(scores, j):
        last = jnp.where(causal, scores[j * block :], MASKED)
        scores = last if j == 0 else jnp.concatenate([scores[: j * block], last], axis=0)
        highest = jnp.max(scores, axis=0, keepdims=True) * factor
        return jnp.exp2(scores * factor - highest).astype(bf16), highest

    def finish(powers, highest, h, j):
        rows = slice(j * block, (j + 1) * block)
        total = nn(values[h][:, : (j + 1) * block], powers)
        summed = total[HEAD_DIM : HEAD_DIM + 1]
        mixed = total[:HEAD_DIM] * (1.0 / summed)
        o_ref[rows, h * HEAD_DIM : (h + 1) * HEAD_DIM] = mixed.T.astype(bf16)
        log_ref[h // 2, h % 2 : h % 2 + 1, rows] = highest + jnp.log2(summed)

    ahead = score(*order[0])
    behind = None
    for step, (h, j) in enumerate(order):
        scores = ahead
        if step + 1 < len(order):
            ahead = score(*order[step + 1])
        if behind is not None:
            finish(*behind, *order[step - 1])
        behind = soften(scores, j)
    finish(*behind, *order[-1])

    @pl.when(pl.program_id(0) == pl.num_programs(0) - 1)
    def _():
        finish_exchange(send_ref, recv_ref, send_sems, recv_sems)


def attend(lengths, q, k, v, send, block=256, pairs=2, after=()):
    rows, width = q.shape
    lanes = pl.BlockSpec((rows, pairs * PAIR), lambda i: (0, i))
    return launch(
        functools.partial(attend_kernel, block=block, pairs=pairs),
        (lengths, q, k, v, send),
        [pl.BlockSpec(memory_space=pltpu.SMEM)] + [lanes] * 3 + [ANY],
        24,
        after,
        collective_id=0,
        grid=(width // (pairs * PAIR),),
        out_specs=[lanes, pl.BlockSpec((pairs, 2, rows), lambda i: (i, 0, 0)), ANY],
        out_shape=[
            shape((rows, width), bf16),
            shape((width // PAIR, 2, rows), f32),
            shape(send.shape, bf16),
        ],
        scratch_shapes=exchange_scratch(send),
    )


def attend_back_kernel(
    len_ref, q_ref, k_ref, v_ref, o_ref, g_ref, log_ref, send_ref,
    dq_ref, dk_ref, dv_ref, recv_ref, send_sems, recv_sems, *, block, pairs,
):
    @pl.when(pl.program_id(0) == 0)
    def _():
        start_exchange(send_ref, recv_ref, send_sems, recv_sems)

    seq_len = q_ref.shape[0]
    blocks = seq_len // block
    scale = HEAD_DIM**-0.5
    factor = scale * math.log2(math.e)
    half, first_lane, bias, causal = head_parts(len_ref[0], block, seq_len)
    zero = jnp.zeros_like(bias)
    keys, queries, values, keys_t, logs, deltas = [], [], [], [], [], []
    for pair in range(pairs):
        lanes = slice(pair * PAIR, (pair + 1) * PAIR)
        q, k, v = q_ref[:, lanes], k_ref[:, lanes], v_ref[:, lanes]
        key_t = k.T
        product = (g_ref[:, lanes].astype(f32) * o_ref[:, lanes].astype(f32)).T
        for h in range(2):
            rows = slice(h * HEAD_DIM, (h + 1) * HEAD_DIM)
            spare = jnp.where(first_lane & (half != h), 1.0, 0.0).astype(bf16)
            keys.append(jnp.where(half == h, k, bias * spare))
            queries.append(jnp.where(half == h, q, spare))
            values.append(jnp.where(half == h, v, zero))
            keys_t.append(key_t[rows])
            logs.append(log_ref[pair, h : h + 1, :])
            deltas.append(jnp.sum(product[rows], axis=0, keepdims=True))
    order = [(h, i) for i in range(blocks) for h in range(2 * pairs)]
    query_sums = [[None] * blocks for _ in range(2 * pairs)]
    kept = {}

    def lanes_of(h):
        return slice((h // 2) * PAIR, (h // 2 + 1) * PAIR)

    def products(h, i):
        rows = slice(i * block, (i + 1) * block)
        return (
            nt(keys[h][rows], queries[h][i * block :]),
            nt(values[h][rows], g_ref[i * block :, lanes_of(h)]),
        )

    def shares_of(scores, grad_shares, h, i):
        shares = jnp.exp2(scores * factor - logs[h][:, i * block :])
        first = jnp.where(causal, shares[:, :block], 0.0)
        if i + 1 < blocks:
            first = jnp.concatenate([first, shares[:, block:]], axis=1)
        grad_scores = first * (grad_shares - deltas[h][:, i * block :])
        return first.astype(bf16), grad_scores.astype(bf16)

    def finish(shares, grad_scores, h, i):
        rows, lanes = slice(i * block, (i + 1) * block), lanes_of(h)
        grad_v = nn(shares, g_ref[i * block :, lanes])
        grad_k = nn(grad_scores, q_ref[i * block :, lanes])
        part = nn(keys_t[h][:, rows], grad_scores)
        for j in range(i, blocks):
            term = part[:, (j - i) * block : (j - i + 1) * block]
            held = query_sums[h][j]
            query_sums[h][j] = term if held is None else held + term
        dq_ref[rows, h * HEAD_DIM : (h + 1) * HEAD_DIM] = (
            (query_sums[h][i] * scale).T.astype(bf16)
        )
        kept[h] = (grad_k, grad_v)
        if h % 2:
            other_k, other_v = kept[h - 1]
            dk_ref[rows, lanes] = (jnp.where(half == 0, other_k, grad_k) * scale).astype(bf16)
            dv_ref[rows, lanes] = jnp.where(half == 0, other_v, grad_v).astype(bf16)

    ahead = products(*order[0])
    behind = None
    for step, (h, i) in enumerate(order):
        now = ahead
        if step + 1 < len(order):
            ahead = products(*order[step + 1])
        if behind is not None:
            finish(*behind, *order[step - 1])
        behind = shares_of(*now, h, i)
    finish(*behind, *order[-1])

    @pl.when(pl.program_id(0) == pl.num_programs(0) - 1)
    def _():
        finish_exchange(send_ref, recv_ref, send_sems, recv_sems)


def attend_back(lengths, q, k, v, mixed, grad_mixed, logs, send, block=256, pairs=2, after=()):
    rows, width = q.shape
    lanes = pl.BlockSpec((rows, pairs * PAIR), lambda i: (0, i))
    return launch(
        functools.partial(attend_back_kernel, block=block, pairs=pairs),
        (lengths, q, k, v, mixed, grad_mixed, logs, send),
        [pl.BlockSpec(memory_space=pltpu.SMEM)]
        + [lanes] * 5
        + [pl.BlockSpec((pairs, 2, rows), lambda i: (i, 0, 0)), ANY],
        31,
        after,
        collective_id=3,
        grid=(width // (pairs * PAIR),),
        out_specs=[lanes] * 3 + [ANY],
        out_shape=[shape((rows, width), bf16)] * 3 + [shape(send.shape, bf16)],
        scratch_shapes=exchange_scratch(send),
    )


def middle_kernel(x_ref, m_ref, w_ref, gain_ref, shift_ref, place_ref, mid_ref, send_ref, sent):
    step = pl.program_id(0)
    block = x_ref.shape[0]
    middle = x_ref[...].astype(f32) + nn(m_ref[...], w_ref[...])
    mid_ref[...] = middle
    normal, _ = normalize(middle)
    sent[pl.ds(step * block, block)] = (normal * gain_ref[...] + shift_ref[...]).astype(bf16)

    @pl.when(step == pl.num_programs(0) - 1)
    def _():
        pick = slot_pick(place_ref[:1], send_ref.shape[0])
        send_ref[...] = nn(pick, sent[...]).astype(bf16)


def middle_and_send(x, mixed, w_output, gain, shift, place, slot_total, block=256, after=()):
    rows, width = x.shape
    blocked = row_spec(block, width)
    return launch(
        middle_kernel,
        (x, mixed, w_output, gain, shift, place,),
        [blocked, blocked] + [whole(a) for a in (w_output, gain, shift, place)],
        10,
        after,
        grid=(rows // block,),
        out_specs=[blocked, pl.BlockSpec((slot_total, width), lambda i: (0, 0))],
        out_shape=[shape((rows, width), f32), shape((slot_total, width), bf16)],
        scratch_shapes=[pltpu.VMEM((rows, width), bf16)],
    )


def expert_kernel(
    send_ref, ga_ref, gb_ref, in_hbm, out_hbm, back_ref, result_ref, arrived_0, arrived_1, arrived_2, arrived_3,
    w_in, w_out, x_all, slots_all, result_all,
    w_sems, send_sems, recv_sems, back_sems, back_recv, keep_sems,
    *, rows, sub,
):
    groups, capacity, width = send_ref.shape
    me = lax.axis_index("exp")
    units = w_in.shape[0]
    sources = rows // capacity
    blocks = groups // sources
    mine = me // sources
    count = units // sub
    loads = []
    for f in range(count):
        part = slice(f * sub, (f + 1) * sub)
        pair = [
            pltpu.make_async_copy(hbm.at[part], vmem.at[part], w_sems.at[n, f])
            for n, (hbm, vmem) in enumerate(((in_hbm, w_in), (out_hbm, w_out)))
        ]
        for load in pair:
            load.start()
        loads.append(pair)
    greet(groups)

    def send_block(j, carry):
        block = lax.rem(mine + blocks - j, blocks)

        def send(i, inner):
            peer = block * sources + i

            @pl.when(peer == me)
            def _():
                pltpu.make_async_copy(send_ref.at[me], x_all.at[me], recv_sems.at[me]).start()

            @pl.when(peer != me)
            def _():
                remote(
                    send_ref.at[peer], x_all.at[me], send_sems.at[peer], recv_sems.at[me], peer
                ).start()

            return inner

        return lax.fori_loop(0, sources, send, carry)

    lax.fori_loop(0, blocks, send_block, 0)

    def work(j, wait_weights):
        first_source = lax.rem(mine + j, blocks) * sources

        def arrive(i, carry):
            source = first_source + i
            remote(
                send_ref.at[source], x_all.at[source], send_sems.at[source], recv_sems.at[source],
                source,
            ).wait_recv()
            return carry

        lax.fori_loop(0, sources, arrive, 0)
        x = x_all[pl.ds(first_source, sources)].reshape(rows, width)
        halves = [ref[pl.ds(first_source, sources)] for ref in (ga_ref, gb_ref)]
        g = jnp.concatenate(halves, axis=1).reshape(rows, width)

        def first(f):
            part = slice(f * sub, (f + 1) * sub)
            if wait_weights:
                for load in loads[f]:
                    load.wait()
            return nt(x, w_in[part]), nt(g, w_out[part])

        def second(hidden, grad_activated):
            activated, slope = gelu_parts(hidden)
            return activated.astype(bf16), (grad_activated * slope).astype(bf16)

        sums = None
        ahead, behind = first(0), None
        for f in range(count + 1):
            now = ahead
            if f + 1 < count:
                ahead = first(f + 1)
            if behind is not None:
                part = slice((f - 1) * sub, f * sub)
                terms = nn(behind[1], w_in[part]), nn(behind[0], w_out[part])
                sums = terms if sums is None else (sums[0] + terms[0], sums[1] + terms[1])
            if f < count:
                behind = second(*now)
        dims = (sources, capacity, width)
        slots_all[pl.ds(first_source, sources)] = sums[0].astype(bf16).reshape(dims)
        result_all[pl.ds(first_source, sources)] = sums[1].astype(bf16).reshape(dims)

        def answer(i, carry):
            peer = first_source + i

            @pl.when(peer == me)
            def _():
                pltpu.make_async_copy(slots_all.at[me], back_ref.at[me], back_recv.at[me]).start()

            @pl.when(peer != me)
            def _():
                remote(
                    slots_all.at[peer], back_ref.at[me], back_sems.at[peer], back_recv.at[me], peer
                ).start()

            return carry

        lax.fori_loop(0, sources, answer, 0)

    work(0, True)

    def later(j, carry):
        work(j, False)
        return carry

    lax.fori_loop(1, blocks, later, 0)
    keeps = [pltpu.make_async_copy(result_all, result_ref, keep_sems.at[0])]
    for n, ref in enumerate((arrived_0, arrived_1, arrived_2, arrived_3)):
        side, half = groups // 2, capacity // 2
        part = x_all.at[pl.ds((n % 2) * side, side), pl.ds((n // 2) * half, half)]
        keeps.append(pltpu.make_async_copy(part, ref, keep_sems.at[n + 1]))
    for keep in keeps:
        keep.start()

    def close(peer, carry):
        @pl.when(peer != me)
        def _():
            remote(
                send_ref.at[peer], x_all.at[peer], send_sems.at[peer], recv_sems.at[peer], peer
            ).wait_send()
            remote(
                slots_all.at[peer], back_ref.at[peer], back_sems.at[peer], back_recv.at[peer], peer
            ).wait_send()

        remote(
            slots_all.at[peer], back_ref.at[peer], back_sems.at[peer], back_recv.at[peer], peer
        ).wait_recv()
        return carry

    lax.fori_loop(0, groups, close, 0)
    for keep in keeps:
        keep.wait()


def expert_main(send, ga, gb, w_in, w_out, rows=256, sub=512, after=()):
    groups, capacity, width = send.shape
    units = w_in.shape[0]
    dma = pltpu.SemaphoreType.DMA
    part = (groups // 2, capacity // 2, width)
    return launch(
        functools.partial(expert_kernel, rows=rows, sub=sub),
        (send, ga, gb, w_in, w_out),
        [ANY, whole(ga), whole(gb), ANY, ANY],
        60,
        after,
        collective_id=1,
        out_specs=[ANY] * 6,
        out_shape=[shape(send.shape, bf16)] * 2 + [shape(part, bf16)] * 4,
        scratch_shapes=[pltpu.VMEM((units, width), bf16)] * 2
        + [pltpu.VMEM(send.shape, bf16)] * 3
        + [dma((2, units // sub))]
        + [dma((groups,))] * 4
        + [dma((5,))],
    )


def expert_grad_kernel(x_ref, g_ref, in_ref, out_ref, *refs, sub, more):
    gin_ref, gout_ref = refs[-2:]
    copies = x_ref.shape[0]
    order = [(r, p) for r in range(in_ref.shape[0] // sub) for p in range(copies)]

    def rows(r):
        return slice(r * sub, (r + 1) * sub)

    def first(r, p):
        return nt(in_ref[rows(r)], x_ref[p]), nt(out_ref[rows(r)], g_ref[p])

    def second(hidden, grad_activated):
        activated, slope = gelu_parts(hidden)
        return activated.astype(bf16), (grad_activated * slope).astype(bf16)

    def third(activated, grad_hidden, r, p):
        grad_out = nn(activated, g_ref[p])
        grad_in = nn(grad_hidden, x_ref[p])
        if p or more:
            before_in, before_out = (gin_ref, gout_ref) if p else refs[:2]
            grad_in += before_in[rows(r)]
            grad_out += before_out[rows(r)]
        gout_ref[rows(r)] = grad_out
        gin_ref[rows(r)] = grad_in

    ahead, behind = first(*order[0]), None
    for step in range(len(order)):
        now = ahead
        if step + 1 < len(order):
            ahead = first(*order[step + 1])
        if behind is not None:
            third(*behind, *order[step - 1])
        behind = second(*now)
    third(*behind, *order[-1])


def expert_grads(x, g, side, w_in, w_out, before=(), block=256, sub=256, after=()):
    copies, groups, half, width = g.shape
    part_rows = groups * half // 2
    x, g = (a.reshape(copies, -1, width) for a in (x, g))
    units = w_in.shape[0]
    blocked = row_spec(block, width)
    return launch(
        functools.partial(expert_grad_kernel, sub=sub, more=len(before) > 0),
        (x, g, w_in, w_out, *before),
        [
            whole(x),
            pl.BlockSpec((copies, part_rows, width), lambda i: (0, side, 0)),
            blocked,
            blocked,
        ]
        + [blocked] * len(before),
        14,
        after,
        grid=(units // block,),
        out_specs=[blocked, blocked],
        out_shape=[shape((units, width), f32)] * 2,
        input_output_aliases={4: 0, 5: 1} if before else {},
    )


def back_kernel(
    back_ref, place_ref, mid_ref, cot_ref, len_ref, gain_ref, w_ref,
    gmid_ref, branch_ref, gmix_ref, ggain_ref, gshift_ref,
):
    step = pl.program_id(0)
    block = mid_ref.shape[0]
    grad_sent = nn(row_pick(place_ref[...], back_ref.shape[0]), back_ref[...])
    normal, inverse = normalize(mid_ref[...])
    position = step * block + lax.broadcasted_iota(jnp.int32, (block, 1), 0)
    grad_final = jnp.where(position < len_ref[0], cot_ref[...].astype(f32), 0.0)
    grad_middle = grad_final + norm_backward(grad_sent, normal, inverse, gain_ref[...])
    gmid_ref[...] = grad_middle
    branch = grad_middle.astype(bf16)
    branch_ref[...] = branch
    gmix_ref[...] = nt(branch, w_ref[...]).astype(bf16)

    @pl.when(step == 0)
    def _():
        ggain_ref[...] = jnp.zeros_like(ggain_ref)
        gshift_ref[...] = jnp.zeros_like(gshift_ref)

    ggain_ref[...] += jnp.sum(grad_sent * normal, axis=0, keepdims=True)
    gshift_ref[...] += jnp.sum(grad_sent, axis=0, keepdims=True)


def middle_back(back, place, middle, cotangent, lengths, gain, w_output, block=256, after=()):
    rows, width = middle.shape
    blocked = row_spec(block, width)
    vector = pl.BlockSpec((1, width), lambda i: (0, 0))
    return launch(
        back_kernel,
        (back, place, middle, cotangent, lengths, gain, w_output,),
        [
            whole(back),
            pl.BlockSpec((8, block), lambda i: (0, i)),
            blocked,
            blocked,
            pl.BlockSpec(memory_space=pltpu.SMEM),
            whole(gain),
            whole(w_output),
        ],
        12,
        after,
        grid=(rows // block,),
        out_specs=[blocked, blocked, blocked, vector, vector],
        out_shape=[shape((rows, width), f32)]
        + [shape((rows, width), bf16)] * 2
        + [shape((1, width), f32)] * 2,
    )


def weight_grad_kernel(a_ref, *refs):
    left = a_ref[...].T
    groups, _, _, share, width = refs[-1].shape
    for n, b_ref in enumerate(refs[:-1]):
        product = nn(left, b_ref[...]).reshape(groups, share, width)
        refs[-1][:, 0, n] = product.astype(bf16)


def weight_grads(a, bs, groups, copies, after=()):
    rows, width = a.shape
    out_width = bs[0].shape[1]
    block = width // copies
    dims = (groups, copies, len(bs), block // groups, out_width)
    return launch(
        weight_grad_kernel,
        (a, *bs),
        [pl.BlockSpec((rows, block), lambda i: (0, i))] + [whole(b) for b in bs],
        4 * len(bs),
        after,
        grid=(copies,),
        out_specs=pl.BlockSpec((groups, 1) + dims[2:], lambda i: (0, i, 0, 0, 0)),
        out_shape=shape(dims, bf16),
    )


def near_add_kernel(*refs):
    o_ref = refs[-1]
    start = 0
    for ref in refs[:-1]:
        count = ref.shape[2]
        o_ref[0, start : start + count] = jnp.sum(ref[:, 0].astype(f32), axis=0).astype(bf16)
        start += count


def near_add(parts, after=()):
    copies = parts[0].shape[1]
    dims = (sum(p.shape[2] for p in parts),) + parts[0].shape[3:]

    def spec(p):
        return pl.BlockSpec(p.shape[:1] + (1,) + p.shape[2:], lambda i: (0, i, 0, 0, 0))

    return launch(
        near_add_kernel,
        tuple(parts),
        [spec(p) for p in parts],
        6,
        after,
        grid=(copies,),
        out_specs=pl.BlockSpec((1,) + dims, lambda i: (i, 0, 0, 0)),
        out_shape=shape((copies,) + dims, bf16),
    )


def input_back_kernel(
    gq_ref, gk_ref, gv_ref, wq_ref, wk_ref, wv_ref, x_ref, gmid_ref, gain_ref,
    gin_ref, ggain_ref, gshift_ref,
):
    grad_normed = (
        nt(gq_ref[...], wq_ref[...]) + nt(gk_ref[...], wk_ref[...]) + nt(gv_ref[...], wv_ref[...])
    )
    normal, inverse = normalize(x_ref[...].astype(f32))
    gin_ref[...] = gmid_ref[...] + norm_backward(grad_normed, normal, inverse, gain_ref[...])

    @pl.when(pl.program_id(0) == 0)
    def _():
        ggain_ref[...] = jnp.zeros_like(ggain_ref)
        gshift_ref[...] = jnp.zeros_like(gshift_ref)

    ggain_ref[...] += jnp.sum(grad_normed * normal, axis=0, keepdims=True)
    gshift_ref[...] += jnp.sum(grad_normed, axis=0, keepdims=True)


def input_back(gq, gk, gv, wq, wk, wv, x, grad_middle, gain, block=256, after=()):
    rows, width = x.shape
    blocked = row_spec(block, width)
    vector = pl.BlockSpec((1, width), lambda i: (0, 0))
    return launch(
        input_back_kernel,
        (gq, gk, gv, wq, wk, wv, x, grad_middle, gain,),
        [blocked] * 3 + [whole(w) for w in (wq, wk, wv)] + [blocked, blocked, whole(gain)],
        14,
        after,
        grid=(rows // block,),
        out_specs=[blocked, vector, vector],
        out_shape=[shape((rows, width), f32)] + [shape((1, width), f32)] * 2,
    )


def output_kernel(back_ref, place_ref, mid_ref, o_ref):
    combined = nn(row_pick(place_ref[...], back_ref.shape[0]), back_ref[...])
    o_ref[...] = (mid_ref[...] + combined).astype(bf16)


def combine(back, place, middle, block=256, after=()):
    rows, width = middle.shape
    return launch(
        output_kernel,
        (back, place, middle,),
        [
            whole(back),
            pl.BlockSpec((8, block), lambda i: (0, i)),
            row_spec(block, width),
        ],
        7,
        after,
        grid=(rows // block,),
        out_specs=row_spec(block, width),
        out_shape=shape((rows, width), bf16),
    )


def body(
    inputs,
    cotangent,
    token_ids,
    lengths,
    hash_table,
    first_gain,
    first_shift,
    w_query,
    w_key,
    w_value,
    w_output,
    second_gain,
    second_shift,
    expert_in,
    expert_out,
):
    seq_count, seq_len, width = inputs.shape
    rows = seq_count * seq_len
    groups = lax.axis_size("exp")
    copies = lax.axis_size("rep")
    place_z = lax.axis_index("rep")
    capacity = rows // groups
    slot_total = groups * capacity
    x = inputs.reshape(rows, width)
    cot = cotangent.reshape(rows, width)
    gain_one, shift_one, gain_two, shift_two = (
        v.reshape(1, width) for v in (first_gain, first_shift, second_gain, second_shift)
    )
    table_rows = -(-hash_table.shape[0] // (8 * 128)) * 8
    table = jnp.pad(hash_table, (0, table_rows * 128 - hash_table.shape[0]))
    table = table.reshape(table_rows, 128)

    def gather(array):
        return lax.all_gather(array, "rep", axis=0, tiled=False)

    def near(parts):
        return lax.all_to_all(parts, "exp", split_axis=0, concat_axis=0, tiled=True)

    def far_sum(parts):
        far = lax.all_to_all(parts, "rep", split_axis=0, concat_axis=0, tiled=True)
        return jnp.sum(far.astype(f32), axis=0)

    place, send_a, send_b = route(lengths, token_ids.reshape(1, rows), table, cot, groups, capacity)
    normed, q, k, v, cot_a = project(x, gain_one, shift_one, w_query, w_key, w_value, send_a)
    cots_a = gather(cot_a)
    mixed, logs, cot_b = attend(lengths, q, k, v, send_b)
    cots_b = gather(cot_b)
    middle, send_rows = middle_and_send(
        x, mixed, w_output, gain_two, shift_two, place, slot_total, after=(cot_b,)
    )
    grad_back, result, *arrived = expert_main(
        send_rows.reshape(groups, capacity, width), cot_a, cot_b, expert_in[0], expert_out[0]
    )
    sent = [gather(a) for a in arrived]
    grad_middle, branch, grad_mixed, grad_second_gain, grad_second_shift = middle_back(
        grad_back.reshape(slot_total, width), place, middle, cot, lengths, gain_two, w_output
    )
    parts_output = weight_grads(mixed, [branch], groups, copies, after=(cots_a,))
    gq, gk, gv, returned = attend_back(
        lengths, q, k, v, mixed, grad_mixed, logs, result, after=(parts_output,)
    )
    near_output = near(parts_output)
    grad_inputs, grad_first_gain, grad_first_shift = input_back(
        gq, gk, gv, w_query, w_key, w_value, x, grad_middle, gain_one
    )
    parts_qkv = weight_grads(normed, [gq, gk, gv], groups, copies, after=(grad_first_gain,))
    near_qkv = near(parts_qkv)
    outputs = combine(
        returned.reshape(slot_total, width), place, middle, after=(parts_qkv, cots_b)
    )
    devices = groups * copies
    vectors = jnp.concatenate(
        [grad_first_gain, grad_first_shift, grad_second_gain, grad_second_shift], axis=0
    )
    vectors = vectors.reshape(4, devices, width // devices).transpose(1, 0, 2)
    vectors = lax.all_to_all(vectors, ("rep", "exp"), split_axis=0, concat_axis=0, tiled=True)
    vectors = jnp.sum(vectors, axis=0)

    share = expert_in.shape[1] // copies
    shares = [
        lax.dynamic_slice_in_dim(w[0], place_z * share, share, axis=0)
        for w in (expert_in, expert_out)
    ]
    sums = expert_grads(sent[0], cots_a, 0, *shares, after=(outputs,))
    sums = expert_grads(sent[1], cots_a, 1, *shares, before=sums)
    near_all = near_add([near_output, near_qkv], after=(sums[0],))
    dense = far_sum(near_all)
    sums = expert_grads(sent[2], cots_b, 0, *shares, before=sums, after=(near_all, vectors))
    sums = expert_grads(sent[3], cots_b, 1, *shares, before=sums, after=(dense,))
    grad_expert_in, grad_expert_out = sums
    dense_output, dense_query, dense_key, dense_value = dense
    return (
        outputs.reshape(seq_count, seq_len, width),
        grad_inputs.reshape(seq_count, seq_len, width),
        vectors[0],
        vectors[1],
        dense_query,
        dense_key,
        dense_value,
        dense_output,
        vectors[2],
        vectors[3],
        grad_expert_in[None],
        grad_expert_out[None],
    )


def solution(mesh):
    both = ("rep", "exp")
    placed = (
        P(both, None, None),
        P(both, None, None),
        P(both, None),
        P(both),
    ) + (P(),) * 9 + (P("exp", None, None),) * 2
    return jax.shard_map(
        body,
        mesh=mesh,
        in_specs=placed,
        out_specs=(
            P(both, None, None),
            P(both, None, None),
            P(both),
            P(both),
            P(both, None),
            P(both, None),
            P(both, None),
            P(both, None),
            P(both),
            P(both),
            P("exp", "rep", None),
            P("exp", "rep", None),
        ),
        check_vma=False,
    )
```

```python
import functools
import math

import jax
import jax.numpy as jnp
from jax import lax
from jax.experimental import pallas as pl
from jax.experimental.pallas import tpu as pltpu
from jax.sharding import PartitionSpec as P

HEAD_DIM = 64
PAIR = 2 * HEAD_DIM
MASKED = -1e30
epsilon = 1e-05
bf16, f32 = jnp.bfloat16, jnp.float32
MESH = pl.DeviceIdType.MESH
ANY = pl.BlockSpec(memory_space=pl.ANY)
VMEM_BYTES = 56 * 1024 * 1024
PARTS = 4


def params(collective_id=None):
    if collective_id is None:
        return pltpu.CompilerParams(vmem_limit_bytes=VMEM_BYTES)
    return pltpu.CompilerParams(
        vmem_limit_bytes=VMEM_BYTES, collective_id=collective_id, has_side_effects=True
    )


def launch(kernel, operands, in_specs, micros, after=(), collective_id=None, **options):
    count = len(operands)

    def run(*refs):
        kernel(*refs[:count], *refs[count + len(after) :])

    return pl.pallas_call(
        run,
        in_specs=list(in_specs) + [pl.BlockSpec(memory_space=pl.ANY)] * len(after),
        compiler_params=params(collective_id),
        cost_estimate=pl.CostEstimate(
            flops=int(1e9), bytes_accessed=int(1e6), transcendentals=0
        ),
        **options,
    )(*operands, *after)


def at_rep(place):
    return {"rep": place}


def at_exp(place):
    return {"exp": place}


def greet(*axes):
    barrier = pltpu.get_barrier_semaphore()
    count = 0
    for axis in axes or ("exp",):
        size, me = lax.axis_size(axis), lax.axis_index(axis)

        def tell(step, carry, axis=axis, size=size, me=me):
            peer = lax.rem(me + step, size)
            pl.semaphore_signal(barrier, inc=1, device_id={axis: peer}, device_id_type=MESH)
            return carry

        lax.fori_loop(1, size, tell, 0)
        count += size - 1
    pl.semaphore_wait(barrier, count)


def push(source, target, send_sem, recv_sem, device):
    return pltpu.make_async_remote_copy(
        src_ref=source,
        dst_ref=target,
        send_sem=send_sem,
        recv_sem=recv_sem,
        device_id=device,
        device_id_type=MESH,
    )


def remote(source, target, send_sem, recv_sem, peer):
    return push(source, target, send_sem, recv_sem, at_exp(peer))


def start_exchange(send_ref, recv_ref, send_sems, recv_sems, stride=1, axis="exp"):
    groups = send_ref.shape[0]
    me = lax.axis_index(axis)
    mine = me // stride
    pltpu.make_async_copy(send_ref.at[mine], recv_ref.at[mine], recv_sems.at[mine]).start()

    def send(step, carry):
        entry = lax.rem(mine + step, groups)
        peer = entry * stride + lax.rem(me, stride)
        push(
            send_ref.at[entry], recv_ref.at[mine], send_sems.at[entry], recv_sems.at[mine], {axis: peer}
        ).start()
        return carry

    lax.fori_loop(1, groups, send, 0)


def finish_exchange(send_ref, recv_ref, send_sems, recv_sems, stride=1, axis="exp"):
    groups = send_ref.shape[0]
    me = lax.axis_index(axis)
    mine = me // stride
    pltpu.make_async_copy(send_ref.at[mine], recv_ref.at[mine], recv_sems.at[mine]).wait()

    def wait(step, carry):
        entry = lax.rem(mine + step, groups)
        peer = entry * stride + lax.rem(me, stride)
        copy = push(
            send_ref.at[entry], recv_ref.at[entry], send_sems.at[entry], recv_sems.at[entry], {axis: peer}
        )
        copy.wait_send()
        copy.wait_recv()
        return carry

    lax.fori_loop(1, groups, wait, 0)


def remote(source, target, send_sem, recv_sem, peer):
    return push(source, target, send_sem, recv_sem, at_exp(peer))


def exchange_planes(send_ref, recv_ref, send_sems, recv_sems, begin):
    copies, groups = send_ref.shape[:2]
    z, me = lax.axis_index("rep"), lax.axis_index("exp")

    def shift(n, carry):
        plane = lax.rem(z + n + 1, copies)
        own = pltpu.make_async_copy(send_ref.at[plane, me], recv_ref.at[n, me], recv_sems.at[n, me])
        own.start() if begin else own.wait()

        def one(step, inner):
            peer = lax.rem(me + step, groups)
            entry = me if begin else peer
            copy = push(
                send_ref.at[plane, peer], recv_ref.at[n, entry],
                send_sems.at[n, peer], recv_sems.at[n, entry], at_exp(peer),
            )
            if begin:
                copy.start()
            else:
                copy.wait_send()
                copy.wait_recv()
            return inner

        return lax.fori_loop(1, groups, one, carry)

    lax.fori_loop(0, copies - 1, shift, 0)


def exchange_scratch(groups):
    return [pltpu.SemaphoreType.DMA((groups,))] * 2


def shape(dims, kind):
    return jax.ShapeDtypeStruct(dims, kind)


def nn(left, right):
    return lax.dot_general(left, right, (((1,), (0,)), ((), ())), preferred_element_type=f32)


def nt(left, right):
    return lax.dot_general(left, right, (((1,), (1,)), ((), ())), preferred_element_type=f32)


def tn(left, right):
    return lax.dot_general(left, right, (((0,), (0,)), ((), ())), preferred_element_type=f32)


def whole(array):
    return pl.BlockSpec(array.shape, lambda *_: (0,) * array.ndim)


def row_spec(rows, width):
    return pl.BlockSpec((rows, width), lambda i: (i, 0))


def normalize(values):
    average = jnp.mean(values, axis=1, keepdims=True)
    centered = values - average
    spread = jnp.mean(centered * centered, axis=1, keepdims=True)
    inverse = lax.rsqrt(spread + epsilon)
    return centered * inverse, inverse


def norm_backward(grad_out, normal, inverse, gain):
    grad_normal = grad_out * gain
    inner = (
        grad_normal
        - jnp.mean(grad_normal, axis=1, keepdims=True)
        - normal * jnp.mean(grad_normal * normal, axis=1, keepdims=True)
    )
    return inner * inverse


def gelu_parts(hidden):
    share = 0.5 * (1.0 + lax.erf(hidden * (1.0 / math.sqrt(2.0))))
    slope = share + hidden * jnp.exp(-0.5 * hidden * hidden) * (1.0 / math.sqrt(2.0 * math.pi))
    return hidden * share, slope


def route_kernel(
    len_ref, ids_ref, table_ref, cot_ref, place_ref, send_ref, first_ref, *, groups, capacity
):
    seq_len = ids_ref.shape[1]
    slot_total = groups * capacity
    high_count, low_count = table_ref.shape
    ids = ids_ref[...]
    high, low = ids // low_count, ids % low_count
    high_pick = (
        lax.broadcasted_iota(jnp.int32, (high_count, seq_len), 0) == high
    ).astype(f32).astype(bf16)
    picked = tn(table_ref[...].astype(bf16), high_pick)
    low_pick = lax.broadcasted_iota(jnp.int32, (low_count, seq_len), 0) == low
    expert = jnp.sum(jnp.where(low_pick, picked, 0.0), axis=0, keepdims=True)
    valid = lax.broadcasted_iota(jnp.int32, (1, seq_len), 1) < len_ref[0]
    own = lax.broadcasted_iota(jnp.int32, (groups, seq_len), 0).astype(f32)
    chosen = jnp.where((own == expert) & valid, 1.0, 0.0)
    earlier = (
        lax.broadcasted_iota(jnp.int32, (seq_len, seq_len), 0)
        < lax.broadcasted_iota(jnp.int32, (seq_len, seq_len), 1)
    ).astype(f32).astype(bf16)
    before = nn(chosen.astype(bf16), earlier)
    slot = jnp.sum(before * chosen, axis=0, keepdims=True)
    place = jnp.where(valid & (slot < capacity), expert * capacity + slot, float(slot_total))
    place_ref[...] = jnp.broadcast_to(place, place_ref.shape)
    sent = nn(slot_pick(place, slot_total), cot_ref[...]).astype(bf16)
    sent = sent.reshape(send_ref.shape)
    send_ref[...] = sent
    first_ref[...] = sent[:, : first_ref.shape[1]]


def slot_pick(place_row, slot_total):
    slots = lax.broadcasted_iota(jnp.int32, (slot_total, place_row.shape[1]), 0).astype(f32)
    return jnp.where(slots == place_row, 1.0, 0.0).astype(bf16)


def row_pick(place_rows, slot_total):
    column = place_rows.T[:, :1]
    slots = lax.broadcasted_iota(jnp.int32, (column.shape[0], slot_total), 1).astype(f32)
    return jnp.where(slots == column, 1.0, 0.0).astype(bf16)


def route(lengths, ids, table, cotangent, groups, capacity, first, after=()):
    rows, width = cotangent.shape
    return launch(
        functools.partial(route_kernel, groups=groups, capacity=capacity),
        (lengths, ids, table, cotangent,),
        [
            pl.BlockSpec(memory_space=pltpu.SMEM),
            whole(ids),
            whole(table),
            whole(cotangent),
        ],
        10,
        after,
        out_specs=[
            pl.BlockSpec((8, rows), lambda: (0, 0)),
            pl.BlockSpec((groups, capacity, width), lambda: (0, 0, 0)),
            pl.BlockSpec((groups, first, width), lambda: (0, 0, 0)),
        ],
        out_shape=[shape((8, rows), f32)]
        + [shape((groups, slots, width), bf16) for slots in (capacity, first)],
    )


def project_kernel(x_ref, gain_ref, shift_ref, wq_ref, wk_ref, wv_ref, n_ref, q_ref, k_ref, v_ref):
    normal, _ = normalize(x_ref[...].astype(f32))
    normed = (normal * gain_ref[...] + shift_ref[...]).astype(bf16)
    n_ref[...] = normed
    q_ref[...] = nn(normed, wq_ref[...]).astype(bf16)
    k_ref[...] = nn(normed, wk_ref[...]).astype(bf16)
    v_ref[...] = nn(normed, wv_ref[...]).astype(bf16)


def project(x, gain, shift, wq, wk, wv, block=256, after=()):
    rows, width = x.shape
    return launch(
        project_kernel,
        (x, gain, shift, wq, wk, wv),
        [row_spec(block, width)] + [whole(a) for a in (gain, shift, wq, wk, wv)],
        13,
        after,
        grid=(rows // block,),
        out_specs=[row_spec(block, width)] * 4,
        out_shape=[shape((rows, width), bf16)] * 4,
    )


def head_parts(length, block, seq_len):
    lane = lax.broadcasted_iota(jnp.int32, (1, PAIR), 1)
    position = lax.broadcasted_iota(jnp.int32, (seq_len, 1), 0)
    bias = jnp.where(position < length, 0.0, MASKED).astype(bf16)
    down = lax.broadcasted_iota(jnp.int32, (block, block), 0)
    across = lax.broadcasted_iota(jnp.int32, (block, block), 1)
    return lane // HEAD_DIM, lane % HEAD_DIM == 0, bias, down <= across


def attend_kernel(
    len_ref, q_ref, k_ref, v_ref, o_ref, log_ref, *, block, pairs
):
    seq_len = q_ref.shape[0]
    factor = HEAD_DIM**-0.5 * math.log2(math.e)
    half, first_lane, bias, causal = head_parts(len_ref[0], block, seq_len)
    zero = jnp.zeros_like(bias)
    keys, queries, values = [], [], []
    for pair in range(pairs):
        lanes = slice(pair * PAIR, (pair + 1) * PAIR)
        q, k = q_ref[:, lanes], k_ref[:, lanes]
        value_t = v_ref[:, lanes].T
        for h in range(2):
            spare = jnp.where(first_lane & (half != h), 1.0, 0.0).astype(bf16)
            keys.append(jnp.where(half == h, k, bias * spare))
            queries.append(jnp.where(half == h, q, spare))
            values.append(
                jnp.concatenate(
                    [value_t[h * HEAD_DIM : (h + 1) * HEAD_DIM], jnp.ones((16, seq_len), bf16)],
                    axis=0,
                )
            )
    order = [(h, j) for j in range(seq_len // block) for h in range(2 * pairs)]

    def score(h, j):
        end = (j + 1) * block
        return nt(keys[h][:end], queries[h][j * block : end])

    def soften(scores, j):
        last = jnp.where(causal, scores[j * block :], MASKED)
        scores = last if j == 0 else jnp.concatenate([scores[: j * block], last], axis=0)
        highest = jnp.max(scores, axis=0, keepdims=True) * factor
        return jnp.exp2(scores * factor - highest).astype(bf16), highest

    def finish(powers, highest, h, j):
        rows = slice(j * block, (j + 1) * block)
        total = nn(values[h][:, : (j + 1) * block], powers)
        summed = total[HEAD_DIM : HEAD_DIM + 1]
        mixed = total[:HEAD_DIM] * (1.0 / summed)
        o_ref[rows, h * HEAD_DIM : (h + 1) * HEAD_DIM] = mixed.T.astype(bf16)
        log_ref[h // 2, h % 2 : h % 2 + 1, rows] = highest + jnp.log2(summed)

    ahead = score(*order[0])
    behind = None
    for step, (h, j) in enumerate(order):
        scores = ahead
        if step + 1 < len(order):
            ahead = score(*order[step + 1])
        if behind is not None:
            finish(*behind, *order[step - 1])
        behind = soften(scores, j)
    finish(*behind, *order[-1])


def attend(lengths, q, k, v, block=256, pairs=2, after=()):
    rows, width = q.shape
    lanes = pl.BlockSpec((rows, pairs * PAIR), lambda i: (0, i))
    return launch(
        functools.partial(attend_kernel, block=block, pairs=pairs),
        (lengths, q, k, v),
        [pl.BlockSpec(memory_space=pltpu.SMEM)] + [lanes] * 3,
        18,
        after,
        grid=(width // (pairs * PAIR),),
        out_specs=[lanes, pl.BlockSpec((pairs, 2, rows), lambda i: (i, 0, 0))],
        out_shape=[shape((rows, width), bf16), shape((width // PAIR, 2, rows), f32)],
    )


def attend_back_kernel(
    len_ref, q_ref, k_ref, v_ref, o_ref, g_ref, log_ref, send_ref,
    dq_ref, dk_ref, dv_ref, recv_ref, send_sems, recv_sems, *, block, pairs,
):
    @pl.when(pl.program_id(0) == 0)
    def _():
        greet()
        exchange_planes(send_ref, recv_ref, send_sems, recv_sems, True)

    seq_len = q_ref.shape[0]
    blocks = seq_len // block
    scale = HEAD_DIM**-0.5
    factor = scale * math.log2(math.e)
    half, first_lane, bias, causal = head_parts(len_ref[0], block, seq_len)
    zero = jnp.zeros_like(bias)
    keys, queries, values, keys_t, logs, deltas = [], [], [], [], [], []
    for pair in range(pairs):
        lanes = slice(pair * PAIR, (pair + 1) * PAIR)
        q, k, v = q_ref[:, lanes], k_ref[:, lanes], v_ref[:, lanes]
        key_t = k.T
        product = (g_ref[:, lanes].astype(f32) * o_ref[:, lanes].astype(f32)).T
        for h in range(2):
            rows = slice(h * HEAD_DIM, (h + 1) * HEAD_DIM)
            spare = jnp.where(first_lane & (half != h), 1.0, 0.0).astype(bf16)
            keys.append(jnp.where(half == h, k, bias * spare))
            queries.append(jnp.where(half == h, q, spare))
            values.append(jnp.where(half == h, v, zero))
            keys_t.append(key_t[rows])
            logs.append(log_ref[pair, h : h + 1, :])
            deltas.append(jnp.sum(product[rows], axis=0, keepdims=True))
    order = [(h, i) for i in range(blocks) for h in range(2 * pairs)]
    query_sums = [[None] * blocks for _ in range(2 * pairs)]
    kept = {}

    def lanes_of(h):
        return slice((h // 2) * PAIR, (h // 2 + 1) * PAIR)

    def products(h, i):
        rows = slice(i * block, (i + 1) * block)
        return (
            nt(keys[h][rows], queries[h][i * block :]),
            nt(values[h][rows], g_ref[i * block :, lanes_of(h)]),
        )

    def shares_of(scores, grad_shares, h, i):
        shares = jnp.exp2(scores * factor - logs[h][:, i * block :])
        first = jnp.where(causal, shares[:, :block], 0.0)
        if i + 1 < blocks:
            first = jnp.concatenate([first, shares[:, block:]], axis=1)
        grad_scores = first * (grad_shares - deltas[h][:, i * block :])
        return first.astype(bf16), grad_scores.astype(bf16)

    def finish(shares, grad_scores, h, i):
        rows, lanes = slice(i * block, (i + 1) * block), lanes_of(h)
        grad_v = nn(shares, g_ref[i * block :, lanes])
        grad_k = nn(grad_scores, q_ref[i * block :, lanes])
        part = nn(keys_t[h][:, rows], grad_scores)
        for j in range(i, blocks):
            term = part[:, (j - i) * block : (j - i + 1) * block]
            held = query_sums[h][j]
            query_sums[h][j] = term if held is None else held + term
        dq_ref[rows, h * HEAD_DIM : (h + 1) * HEAD_DIM] = (
            (query_sums[h][i] * scale).T.astype(bf16)
        )
        kept[h] = (grad_k, grad_v)
        if h % 2:
            other_k, other_v = kept[h - 1]
            dk_ref[rows, lanes] = (jnp.where(half == 0, other_k, grad_k) * scale).astype(bf16)
            dv_ref[rows, lanes] = jnp.where(half == 0, other_v, grad_v).astype(bf16)

    ahead = products(*order[0])
    behind = None
    for step, (h, i) in enumerate(order):
        now = ahead
        if step + 1 < len(order):
            ahead = products(*order[step + 1])
        if behind is not None:
            finish(*behind, *order[step - 1])
        behind = shares_of(*now, h, i)
    finish(*behind, *order[-1])

    @pl.when(pl.program_id(0) == pl.num_programs(0) - 1)
    def _():
        exchange_planes(send_ref, recv_ref, send_sems, recv_sems, False)


def attend_back(lengths, q, k, v, mixed, grad_mixed, logs, send, block=256, pairs=2, after=()):
    rows, width = q.shape
    lanes = pl.BlockSpec((rows, pairs * PAIR), lambda i: (0, i))
    return launch(
        functools.partial(attend_back_kernel, block=block, pairs=pairs),
        (lengths, q, k, v, mixed, grad_mixed, logs, send),
        [pl.BlockSpec(memory_space=pltpu.SMEM)]
        + [lanes] * 5
        + [pl.BlockSpec((pairs, 2, rows), lambda i: (i, 0, 0)), ANY],
        31,
        after,
        collective_id=3,
        grid=(width // (pairs * PAIR),),
        out_specs=[lanes] * 3 + [ANY],
        out_shape=[shape((rows, width), bf16)] * 3
        + [shape((send.shape[0] - 1,) + send.shape[1:], bf16)],
        scratch_shapes=[pltpu.SemaphoreType.DMA((send.shape[0] - 1, send.shape[1]))] * 2,
    )


def middle_kernel(x_ref, m_ref, w_ref, gain_ref, shift_ref, place_ref, mid_ref, send_ref, sent):
    step = pl.program_id(0)
    block = x_ref.shape[0]
    middle = x_ref[...].astype(f32) + nn(m_ref[...], w_ref[...])
    mid_ref[...] = middle
    normal, _ = normalize(middle)
    sent[pl.ds(step * block, block)] = (normal * gain_ref[...] + shift_ref[...]).astype(bf16)

    @pl.when(step == pl.num_programs(0) - 1)
    def _():
        pick = slot_pick(place_ref[:1], send_ref.shape[0])
        send_ref[...] = nn(pick, sent[...]).astype(bf16)


def middle_and_send(x, mixed, w_output, gain, shift, place, slot_total, block=256, after=()):
    rows, width = x.shape
    blocked = row_spec(block, width)
    return launch(
        middle_kernel,
        (x, mixed, w_output, gain, shift, place,),
        [blocked, blocked] + [whole(a) for a in (w_output, gain, shift, place)],
        10,
        after,
        grid=(rows // block,),
        out_specs=[blocked, pl.BlockSpec((slot_total, width), lambda i: (0, 0))],
        out_shape=[shape((rows, width), f32), shape((slot_total, width), bf16)],
        scratch_shapes=[pltpu.VMEM((rows, width), bf16)],
    )


def expert_kernel(
    send_ref, g_ref, in_hbm, out_hbm,
    back_ref, result_ref, most_ref, rest_ref,
    w_in, w_out, x_all, slots_all, result_all,
    w_sems, send_sems, recv_sems, back_sems, back_recv, keep_sems,
    *, rows, sub,
):
    groups, capacity, width = send_ref.shape
    me = lax.axis_index("exp")
    units = w_in.shape[0]
    sources = rows // capacity
    blocks = groups // sources
    mine = me // sources
    count = units // sub
    loads = []
    for f in range(count):
        part = slice(f * sub, (f + 1) * sub)
        pair = [
            pltpu.make_async_copy(hbm.at[part], vmem.at[part], w_sems.at[n, f])
            for n, (hbm, vmem) in enumerate(((in_hbm, w_in), (out_hbm, w_out)))
        ]
        for load in pair:
            load.start()
        loads.append(pair)
    greet()
    def send_block(j, carry):
        block = lax.rem(mine + blocks - j, blocks)

        def send(i, inner):
            peer = block * sources + i

            @pl.when(peer == me)
            def _():
                pltpu.make_async_copy(send_ref.at[me], x_all.at[me], recv_sems.at[me]).start()

            @pl.when(peer != me)
            def _():
                remote(
                    send_ref.at[peer], x_all.at[me], send_sems.at[peer], recv_sems.at[me], peer
                ).start()

            return inner

        return lax.fori_loop(0, sources, send, carry)

    lax.fori_loop(0, blocks, send_block, 0)

    def work(j, wait_weights):
        first_source = lax.rem(mine + j, blocks) * sources

        def arrive(i, carry):
            source = first_source + i
            remote(
                send_ref.at[source], x_all.at[source], send_sems.at[source], recv_sems.at[source],
                source,
            ).wait_recv()
            return carry

        lax.fori_loop(0, sources, arrive, 0)
        x = x_all[pl.ds(first_source, sources)].reshape(rows, width)
        g = g_ref[pl.ds(first_source, sources)].reshape(rows, width)

        def first(f):
            part = slice(f * sub, (f + 1) * sub)
            if wait_weights:
                for load in loads[f]:
                    load.wait()
            return nt(x, w_in[part]), nt(g, w_out[part])

        def second(hidden, grad_activated):
            activated, slope = gelu_parts(hidden)
            return activated.astype(bf16), (grad_activated * slope).astype(bf16)

        sums = None
        ahead, behind = first(0), None
        for f in range(count + 1):
            now = ahead
            if f + 1 < count:
                ahead = first(f + 1)
            if behind is not None:
                part = slice((f - 1) * sub, f * sub)
                terms = nn(behind[1], w_in[part]), nn(behind[0], w_out[part])
                sums = terms if sums is None else (sums[0] + terms[0], sums[1] + terms[1])
            if f < count:
                behind = second(*now)
        dims = (sources, capacity, width)
        slots_all[pl.ds(first_source, sources)] = sums[0].astype(bf16).reshape(dims)
        result_all[pl.ds(first_source, sources)] = sums[1].astype(bf16).reshape(dims)

        def answer(i, carry):
            peer = first_source + i

            @pl.when(peer == me)
            def _():
                pltpu.make_async_copy(slots_all.at[me], back_ref.at[me], back_recv.at[me]).start()

            @pl.when(peer != me)
            def _():
                remote(
                    slots_all.at[peer], back_ref.at[me], back_sems.at[peer], back_recv.at[me], peer
                ).start()

            return carry

        lax.fori_loop(0, sources, answer, 0)

    work(0, True)

    def later(j, carry):
        work(j, False)
        return carry

    lax.fori_loop(1, blocks, later, 0)
    most = most_ref.shape[0]
    keeps = [
        pltpu.make_async_copy(result_all, result_ref, keep_sems.at[0]),
        pltpu.make_async_copy(x_all.at[pl.ds(0, most)], most_ref, keep_sems.at[1]),
        pltpu.make_async_copy(x_all.at[pl.ds(most, groups - most)], rest_ref, keep_sems.at[2]),
    ]
    for keep in keeps:
        keep.start()
    def close(peer, carry):
        @pl.when(peer != me)
        def _():
            remote(
                send_ref.at[peer], x_all.at[peer], send_sems.at[peer], recv_sems.at[peer], peer
            ).wait_send()
            remote(
                slots_all.at[peer], back_ref.at[peer], back_sems.at[peer], back_recv.at[peer], peer
            ).wait_send()

        remote(
            slots_all.at[peer], back_ref.at[peer], back_sems.at[peer], back_recv.at[peer], peer
        ).wait_recv()
        return carry

    lax.fori_loop(0, groups, close, 0)

    for keep in keeps:
        keep.wait()


def expert_main(send, g, w_in, w_out, rows=256, sub=512, after=()):
    groups, capacity, width = send.shape
    units = w_in.shape[0]
    dma = pltpu.SemaphoreType.DMA
    return launch(
        functools.partial(expert_kernel, rows=rows, sub=sub),
        (send, g, w_in, w_out),
        [ANY, whole(g), ANY, ANY],
        60,
        after,
        collective_id=1,
        out_specs=[ANY] * 4,
        out_shape=[shape(send.shape, bf16)] * 2
        + [shape((n, capacity, width), bf16) for n in (groups - groups // 4, groups // 4)],
        scratch_shapes=[pltpu.VMEM((units, width), bf16)] * 2
        + [pltpu.VMEM(send.shape, bf16)] * 3
        + [dma((2, units // sub))]
        + [dma((groups,))] * 4
        + [dma((3,))],
    )


def grad_steps(held, place, w_in, w_out, total, sub):
    devices, slots, width = held.shape[2:]
    x = held[place, 0].reshape(devices * slots, width)
    g = held[place, 1].reshape(devices * slots, width)
    count = w_in.shape[0] // sub

    def rows(r):
        return slice(r * sub, (r + 1) * sub)

    def first(r):
        return nt(w_in[rows(r)], x), nt(w_out[rows(r)], g)

    def second(hidden, grad_activated):
        activated, slope = gelu_parts(hidden)
        return activated.astype(bf16), (grad_activated * slope).astype(bf16)

    def third(activated, grad_hidden, r):
        total[0, rows(r)] += nn(grad_hidden, x)
        total[1, rows(r)] += nn(activated, g)

    ahead, behind = first(0), None
    for r in range(count):
        now = ahead
        if r + 1 < count:
            ahead = first(r + 1)
        if behind is not None:
            third(*behind, r - 1)
        behind = second(*now)
    third(*behind, count - 1)


def share_copies(in_hbm, out_hbm, w_in, w_out, sems):
    part = pl.ds(lax.axis_index("rep") * w_in.shape[0], w_in.shape[0])
    return [
        pltpu.make_async_copy(in_hbm.at[part], w_in, sems.at[0]),
        pltpu.make_async_copy(out_hbm.at[part], w_out, sems.at[1]),
    ]


def plane_copies(held, sems, place, x_ref, first_ref, later_ref, start):
    devices, slots = held.shape[2:4]
    split = first_ref.shape[1]
    part = pl.ds(start, devices)
    return [
        pltpu.make_async_copy(source, target, sems.at[place, n])
        for n, (source, target) in enumerate(
            (
                (x_ref, held.at[place, 0]),
                (first_ref.at[part], held.at[place, 1, :, pl.ds(0, split)]),
                (later_ref.at[part], held.at[place, 1, :, pl.ds(split, slots - split)]),
            )
        )
    ]


def own_grad_kernel(
    most_ref, rest_ref, g_ref, in_hbm, out_hbm, send_ref, sums_ref, recv_ref,
    held, w_in, w_out, total, sems, w_sems, out_sems, send_sems, recv_sems, *, sub,
):
    most, rest = most_ref.shape[0], rest_ref.shape[0]
    copies = share_copies(in_hbm, out_hbm, w_in, w_out, w_sems)
    for n, (source, place) in enumerate(
        ((most_ref, (0, pl.ds(0, most))), (rest_ref, (0, pl.ds(most, rest))), (g_ref, (1,)))
    ):
        copies.append(pltpu.make_async_copy(source, held.at[(0,) + place], sems.at[n // 2, n % 2]))
    for copy in copies:
        copy.start()
    greet()
    start_exchange(send_ref, recv_ref, send_sems, recv_sems, 2)
    total[...] = jnp.zeros_like(total)
    for copy in copies:
        copy.wait()
    grad_steps(held, 0, w_in, w_out, total, sub)
    copy = pltpu.make_async_copy(total, sums_ref, out_sems.at[0])
    copy.start()
    finish_exchange(send_ref, recv_ref, send_sems, recv_sems, 2)
    copy.wait()


def grad_scratch(sets, devices, slots, width, share):
    dma = pltpu.SemaphoreType.DMA
    return [
        pltpu.VMEM((sets, 2, devices, slots, width), bf16),
        pltpu.VMEM((share, width), bf16),
        pltpu.VMEM((share, width), bf16),
        pltpu.VMEM((2, share, width), f32),
        dma((max(sets, 2), 3)),
        dma((2,)),
        dma((2,)),
    ]


def own_grads(most, rest, g, w_in, w_out, send, sub=256, after=()):
    groups, slots, width = g.shape
    share = w_in.shape[0] // lax.axis_size("rep")
    return launch(
        functools.partial(own_grad_kernel, sub=sub),
        (most, rest, g, w_in, w_out, send),
        [ANY] * 6,
        15,
        after,
        collective_id=7,
        out_specs=[ANY] * 2,
        out_shape=[shape((2, share, width), f32), shape(send.shape, bf16)],
        scratch_shapes=grad_scratch(1, groups, slots, width, share)
        + exchange_scratch(send.shape[0]),
    )


def most_grad_kernel(
    all_ref, firsts_ref, laters_ref, in_hbm, out_hbm, before_ref, sums_ref,
    held, w_in, w_out, total, sems, w_sems, out_sems, *, sub,
):
    step = pl.program_id(0)
    z, copies = lax.axis_index("rep"), lax.axis_size("rep")
    weights = share_copies(in_hbm, out_hbm, w_in, w_out, w_sems)
    load = pltpu.make_async_copy(before_ref, total, out_sems.at[0])

    def plane(n, place):
        at = lax.rem(z + n + 1, copies)
        return plane_copies(held, sems, place, all_ref.at[at], firsts_ref.at[n], laters_ref.at[at], 0)

    @pl.when(step == 0)
    def _():
        for copy in weights + plane(0, 0) + [load]:
            copy.start()
        for n in range(1, copies - 1):
            for copy in plane(n, n):
                copy.start()
        for copy in weights + [load]:
            copy.wait()

    for copy in plane(0, step):
        copy.wait()
    grad_steps(held, step, w_in, w_out, total, sub)

    @pl.when(step == pl.num_programs(0) - 1)
    def _():
        copy = pltpu.make_async_copy(total, sums_ref, out_sems.at[0])
        copy.start()
        copy.wait()


def most_grads(gathered, gs, w_in, w_out, before, sub=256, after=()):
    copies, devices, capacity, width = gathered.shape
    share = w_in.shape[0] // copies
    return launch(
        functools.partial(most_grad_kernel, sub=sub),
        (gathered, *gs, w_in, w_out, before),
        [ANY] * 6,
        30,
        after,
        grid=(copies - 1,),
        out_specs=ANY,
        out_shape=shape((2, share, width), f32),
        scratch_shapes=grad_scratch(copies - 1, devices, capacity, width, share),
    )


def rest_grad_kernel(
    shard_ref, all_ref, firsts_ref, laters_ref, in_ref, out_ref, before_ref, gin_ref, gout_ref, held, sems
):
    z, copies = lax.axis_index("rep"), lax.axis_size("rep")
    devices, slots, width = held.shape[2:]
    start = firsts_ref.shape[1] - devices
    planes = []
    for n in range(copies - 1):
        at = lax.rem(z + n + 1, copies)
        planes += plane_copies(
            held, sems, n, all_ref.at[at], firsts_ref.at[n], laters_ref.at[at], start
        )

    @pl.when(pl.program_id(0) == 0)
    def _():
        for copy in planes:
            copy.start()
        for copy in planes:
            copy.wait()

    rows = devices * slots

    def first(n):
        x, g = held[n, 0].reshape(rows, width), held[n, 1].reshape(rows, width)
        return nt(in_ref[...], x), nt(out_ref[...], g)

    grad_in, grad_out = before_ref[0], before_ref[1]
    ahead = first(0)
    for n in range(copies - 1):
        hidden, grad_activated = ahead
        if n + 2 < copies:
            ahead = first(n + 1)
        activated, slope = gelu_parts(hidden)
        grad_out += nn(activated.astype(bf16), held[n, 1].reshape(rows, width))
        grad_in += nn((grad_activated * slope).astype(bf16), held[n, 0].reshape(rows, width))
    gin_ref[...] = grad_in
    gout_ref[...] = grad_out


def rest_grads(gathered, gs, shard, w_in, w_out, before, block=256, after=()):
    copies, devices, capacity, width = gathered.shape
    share = w_in.shape[0] // copies
    steps = share // block
    weights = pl.BlockSpec((block, width), lambda i, shard: (shard[0] * steps + i, 0))
    both = pl.BlockSpec((2, block, width), lambda i, shard: (0, i, 0))
    blocked = pl.BlockSpec((block, width), lambda i, shard: (i, 0))

    def kernel(*refs):
        rest_grad_kernel(*refs[:7], *refs[7 + len(after) :])

    return pl.pallas_call(
        kernel,
        grid_spec=pltpu.PrefetchScalarGridSpec(
            num_scalar_prefetch=1,
            grid=(steps,),
            in_specs=[ANY] * 3 + [weights] * 2 + [both] + [ANY] * len(after),
            out_specs=[blocked] * 2,
            scratch_shapes=[
                pltpu.VMEM((copies - 1, 2, devices, capacity, width), bf16),
                pltpu.SemaphoreType.DMA((copies - 1, 3)),
            ],
        ),
        out_shape=[shape((share, width), f32)] * 2,
        compiler_params=params(),
        cost_estimate=pl.CostEstimate(flops=int(1e9), bytes_accessed=int(1e6), transcendentals=0),
    )(shard, gathered, *gs, w_in, w_out, before, *after)


def fence_kernel(*refs):
    pass


def fence(arrays, after):
    count = len(arrays)
    return launch(
        fence_kernel,
        tuple(arrays),
        [ANY] * count,
        1,
        after,
        out_specs=[ANY] * count,
        out_shape=[shape(a.shape, a.dtype) for a in arrays],
        input_output_aliases={n: n for n in range(count)},
    )


def back_kernel(
    back_ref, place_ref, mid_ref, cot_ref, len_ref, gain_ref, w_ref,
    gmid_ref, branch_ref, gmix_ref, ggain_ref, gshift_ref,
):
    step = pl.program_id(0)
    block = mid_ref.shape[0]
    grad_sent = nn(row_pick(place_ref[...], back_ref.shape[0]), back_ref[...])
    normal, inverse = normalize(mid_ref[...])
    position = step * block + lax.broadcasted_iota(jnp.int32, (block, 1), 0)
    grad_final = jnp.where(position < len_ref[0], cot_ref[...].astype(f32), 0.0)
    grad_middle = grad_final + norm_backward(grad_sent, normal, inverse, gain_ref[...])
    gmid_ref[...] = grad_middle
    branch = grad_middle.astype(bf16)
    branch_ref[...] = branch
    gmix_ref[...] = nt(branch, w_ref[...]).astype(bf16)

    @pl.when(step == 0)
    def _():
        ggain_ref[...] = jnp.zeros_like(ggain_ref)
        gshift_ref[...] = jnp.zeros_like(gshift_ref)

    ggain_ref[...] += jnp.sum(grad_sent * normal, axis=0, keepdims=True)
    gshift_ref[...] += jnp.sum(grad_sent, axis=0, keepdims=True)


def middle_back(back, place, middle, cotangent, lengths, gain, w_output, block=256, after=()):
    rows, width = middle.shape
    blocked = row_spec(block, width)
    vector = pl.BlockSpec((1, width), lambda i: (0, 0))
    return launch(
        back_kernel,
        (back, place, middle, cotangent, lengths, gain, w_output,),
        [
            whole(back),
            pl.BlockSpec((8, block), lambda i: (0, i)),
            blocked,
            blocked,
            pl.BlockSpec(memory_space=pltpu.SMEM),
            whole(gain),
            whole(w_output),
        ],
        12,
        after,
        grid=(rows // block,),
        out_specs=[blocked, blocked, blocked, vector, vector],
        out_shape=[shape((rows, width), f32)]
        + [shape((rows, width), bf16)] * 2
        + [shape((1, width), f32)] * 2,
    )


def weight_grad_kernel(m_ref, branch_ref, n_ref, gq_ref, gk_ref, gv_ref, o_ref):
    groups, _, _, share, width = o_ref.shape

    def put(n, left, right_ref):
        o_ref[:, 0, n] = nn(left, right_ref[...]).reshape(groups, share, width).astype(bf16)

    put(0, m_ref[...].T, branch_ref)
    left = n_ref[...].T
    for n, ref in enumerate((gq_ref, gk_ref, gv_ref)):
        put(n + 1, left, ref)


def weight_grads(mixed, branch, normed, gq, gk, gv, groups, copies, after=()):
    rows, width = mixed.shape
    block = width // copies
    dims = (groups, copies, 4, block // groups, width)
    column = pl.BlockSpec((rows, block), lambda i: (0, i))
    return launch(
        weight_grad_kernel,
        (mixed, branch, normed, gq, gk, gv),
        [column, whole(branch), column] + [whole(a) for a in (gq, gk, gv)],
        16,
        after,
        grid=(copies,),
        out_specs=pl.BlockSpec((groups, 1) + dims[2:], lambda i: (0, i, 0, 0, 0)),
        out_shape=shape(dims, bf16),
    )


def input_back_kernel(
    gq_ref, gk_ref, gv_ref, wq_ref, wk_ref, wv_ref, x_ref, gmid_ref, gain_ref,
    gin_ref, ggain_ref, gshift_ref,
):
    grad_normed = (
        nt(gq_ref[...], wq_ref[...]) + nt(gk_ref[...], wk_ref[...]) + nt(gv_ref[...], wv_ref[...])
    )
    normal, inverse = normalize(x_ref[...].astype(f32))
    gin_ref[...] = gmid_ref[...] + norm_backward(grad_normed, normal, inverse, gain_ref[...])

    @pl.when(pl.program_id(0) == 0)
    def _():
        ggain_ref[...] = jnp.zeros_like(ggain_ref)
        gshift_ref[...] = jnp.zeros_like(gshift_ref)

    ggain_ref[...] += jnp.sum(grad_normed * normal, axis=0, keepdims=True)
    gshift_ref[...] += jnp.sum(grad_normed, axis=0, keepdims=True)


def input_back(gq, gk, gv, wq, wk, wv, x, grad_middle, gain, block=256, after=()):
    rows, width = x.shape
    blocked = row_spec(block, width)
    vector = pl.BlockSpec((1, width), lambda i: (0, 0))
    return launch(
        input_back_kernel,
        (gq, gk, gv, wq, wk, wv, x, grad_middle, gain,),
        [blocked] * 3 + [whole(w) for w in (wq, wk, wv)] + [blocked, blocked, whole(gain)],
        14,
        after,
        grid=(rows // block,),
        out_specs=[blocked, vector, vector],
        out_shape=[shape((rows, width), f32)] + [shape((1, width), f32)] * 2,
    )


def chip_add_kernel(dense_ref, o_ref, kept, got, sems, keep_sems):
    me = lax.axis_index("exp")
    core = lax.rem(me, 2)
    half = o_ref.shape[0]
    sibling = at_exp(me + 1 - 2 * core)
    copies = []
    for n in range(half):
        copies.append(
            (
                pltpu.make_async_copy(dense_ref.at[2 * n + core], kept.at[n], keep_sems.at[0, n]),
                push(dense_ref.at[2 * n + 1 - core], got.at[n], sems.at[0, n], sems.at[1, n], sibling),
                pltpu.make_async_copy(kept.at[n], o_ref.at[n], keep_sems.at[1, n]),
            )
        )
        copies[-1][0].start()
    greet()
    for _, give, _ in copies:
        give.start()
    for n, (keep, give, write) in enumerate(copies):
        keep.wait()
        give.wait_recv()
        kept[n] = (kept[n].astype(f32) + got[n].astype(f32)).astype(bf16)
        write.start()
    for _, give, write in copies:
        give.wait_send()
        write.wait()


def chip_add(dense, after=()):
    half = dense.shape[0] // 2
    dims = (half,) + dense.shape[1:]
    dma = pltpu.SemaphoreType.DMA
    return launch(
        chip_add_kernel,
        (dense,),
        [ANY],
        8,
        after,
        collective_id=4,
        out_specs=ANY,
        out_shape=shape(dims, bf16),
        scratch_shapes=[pltpu.VMEM(dims, bf16)] * 2 + [dma((2, half))] * 2,
    )


def near_add_kernel(parts_ref, o_ref):
    o_ref[0] = jnp.sum(parts_ref[:, 0].astype(f32), axis=0).astype(bf16)


def near_add(parts, after=()):
    groups, copies = parts.shape[:2]
    dims = parts.shape[2:]
    return launch(
        near_add_kernel,
        (parts,),
        [pl.BlockSpec((groups, 1) + dims, lambda i: (0, i, 0, 0, 0))],
        6,
        after,
        grid=(copies,),
        out_specs=pl.BlockSpec((1,) + dims, lambda i: (i, 0, 0, 0)),
        out_shape=shape((copies,) + dims, bf16),
    )


def far_add_kernel(parts_ref, *out_refs):
    for n, ref in enumerate(out_refs):
        ref[...] = jnp.sum(parts_ref[:, n].astype(f32), axis=0)


def far_add(parts, after=()):
    _, count, share, width = parts.shape
    return launch(
        far_add_kernel,
        (parts,),
        [whole(parts)],
        1,
        after,
        out_specs=[pl.BlockSpec((share, width), lambda: (0, 0))] * count,
        out_shape=[shape((share, width), f32)] * count,
    )


def output_kernel(back_ref, place_ref, mid_ref, o_ref):
    combined = nn(row_pick(place_ref[...], back_ref.shape[0]), back_ref[...])
    o_ref[...] = (mid_ref[...] + combined).astype(bf16)


def combine(back, place, middle, block=256, after=()):
    rows, width = middle.shape
    return launch(
        output_kernel,
        (back, place, middle),
        [
            whole(back),
            pl.BlockSpec((8, block), lambda i: (0, i)),
            row_spec(block, width),
        ],
        7,
        after,
        grid=(rows // block,),
        out_specs=row_spec(block, width),
        out_shape=shape((rows, width), bf16),
    )


def body(
    inputs,
    cotangent,
    token_ids,
    lengths,
    hash_table,
    first_gain,
    first_shift,
    w_query,
    w_key,
    w_value,
    w_output,
    second_gain,
    second_shift,
    expert_in,
    expert_out,
):
    seq_count, seq_len, width = inputs.shape
    rows = seq_count * seq_len
    groups = lax.axis_size("exp")
    copies = lax.axis_size("rep")
    place_z = lax.axis_index("rep")
    capacity = rows // groups
    slot_total = groups * capacity
    x = inputs.reshape(rows, width)
    cot = cotangent.reshape(rows, width)
    gain_one, shift_one, gain_two, shift_two = (
        v.reshape(1, width) for v in (first_gain, first_shift, second_gain, second_shift)
    )
    table_rows = -(-hash_table.shape[0] // (8 * 128)) * 8
    table = jnp.pad(hash_table, (0, table_rows * 128 - hash_table.shape[0]))
    table = table.reshape(table_rows, 128)

    place_e = lax.axis_index("exp")

    def exchange(parts, axis="exp"):
        return lax.all_to_all(parts, axis, split_axis=0, concat_axis=0, tiled=True)

    def gather(array):
        return lax.all_gather(array, "rep", axis=0, tiled=False)

    flat = (slot_total, width)
    by_group = (groups, capacity, width)
    w_in, w_out = expert_in[0], expert_out[0]
    first = max(16, capacity // 4)
    place, grad_send, send_first = route(
        lengths, token_ids.reshape(1, rows), table, cot, groups, capacity, first
    )
    firsts = gather(send_first)
    grads = exchange(grad_send)
    normed, q, k, v = project(x, gain_one, shift_one, w_query, w_key, w_value, after=(grad_send,))
    mixed, logs = attend(lengths, q, k, v)
    (grads,) = fence((grads,), (mixed,))
    laters = gather(grads[:, first:])
    middle, send_rows = middle_and_send(
        x, mixed, w_output, gain_two, shift_two, place, slot_total, after=(grads,)
    )
    grad_back, result, most, rest = expert_main(send_rows.reshape(by_group), grads, w_in, w_out)
    all_most, all_rest = gather(most), gather(rest)
    returned = exchange(result)
    grad_middle, branch, grad_mixed, grad_second_gain, grad_second_shift = middle_back(
        grad_back.reshape(flat), place, middle, cot, lengths, gain_two, w_output
    )
    gq, gk, gv, firsts = attend_back(lengths, q, k, v, mixed, grad_mixed, logs, firsts)
    parts = weight_grads(mixed, branch, normed, gq, gk, gv, groups, copies)
    chip_parts = chip_add(parts, after=(returned,))
    grad_inputs, grad_first_gain, grad_first_shift = input_back(
        gq, gk, gv, w_query, w_key, w_value, x, grad_middle, gain_one, after=(chip_parts,)
    )
    vectors = jnp.concatenate(
        [grad_first_gain, grad_first_shift, grad_second_gain, grad_second_shift], axis=0
    )
    devices = groups * copies
    part = width // devices
    vectors = vectors.reshape(4, devices, part).transpose(1, 0, 2)
    vectors = jnp.sum(exchange(vectors, ("rep", "exp")), axis=0)
    sums, near_parts = own_grads(
        most, rest, grads, w_in, w_out, chip_parts, after=(grad_first_gain,)
    )
    near_all = near_add(near_parts)
    outputs = combine(returned.reshape(flat), place, middle, after=(near_all, laters))
    sums = most_grads(
        all_most, (firsts, laters), w_in, w_out, sums, after=(outputs, vectors)
    )
    (near_all,) = fence((near_all,), (sums,))
    far = exchange(near_all, "rep")
    grad_expert_in, grad_expert_out = rest_grads(
        all_rest, (firsts, laters), place_z.astype(jnp.int32).reshape(1), w_in, w_out, sums, after=(near_all,)
    )
    dense = far_add(far, after=(grad_expert_in,))
    dense_output, dense_query, dense_key, dense_value = dense
    return (
        outputs.reshape(seq_count, seq_len, width),
        grad_inputs.reshape(seq_count, seq_len, width),
        vectors[0],
        vectors[1],
        dense_query,
        dense_key,
        dense_value,
        dense_output,
        vectors[2],
        vectors[3],
        grad_expert_in[None],
        grad_expert_out[None],
    )


def solution(mesh):
    both = ("rep", "exp")
    placed = (
        P(both, None, None),
        P(both, None, None),
        P(both, None),
        P(both),
    ) + (P(),) * 9 + (P("exp", None, None),) * 2
    return jax.shard_map(
        body,
        mesh=mesh,
        in_specs=placed,
        out_specs=(
            P(both, None, None),
            P(both, None, None),
            P(both),
            P(both),
            P(both, None),
            P(both, None),
            P(both, None),
            P(both, None),
            P(both),
            P(both),
            P("exp", "rep", None),
            P("exp", "rep", None),
        ),
        check_vma=False,
    )
```

```python
import functools
import math

import jax
import jax.numpy as jnp
from jax import lax
from jax.experimental import pallas as pl
from jax.experimental.pallas import tpu as pltpu
from jax.sharding import PartitionSpec as P

HEAD_DIM = 64
PAIR = 2 * HEAD_DIM
MASKED = -1e30
epsilon = 1e-05
bf16, f32 = jnp.bfloat16, jnp.float32
MESH = pl.DeviceIdType.MESH
ANY = pl.BlockSpec(memory_space=pl.ANY)
VMEM_BYTES = 56 * 1024 * 1024
PARTS = 4


def params(collective_id=None):
    if collective_id is None:
        return pltpu.CompilerParams(vmem_limit_bytes=VMEM_BYTES)
    return pltpu.CompilerParams(
        vmem_limit_bytes=VMEM_BYTES, collective_id=collective_id, has_side_effects=True
    )


def launch(kernel, operands, in_specs, micros, after=(), collective_id=None, **options):
    count = len(operands)

    def run(*refs):
        kernel(*refs[:count], *refs[count + len(after) :])

    return pl.pallas_call(
        run,
        in_specs=list(in_specs) + [pl.BlockSpec(memory_space=pl.ANY)] * len(after),
        compiler_params=params(collective_id),
        cost_estimate=pl.CostEstimate(
            flops=int(1e9), bytes_accessed=int(1e6), transcendentals=0
        ),
        **options,
    )(*operands, *after)


def at_rep(place):
    return {"rep": place}


def at_exp(place):
    return {"exp": place}


def greet(*axes):
    barrier = pltpu.get_barrier_semaphore()
    count = 0
    for axis in axes or ("exp",):
        size, me = lax.axis_size(axis), lax.axis_index(axis)

        def tell(step, carry, axis=axis, size=size, me=me):
            peer = lax.rem(me + step, size)
            pl.semaphore_signal(barrier, inc=1, device_id={axis: peer}, device_id_type=MESH)
            return carry

        lax.fori_loop(1, size, tell, 0)
        count += size - 1
    pl.semaphore_wait(barrier, count)


def push(source, target, send_sem, recv_sem, device):
    return pltpu.make_async_remote_copy(
        src_ref=source,
        dst_ref=target,
        send_sem=send_sem,
        recv_sem=recv_sem,
        device_id=device,
        device_id_type=MESH,
    )


def remote(source, target, send_sem, recv_sem, peer):
    return push(source, target, send_sem, recv_sem, at_exp(peer))


def start_exchange(send_ref, recv_ref, send_sems, recv_sems, stride=1, axis="exp"):
    groups = send_ref.shape[0]
    me = lax.axis_index(axis)
    mine = me // stride
    pltpu.make_async_copy(send_ref.at[mine], recv_ref.at[mine], recv_sems.at[mine]).start()

    def send(step, carry):
        entry = lax.rem(mine + step, groups)
        peer = entry * stride + lax.rem(me, stride)
        push(
            send_ref.at[entry], recv_ref.at[mine], send_sems.at[entry], recv_sems.at[mine], {axis: peer}
        ).start()
        return carry

    lax.fori_loop(1, groups, send, 0)


def finish_exchange(send_ref, recv_ref, send_sems, recv_sems, stride=1, axis="exp"):
    groups = send_ref.shape[0]
    me = lax.axis_index(axis)
    mine = me // stride
    pltpu.make_async_copy(send_ref.at[mine], recv_ref.at[mine], recv_sems.at[mine]).wait()

    def wait(step, carry):
        entry = lax.rem(mine + step, groups)
        peer = entry * stride + lax.rem(me, stride)
        copy = push(
            send_ref.at[entry], recv_ref.at[entry], send_sems.at[entry], recv_sems.at[entry], {axis: peer}
        )
        copy.wait_send()
        copy.wait_recv()
        return carry

    lax.fori_loop(1, groups, wait, 0)


def remote(source, target, send_sem, recv_sem, peer):
    return push(source, target, send_sem, recv_sem, at_exp(peer))


def exchange_planes(send_ref, recv_ref, send_sems, recv_sems, begin):
    copies, groups = send_ref.shape[:2]
    z, me = lax.axis_index("rep"), lax.axis_index("exp")

    def shift(n, carry):
        plane = lax.rem(z + n + 1, copies)
        own = pltpu.make_async_copy(send_ref.at[plane, me], recv_ref.at[n, me], recv_sems.at[n, me])
        own.start() if begin else own.wait()

        def one(step, inner):
            peer = lax.rem(me + step, groups)
            entry = me if begin else peer
            copy = push(
                send_ref.at[plane, peer], recv_ref.at[n, entry],
                send_sems.at[n, peer], recv_sems.at[n, entry], at_exp(peer),
            )
            if begin:
                copy.start()
            else:
                copy.wait_send()
                copy.wait_recv()
            return inner

        return lax.fori_loop(1, groups, one, carry)

    lax.fori_loop(0, copies - 1, shift, 0)


def exchange_scratch(groups):
    return [pltpu.SemaphoreType.DMA((groups,))] * 2


def shape(dims, kind):
    return jax.ShapeDtypeStruct(dims, kind)


def nn(left, right):
    return lax.dot_general(left, right, (((1,), (0,)), ((), ())), preferred_element_type=f32)


def nt(left, right):
    return lax.dot_general(left, right, (((1,), (1,)), ((), ())), preferred_element_type=f32)


def tn(left, right):
    return lax.dot_general(left, right, (((0,), (0,)), ((), ())), preferred_element_type=f32)


def whole(array):
    return pl.BlockSpec(array.shape, lambda *_: (0,) * array.ndim)


def row_spec(rows, width):
    return pl.BlockSpec((rows, width), lambda i: (i, 0))


def normalize(values):
    average = jnp.mean(values, axis=1, keepdims=True)
    centered = values - average
    spread = jnp.mean(centered * centered, axis=1, keepdims=True)
    inverse = lax.rsqrt(spread + epsilon)
    return centered * inverse, inverse


def norm_backward(grad_out, normal, inverse, gain):
    grad_normal = grad_out * gain
    inner = (
        grad_normal
        - jnp.mean(grad_normal, axis=1, keepdims=True)
        - normal * jnp.mean(grad_normal * normal, axis=1, keepdims=True)
    )
    return inner * inverse


def gelu_parts(hidden):
    share = 0.5 * (1.0 + lax.erf(hidden * (1.0 / math.sqrt(2.0))))
    slope = share + hidden * jnp.exp(-0.5 * hidden * hidden) * (1.0 / math.sqrt(2.0 * math.pi))
    return hidden * share, slope


def route_kernel(
    len_ref, ids_ref, table_ref, cot_ref, place_ref, send_ref, first_ref, *, groups, capacity
):
    seq_len = ids_ref.shape[1]
    slot_total = groups * capacity
    high_count, low_count = table_ref.shape
    ids = ids_ref[...]
    high, low = ids // low_count, ids % low_count
    high_pick = (
        lax.broadcasted_iota(jnp.int32, (high_count, seq_len), 0) == high
    ).astype(f32).astype(bf16)
    picked = tn(table_ref[...].astype(bf16), high_pick)
    low_pick = lax.broadcasted_iota(jnp.int32, (low_count, seq_len), 0) == low
    expert = jnp.sum(jnp.where(low_pick, picked, 0.0), axis=0, keepdims=True)
    valid = lax.broadcasted_iota(jnp.int32, (1, seq_len), 1) < len_ref[0]
    own = lax.broadcasted_iota(jnp.int32, (groups, seq_len), 0).astype(f32)
    chosen = jnp.where((own == expert) & valid, 1.0, 0.0)
    earlier = (
        lax.broadcasted_iota(jnp.int32, (seq_len, seq_len), 0)
        < lax.broadcasted_iota(jnp.int32, (seq_len, seq_len), 1)
    ).astype(f32).astype(bf16)
    before = nn(chosen.astype(bf16), earlier)
    slot = jnp.sum(before * chosen, axis=0, keepdims=True)
    place = jnp.where(valid & (slot < capacity), expert * capacity + slot, float(slot_total))
    place_ref[...] = jnp.broadcast_to(place, place_ref.shape)
    sent = nn(slot_pick(place, slot_total), cot_ref[...]).astype(bf16)
    sent = sent.reshape(send_ref.shape)
    send_ref[...] = sent
    first_ref[...] = sent[:, : first_ref.shape[1]]


def slot_pick(place_row, slot_total):
    slots = lax.broadcasted_iota(jnp.int32, (slot_total, place_row.shape[1]), 0).astype(f32)
    return jnp.where(slots == place_row, 1.0, 0.0).astype(bf16)


def row_pick(place_rows, slot_total):
    column = place_rows.T[:, :1]
    slots = lax.broadcasted_iota(jnp.int32, (column.shape[0], slot_total), 1).astype(f32)
    return jnp.where(slots == column, 1.0, 0.0).astype(bf16)


def route(lengths, ids, table, cotangent, groups, capacity, first, after=()):
    rows, width = cotangent.shape
    return launch(
        functools.partial(route_kernel, groups=groups, capacity=capacity),
        (lengths, ids, table, cotangent,),
        [
            pl.BlockSpec(memory_space=pltpu.SMEM),
            whole(ids),
            whole(table),
            whole(cotangent),
        ],
        10,
        after,
        out_specs=[
            pl.BlockSpec((8, rows), lambda: (0, 0)),
            pl.BlockSpec((groups, capacity, width), lambda: (0, 0, 0)),
            pl.BlockSpec((groups, first, width), lambda: (0, 0, 0)),
        ],
        out_shape=[shape((8, rows), f32)]
        + [shape((groups, slots, width), bf16) for slots in (capacity, first)],
    )


def project_kernel(x_ref, gain_ref, shift_ref, wq_ref, wk_ref, wv_ref, n_ref, q_ref, k_ref, v_ref):
    normal, _ = normalize(x_ref[...].astype(f32))
    normed = (normal * gain_ref[...] + shift_ref[...]).astype(bf16)
    n_ref[...] = normed
    q_ref[...] = nn(normed, wq_ref[...]).astype(bf16)
    k_ref[...] = nn(normed, wk_ref[...]).astype(bf16)
    v_ref[...] = nn(normed, wv_ref[...]).astype(bf16)


def project(x, gain, shift, wq, wk, wv, block=256, after=()):
    rows, width = x.shape
    return launch(
        project_kernel,
        (x, gain, shift, wq, wk, wv),
        [row_spec(block, width)] + [whole(a) for a in (gain, shift, wq, wk, wv)],
        13,
        after,
        grid=(rows // block,),
        out_specs=[row_spec(block, width)] * 4,
        out_shape=[shape((rows, width), bf16)] * 4,
    )


def head_parts(length, block, seq_len):
    lane = lax.broadcasted_iota(jnp.int32, (1, PAIR), 1)
    position = lax.broadcasted_iota(jnp.int32, (seq_len, 1), 0)
    bias = jnp.where(position < length, 0.0, MASKED).astype(bf16)
    down = lax.broadcasted_iota(jnp.int32, (block, block), 0)
    across = lax.broadcasted_iota(jnp.int32, (block, block), 1)
    return lane // HEAD_DIM, lane % HEAD_DIM == 0, bias, down <= across


def attend_kernel(
    len_ref, q_ref, k_ref, v_ref, o_ref, log_ref, *, block, pairs
):
    seq_len = q_ref.shape[0]
    factor = HEAD_DIM**-0.5 * math.log2(math.e)
    half, first_lane, bias, causal = head_parts(len_ref[0], block, seq_len)
    zero = jnp.zeros_like(bias)
    keys, queries, values = [], [], []
    for pair in range(pairs):
        lanes = slice(pair * PAIR, (pair + 1) * PAIR)
        q, k = q_ref[:, lanes], k_ref[:, lanes]
        value_t = v_ref[:, lanes].T
        for h in range(2):
            spare = jnp.where(first_lane & (half != h), 1.0, 0.0).astype(bf16)
            keys.append(jnp.where(half == h, k, bias * spare))
            queries.append(jnp.where(half == h, q, spare))
            values.append(
                jnp.concatenate(
                    [value_t[h * HEAD_DIM : (h + 1) * HEAD_DIM], jnp.ones((16, seq_len), bf16)],
                    axis=0,
                )
            )
    order = [(h, j) for j in range(seq_len // block) for h in range(2 * pairs)]

    def score(h, j):
        end = (j + 1) * block
        return nt(keys[h][:end], queries[h][j * block : end])

    def soften(scores, j):
        last = jnp.where(causal, scores[j * block :], MASKED)
        scores = last if j == 0 else jnp.concatenate([scores[: j * block], last], axis=0)
        highest = jnp.max(scores, axis=0, keepdims=True) * factor
        return jnp.exp2(scores * factor - highest).astype(bf16), highest

    def finish(powers, highest, h, j):
        rows = slice(j * block, (j + 1) * block)
        total = nn(values[h][:, : (j + 1) * block], powers)
        summed = total[HEAD_DIM : HEAD_DIM + 1]
        mixed = total[:HEAD_DIM] * (1.0 / summed)
        o_ref[rows, h * HEAD_DIM : (h + 1) * HEAD_DIM] = mixed.T.astype(bf16)
        log_ref[h // 2, h % 2 : h % 2 + 1, rows] = highest + jnp.log2(summed)

    ahead = score(*order[0])
    behind = None
    for step, (h, j) in enumerate(order):
        scores = ahead
        if step + 1 < len(order):
            ahead = score(*order[step + 1])
        if behind is not None:
            finish(*behind, *order[step - 1])
        behind = soften(scores, j)
    finish(*behind, *order[-1])


def attend(lengths, q, k, v, block=256, pairs=2, after=()):
    rows, width = q.shape
    lanes = pl.BlockSpec((rows, pairs * PAIR), lambda i: (0, i))
    return launch(
        functools.partial(attend_kernel, block=block, pairs=pairs),
        (lengths, q, k, v),
        [pl.BlockSpec(memory_space=pltpu.SMEM)] + [lanes] * 3,
        18,
        after,
        grid=(width // (pairs * PAIR),),
        out_specs=[lanes, pl.BlockSpec((pairs, 2, rows), lambda i: (i, 0, 0))],
        out_shape=[shape((rows, width), bf16), shape((width // PAIR, 2, rows), f32)],
    )


def attend_back_kernel(
    len_ref, q_ref, k_ref, v_ref, o_ref, g_ref, log_ref, send_ref,
    dq_ref, dk_ref, dv_ref, recv_ref, send_sems, recv_sems, *, block, pairs,
):
    @pl.when(pl.program_id(0) == 0)
    def _():
        greet()
        exchange_planes(send_ref, recv_ref, send_sems, recv_sems, True)

    seq_len = q_ref.shape[0]
    blocks = seq_len // block
    scale = HEAD_DIM**-0.5
    factor = scale * math.log2(math.e)
    half, first_lane, bias, causal = head_parts(len_ref[0], block, seq_len)
    zero = jnp.zeros_like(bias)
    keys, queries, values, keys_t, logs, deltas = [], [], [], [], [], []
    for pair in range(pairs):
        lanes = slice(pair * PAIR, (pair + 1) * PAIR)
        q, k, v = q_ref[:, lanes], k_ref[:, lanes], v_ref[:, lanes]
        key_t = k.T
        product = (g_ref[:, lanes].astype(f32) * o_ref[:, lanes].astype(f32)).T
        for h in range(2):
            rows = slice(h * HEAD_DIM, (h + 1) * HEAD_DIM)
            spare = jnp.where(first_lane & (half != h), 1.0, 0.0).astype(bf16)
            keys.append(jnp.where(half == h, k, bias * spare))
            queries.append(jnp.where(half == h, q, spare))
            values.append(jnp.where(half == h, v, zero))
            keys_t.append(key_t[rows])
            logs.append(log_ref[pair, h : h + 1, :])
            deltas.append(jnp.sum(product[rows], axis=0, keepdims=True))
    order = [(h, i) for i in range(blocks) for h in range(2 * pairs)]
    query_sums = [[None] * blocks for _ in range(2 * pairs)]
    kept = {}

    def lanes_of(h):
        return slice((h // 2) * PAIR, (h // 2 + 1) * PAIR)

    def products(h, i):
        rows = slice(i * block, (i + 1) * block)
        return (
            nt(keys[h][rows], queries[h][i * block :]),
            nt(values[h][rows], g_ref[i * block :, lanes_of(h)]),
        )

    def shares_of(scores, grad_shares, h, i):
        shares = jnp.exp2(scores * factor - logs[h][:, i * block :])
        first = jnp.where(causal, shares[:, :block], 0.0)
        if i + 1 < blocks:
            first = jnp.concatenate([first, shares[:, block:]], axis=1)
        grad_scores = first * (grad_shares - deltas[h][:, i * block :])
        return first.astype(bf16), grad_scores.astype(bf16)

    def finish(shares, grad_scores, h, i):
        rows, lanes = slice(i * block, (i + 1) * block), lanes_of(h)
        grad_v = nn(shares, g_ref[i * block :, lanes])
        grad_k = nn(grad_scores, q_ref[i * block :, lanes])
        part = nn(keys_t[h][:, rows], grad_scores)
        for j in range(i, blocks):
            term = part[:, (j - i) * block : (j - i + 1) * block]
            held = query_sums[h][j]
            query_sums[h][j] = term if held is None else held + term
        dq_ref[rows, h * HEAD_DIM : (h + 1) * HEAD_DIM] = (
            (query_sums[h][i] * scale).T.astype(bf16)
        )
        kept[h] = (grad_k, grad_v)
        if h % 2:
            other_k, other_v = kept[h - 1]
            dk_ref[rows, lanes] = (jnp.where(half == 0, other_k, grad_k) * scale).astype(bf16)
            dv_ref[rows, lanes] = jnp.where(half == 0, other_v, grad_v).astype(bf16)

    ahead = products(*order[0])
    behind = None
    for step, (h, i) in enumerate(order):
        now = ahead
        if step + 1 < len(order):
            ahead = products(*order[step + 1])
        if behind is not None:
            finish(*behind, *order[step - 1])
        behind = shares_of(*now, h, i)
    finish(*behind, *order[-1])

    @pl.when(pl.program_id(0) == pl.num_programs(0) - 1)
    def _():
        exchange_planes(send_ref, recv_ref, send_sems, recv_sems, False)


def attend_back(lengths, q, k, v, mixed, grad_mixed, logs, send, block=256, pairs=2, after=()):
    rows, width = q.shape
    lanes = pl.BlockSpec((rows, pairs * PAIR), lambda i: (0, i))
    return launch(
        functools.partial(attend_back_kernel, block=block, pairs=pairs),
        (lengths, q, k, v, mixed, grad_mixed, logs, send),
        [pl.BlockSpec(memory_space=pltpu.SMEM)]
        + [lanes] * 5
        + [pl.BlockSpec((pairs, 2, rows), lambda i: (i, 0, 0)), ANY],
        31,
        after,
        collective_id=3,
        grid=(width // (pairs * PAIR),),
        out_specs=[lanes] * 3 + [ANY],
        out_shape=[shape((rows, width), bf16)] * 3
        + [shape((send.shape[0] - 1,) + send.shape[1:], bf16)],
        scratch_shapes=[pltpu.SemaphoreType.DMA((send.shape[0] - 1, send.shape[1]))] * 2,
    )


def middle_kernel(x_ref, m_ref, w_ref, gain_ref, shift_ref, place_ref, mid_ref, send_ref, sent):
    step = pl.program_id(0)
    block = x_ref.shape[0]
    middle = x_ref[...].astype(f32) + nn(m_ref[...], w_ref[...])
    mid_ref[...] = middle
    normal, _ = normalize(middle)
    sent[pl.ds(step * block, block)] = (normal * gain_ref[...] + shift_ref[...]).astype(bf16)

    @pl.when(step == pl.num_programs(0) - 1)
    def _():
        pick = slot_pick(place_ref[:1], send_ref.shape[0])
        send_ref[...] = nn(pick, sent[...]).astype(bf16)


def middle_and_send(x, mixed, w_output, gain, shift, place, slot_total, block=256, after=()):
    rows, width = x.shape
    blocked = row_spec(block, width)
    return launch(
        middle_kernel,
        (x, mixed, w_output, gain, shift, place,),
        [blocked, blocked] + [whole(a) for a in (w_output, gain, shift, place)],
        10,
        after,
        grid=(rows // block,),
        out_specs=[blocked, pl.BlockSpec((slot_total, width), lambda i: (0, 0))],
        out_shape=[shape((rows, width), f32), shape((slot_total, width), bf16)],
        scratch_shapes=[pltpu.VMEM((rows, width), bf16)],
    )


def expert_kernel(
    send_ref, g_ref, in_hbm, out_hbm,
    back_ref, result_ref, arrived_ref,
    w_in, w_out, x_all, slots_all, result_all,
    w_sems, send_sems, recv_sems, back_sems, back_recv, keep_sems,
    *, rows, sub,
):
    groups, capacity, width = send_ref.shape
    me = lax.axis_index("exp")
    units = w_in.shape[0]
    sources = rows // capacity
    blocks = groups // sources
    mine = me // sources
    count = units // sub
    loads = []
    for f in range(count):
        part = slice(f * sub, (f + 1) * sub)
        pair = [
            pltpu.make_async_copy(hbm.at[part], vmem.at[part], w_sems.at[n, f])
            for n, (hbm, vmem) in enumerate(((in_hbm, w_in), (out_hbm, w_out)))
        ]
        for load in pair:
            load.start()
        loads.append(pair)
    greet()
    def send_block(j, carry):
        block = lax.rem(mine + blocks - j, blocks)

        def send(i, inner):
            peer = block * sources + i

            @pl.when(peer == me)
            def _():
                pltpu.make_async_copy(send_ref.at[me], x_all.at[me], recv_sems.at[me]).start()

            @pl.when(peer != me)
            def _():
                remote(
                    send_ref.at[peer], x_all.at[me], send_sems.at[peer], recv_sems.at[me], peer
                ).start()

            return inner

        return lax.fori_loop(0, sources, send, carry)

    lax.fori_loop(0, blocks, send_block, 0)

    def work(j, wait_weights):
        first_source = lax.rem(mine + j, blocks) * sources

        def arrive(i, carry):
            source = first_source + i
            remote(
                send_ref.at[source], x_all.at[source], send_sems.at[source], recv_sems.at[source],
                source,
            ).wait_recv()
            return carry

        lax.fori_loop(0, sources, arrive, 0)
        x = x_all[pl.ds(first_source, sources)].reshape(rows, width)
        g = g_ref[pl.ds(first_source, sources)].reshape(rows, width)

        def first(f):
            part = slice(f * sub, (f + 1) * sub)
            if wait_weights:
                for load in loads[f]:
                    load.wait()
            return nt(x, w_in[part]), nt(g, w_out[part])

        def second(hidden, grad_activated):
            activated, slope = gelu_parts(hidden)
            return activated.astype(bf16), (grad_activated * slope).astype(bf16)

        sums = None
        ahead, behind = first(0), None
        for f in range(count + 1):
            now = ahead
            if f + 1 < count:
                ahead = first(f + 1)
            if behind is not None:
                part = slice((f - 1) * sub, f * sub)
                terms = nn(behind[1], w_in[part]), nn(behind[0], w_out[part])
                sums = terms if sums is None else (sums[0] + terms[0], sums[1] + terms[1])
            if f < count:
                behind = second(*now)
        dims = (sources, capacity, width)
        slots_all[pl.ds(first_source, sources)] = sums[0].astype(bf16).reshape(dims)
        result_all[pl.ds(first_source, sources)] = sums[1].astype(bf16).reshape(dims)

        def answer(i, carry):
            peer = first_source + i

            @pl.when(peer == me)
            def _():
                pltpu.make_async_copy(slots_all.at[me], back_ref.at[me], back_recv.at[me]).start()

            @pl.when(peer != me)
            def _():
                remote(
                    slots_all.at[peer], back_ref.at[me], back_sems.at[peer], back_recv.at[me], peer
                ).start()

            return carry

        lax.fori_loop(0, sources, answer, 0)

    work(0, True)

    def later(j, carry):
        work(j, False)
        return carry

    lax.fori_loop(1, blocks, later, 0)
    keeps = [
        pltpu.make_async_copy(result_all, result_ref, keep_sems.at[0]),
        pltpu.make_async_copy(x_all, arrived_ref, keep_sems.at[1]),
    ]
    for keep in keeps:
        keep.start()
    def close(peer, carry):
        @pl.when(peer != me)
        def _():
            remote(
                send_ref.at[peer], x_all.at[peer], send_sems.at[peer], recv_sems.at[peer], peer
            ).wait_send()
            remote(
                slots_all.at[peer], back_ref.at[peer], back_sems.at[peer], back_recv.at[peer], peer
            ).wait_send()

        remote(
            slots_all.at[peer], back_ref.at[peer], back_sems.at[peer], back_recv.at[peer], peer
        ).wait_recv()
        return carry

    lax.fori_loop(0, groups, close, 0)

    for keep in keeps:
        keep.wait()


def expert_main(send, g, w_in, w_out, rows=256, sub=512, after=()):
    groups, capacity, width = send.shape
    units = w_in.shape[0]
    dma = pltpu.SemaphoreType.DMA
    return launch(
        functools.partial(expert_kernel, rows=rows, sub=sub),
        (send, g, w_in, w_out),
        [ANY, whole(g), ANY, ANY],
        60,
        after,
        collective_id=1,
        out_specs=[ANY] * 3,
        out_shape=[shape(send.shape, bf16)] * 3,
        scratch_shapes=[pltpu.VMEM((units, width), bf16)] * 2
        + [pltpu.VMEM(send.shape, bf16)] * 3
        + [dma((2, units // sub))]
        + [dma((groups,))] * 4
        + [dma((2,))],
    )


def grad_steps(held, place, w_in, w_out, total, sub):
    devices, slots, width = held.shape[2:]
    x = held[place, 0].reshape(devices * slots, width)
    g = held[place, 1].reshape(devices * slots, width)
    count = w_in.shape[0] // sub

    def rows(r):
        return slice(r * sub, (r + 1) * sub)

    def first(r):
        return nt(w_in[rows(r)], x), nt(w_out[rows(r)], g)

    def second(hidden, grad_activated):
        activated, slope = gelu_parts(hidden)
        return activated.astype(bf16), (grad_activated * slope).astype(bf16)

    def third(activated, grad_hidden, r):
        total[0, rows(r)] += nn(grad_hidden, x)
        total[1, rows(r)] += nn(activated, g)

    ahead, behind = first(0), None
    for r in range(count):
        now = ahead
        if r + 1 < count:
            ahead = first(r + 1)
        if behind is not None:
            third(*behind, r - 1)
        behind = second(*now)
    third(*behind, count - 1)


def share_copies(in_hbm, out_hbm, w_in, w_out, sems):
    part = pl.ds(lax.axis_index("rep") * w_in.shape[0], w_in.shape[0])
    return [
        pltpu.make_async_copy(in_hbm.at[part], w_in, sems.at[0]),
        pltpu.make_async_copy(out_hbm.at[part], w_out, sems.at[1]),
    ]


def plane_copies(held, sems, place, x_ref, first_ref, later_ref, start):
    devices, slots = held.shape[2:4]
    split = first_ref.shape[1]
    part = pl.ds(start, devices)
    return [
        pltpu.make_async_copy(source, target, sems.at[place, n])
        for n, (source, target) in enumerate(
            (
                (x_ref, held.at[place, 0]),
                (first_ref.at[part], held.at[place, 1, :, pl.ds(0, split)]),
                (later_ref.at[part], held.at[place, 1, :, pl.ds(split, slots - split)]),
            )
        )
    ]


def own_grad_kernel(
    x_ref, g_ref, in_hbm, out_hbm, send_ref, vec_ref, sums_ref, recv_ref, vec_recv,
    held, w_in, w_out, total, sems, w_sems, out_sems, send_sems, recv_sems, vec_sends, vec_recvs, *, sub,
):
    copies = share_copies(in_hbm, out_hbm, w_in, w_out, w_sems)
    for kind, ref in enumerate((x_ref, g_ref)):
        copies.append(pltpu.make_async_copy(ref, held.at[0, kind], sems.at[0, kind]))
    for copy in copies:
        copy.start()
    greet()
    start_exchange(send_ref, recv_ref, send_sems, recv_sems, 2)
    start_exchange(vec_ref, vec_recv, vec_sends, vec_recvs)
    total[...] = jnp.zeros_like(total)
    for copy in copies:
        copy.wait()
    grad_steps(held, 0, w_in, w_out, total, sub)
    copy = pltpu.make_async_copy(total, sums_ref, out_sems.at[0])
    copy.start()
    finish_exchange(send_ref, recv_ref, send_sems, recv_sems, 2)
    finish_exchange(vec_ref, vec_recv, vec_sends, vec_recvs)
    copy.wait()


def grad_scratch(sets, devices, slots, width, share):
    dma = pltpu.SemaphoreType.DMA
    return [
        pltpu.VMEM((sets, 2, devices, slots, width), bf16),
        pltpu.VMEM((share, width), bf16),
        pltpu.VMEM((share, width), bf16),
        pltpu.VMEM((2, share, width), f32),
        dma((max(sets, 2), 3)),
        dma((2,)),
        dma((2,)),
    ]


def own_grads(x, g, w_in, w_out, send, vectors, sub=256, after=()):
    groups, slots, width = g.shape
    share = w_in.shape[0] // lax.axis_size("rep")
    return launch(
        functools.partial(own_grad_kernel, sub=sub),
        (x, g, w_in, w_out, send, vectors),
        [ANY] * 6,
        15,
        after,
        collective_id=7,
        out_specs=[ANY] * 3,
        out_shape=[shape((2, share, width), f32), shape(send.shape, bf16), shape(vectors.shape, f32)],
        scratch_shapes=grad_scratch(1, groups, slots, width, share)
        + exchange_scratch(send.shape[0])
        + exchange_scratch(groups),
    )


HOLDERS = ((3, 0, 3, 0), (4, 3, 0, 1), (5, 4, 1, 2))


def rows_of(order, xs, firsts_ref, laters_ref, held, sems, place, action):
    z, copies = lax.axis_index("rep"), lax.axis_size("rep")
    low = z < 2
    plane = (z + 1 - 2 * lax.rem(z, 2), jnp.where(low, 2, 1), jnp.where(low, 3, 0))[order]
    shift = lax.rem(plane - z + copies, copies) - 1
    first_ref, later_ref = firsts_ref.at[shift], laters_ref.at[plane]
    if action == "wait":
        for copy in plane_copies(held, sems, place, xs[0], first_ref, later_ref, 0):
            copy.wait()
        return
    for at, index in enumerate(HOLDERS[order]):

        @pl.when(z == at)
        def _(index=index):
            for copy in plane_copies(held, sems, place, xs[index], first_ref, later_ref, 0):
                copy.start()


def two_grad_kernel(*refs, sub):
    xs = refs[:6]
    firsts_ref, laters_ref, in_hbm, out_hbm, before_ref, send_ref, sums_ref, recv_ref = refs[6:14]
    held, w_in, w_out, total, sems, w_sems, out_sems, send_sems, recv_sems = refs[14:]
    step = pl.program_id(0)
    weights = share_copies(in_hbm, out_hbm, w_in, w_out, w_sems)
    load = pltpu.make_async_copy(before_ref, total, out_sems.at[0])

    @pl.when(step == 0)
    def _():
        for copy in weights:
            copy.start()
        rows_of(0, xs, firsts_ref, laters_ref, held, sems, 0, "start")
        load.start()
        rows_of(1, xs, firsts_ref, laters_ref, held, sems, 1, "start")
        greet()
        start_exchange(send_ref, recv_ref, send_sems, recv_sems, 2)
        for copy in weights + [load]:
            copy.wait()

    rows_of(0, xs, firsts_ref, laters_ref, held, sems, step, "wait")
    grad_steps(held, step, w_in, w_out, total, sub)

    @pl.when(step == 1)
    def _():
        copy = pltpu.make_async_copy(total, sums_ref, out_sems.at[0])
        copy.start()
        finish_exchange(send_ref, recv_ref, send_sems, recv_sems, 2)
        copy.wait()


def two_grads(xs, firsts, laters, w_in, w_out, before, send, sub=256, after=()):
    groups, capacity, width = xs[0].shape
    share = w_in.shape[0] // lax.axis_size("rep")
    return launch(
        functools.partial(two_grad_kernel, sub=sub),
        (*xs, firsts, laters, w_in, w_out, before, send),
        [ANY] * 12,
        27,
        after,
        grid=(2,),
        collective_id=4,
        out_specs=[ANY] * 2,
        out_shape=[shape((2, share, width), f32), shape(send.shape, bf16)],
        scratch_shapes=grad_scratch(2, groups, capacity, width, share)
        + exchange_scratch(send.shape[0]),
    )


def last_grad_kernel(shard_ref, *refs, parts):
    xs = refs[:6]
    firsts_ref, laters_ref, in_ref, out_ref, before_ref, gin_ref, gout_ref, held, sems = refs[6:]

    @pl.when(pl.program_id(0) == 0)
    def _():
        rows_of(2, xs, firsts_ref, laters_ref, held, sems, 0, "start")
        rows_of(2, xs, firsts_ref, laters_ref, held, sems, 0, "wait")

    devices, slots, width = held.shape[2:]
    count = devices // parts

    def rows(p, kind):
        return held[0, kind, p * count : (p + 1) * count].reshape(count * slots, width)

    def first(p):
        return nt(in_ref[...], rows(p, 0)), nt(out_ref[...], rows(p, 1))

    grad_in, grad_out = before_ref[0], before_ref[1]
    ahead = first(0)
    for p in range(parts):
        hidden, grad_activated = ahead
        if p + 1 < parts:
            ahead = first(p + 1)
        activated, slope = gelu_parts(hidden)
        grad_out += nn(activated.astype(bf16), rows(p, 1))
        grad_in += nn((grad_activated * slope).astype(bf16), rows(p, 0))
    gin_ref[...] = grad_in
    gout_ref[...] = grad_out


def last_grads(xs, firsts, laters, shard, w_in, w_out, before, block=256, parts=2, after=()):
    groups, capacity, width = xs[0].shape
    share = w_in.shape[0] // lax.axis_size("rep")
    steps = share // block
    weights = pl.BlockSpec((block, width), lambda i, shard: (shard[0] * steps + i, 0))
    both = pl.BlockSpec((2, block, width), lambda i, shard: (0, i, 0))
    blocked = pl.BlockSpec((block, width), lambda i, shard: (i, 0))

    def kernel(*refs):
        last_grad_kernel(*refs[:12], *refs[12 + len(after) :], parts=parts)

    return pl.pallas_call(
        kernel,
        grid_spec=pltpu.PrefetchScalarGridSpec(
            num_scalar_prefetch=1,
            grid=(steps,),
            in_specs=[ANY] * 8 + [weights] * 2 + [both] + [ANY] * len(after),
            out_specs=[blocked] * 2,
            scratch_shapes=[
                pltpu.VMEM((1, 2, groups, capacity, width), bf16),
                pltpu.SemaphoreType.DMA((1, 3)),
            ],
        ),
        out_shape=[shape((share, width), f32)] * 2,
        compiler_params=params(),
        cost_estimate=pl.CostEstimate(flops=int(1e9), bytes_accessed=int(1e6), transcendentals=0),
    )(shard, *xs, firsts, laters, w_in, w_out, before, *after)


def fence_kernel(*refs):
    pass


def fence(arrays, after):
    count = len(arrays)
    return launch(
        fence_kernel,
        tuple(arrays),
        [ANY] * count,
        1,
        after,
        out_specs=[ANY] * count,
        out_shape=[shape(a.shape, a.dtype) for a in arrays],
        input_output_aliases={n: n for n in range(count)},
    )


def back_kernel(
    back_ref, place_ref, mid_ref, cot_ref, len_ref, gain_ref, w_ref,
    gmid_ref, branch_ref, gmix_ref, ggain_ref, gshift_ref,
):
    step = pl.program_id(0)
    block = mid_ref.shape[0]
    grad_sent = nn(row_pick(place_ref[...], back_ref.shape[0]), back_ref[...])
    normal, inverse = normalize(mid_ref[...])
    position = step * block + lax.broadcasted_iota(jnp.int32, (block, 1), 0)
    grad_final = jnp.where(position < len_ref[0], cot_ref[...].astype(f32), 0.0)
    grad_middle = grad_final + norm_backward(grad_sent, normal, inverse, gain_ref[...])
    gmid_ref[...] = grad_middle
    branch = grad_middle.astype(bf16)
    branch_ref[...] = branch
    gmix_ref[...] = nt(branch, w_ref[...]).astype(bf16)

    @pl.when(step == 0)
    def _():
        ggain_ref[...] = jnp.zeros_like(ggain_ref)
        gshift_ref[...] = jnp.zeros_like(gshift_ref)

    ggain_ref[...] += jnp.sum(grad_sent * normal, axis=0, keepdims=True)
    gshift_ref[...] += jnp.sum(grad_sent, axis=0, keepdims=True)


def middle_back(back, place, middle, cotangent, lengths, gain, w_output, block=256, after=()):
    rows, width = middle.shape
    blocked = row_spec(block, width)
    vector = pl.BlockSpec((1, width), lambda i: (0, 0))
    return launch(
        back_kernel,
        (back, place, middle, cotangent, lengths, gain, w_output,),
        [
            whole(back),
            pl.BlockSpec((8, block), lambda i: (0, i)),
            blocked,
            blocked,
            pl.BlockSpec(memory_space=pltpu.SMEM),
            whole(gain),
            whole(w_output),
        ],
        12,
        after,
        grid=(rows // block,),
        out_specs=[blocked, blocked, blocked, vector, vector],
        out_shape=[shape((rows, width), f32)]
        + [shape((rows, width), bf16)] * 2
        + [shape((1, width), f32)] * 2,
    )


def weight_grad_kernel(m_ref, branch_ref, n_ref, gq_ref, gk_ref, gv_ref, o_ref):
    groups, _, _, share, width = o_ref.shape

    def put(n, left, right_ref):
        o_ref[:, 0, n] = nn(left, right_ref[...]).reshape(groups, share, width).astype(bf16)

    put(0, m_ref[...].T, branch_ref)
    left = n_ref[...].T
    for n, ref in enumerate((gq_ref, gk_ref, gv_ref)):
        put(n + 1, left, ref)


def weight_grads(mixed, branch, normed, gq, gk, gv, groups, copies, after=()):
    rows, width = mixed.shape
    block = width // copies
    dims = (groups, copies, 4, block // groups, width)
    column = pl.BlockSpec((rows, block), lambda i: (0, i))
    return launch(
        weight_grad_kernel,
        (mixed, branch, normed, gq, gk, gv),
        [column, whole(branch), column] + [whole(a) for a in (gq, gk, gv)],
        16,
        after,
        grid=(copies,),
        out_specs=pl.BlockSpec((groups, 1) + dims[2:], lambda i: (0, i, 0, 0, 0)),
        out_shape=shape(dims, bf16),
    )


def input_back_kernel(
    gq_ref, gk_ref, gv_ref, wq_ref, wk_ref, wv_ref, x_ref, gmid_ref, gain_ref,
    gin_ref, ggain_ref, gshift_ref,
):
    grad_normed = (
        nt(gq_ref[...], wq_ref[...]) + nt(gk_ref[...], wk_ref[...]) + nt(gv_ref[...], wv_ref[...])
    )
    normal, inverse = normalize(x_ref[...].astype(f32))
    gin_ref[...] = gmid_ref[...] + norm_backward(grad_normed, normal, inverse, gain_ref[...])

    @pl.when(pl.program_id(0) == 0)
    def _():
        ggain_ref[...] = jnp.zeros_like(ggain_ref)
        gshift_ref[...] = jnp.zeros_like(gshift_ref)

    ggain_ref[...] += jnp.sum(grad_normed * normal, axis=0, keepdims=True)
    gshift_ref[...] += jnp.sum(grad_normed, axis=0, keepdims=True)


def input_back(gq, gk, gv, wq, wk, wv, x, grad_middle, gain, block=256, after=()):
    rows, width = x.shape
    blocked = row_spec(block, width)
    vector = pl.BlockSpec((1, width), lambda i: (0, 0))
    return launch(
        input_back_kernel,
        (gq, gk, gv, wq, wk, wv, x, grad_middle, gain,),
        [blocked] * 3 + [whole(w) for w in (wq, wk, wv)] + [blocked, blocked, whole(gain)],
        14,
        after,
        grid=(rows // block,),
        out_specs=[blocked, vector, vector],
        out_shape=[shape((rows, width), f32)] + [shape((1, width), f32)] * 2,
    )


def chip_add_kernel(dense_ref, oa_ref, ob_ref, kept, got, sems, keep_sems):
    me = lax.axis_index("exp")
    core = lax.rem(me, 2)
    half = kept.shape[0]
    cut = kept.shape[2] // 2
    sibling = at_exp(me + 1 - 2 * core)
    copies = []
    for n in range(half):
        keep = pltpu.make_async_copy(dense_ref.at[2 * n + core], kept.at[n], keep_sems.at[0, n])
        give = push(dense_ref.at[2 * n + 1 - core], got.at[n], sems.at[0, n], sems.at[1, n], sibling)
        writes = [
            pltpu.make_async_copy(
                kept.at[n, :, pl.ds(m * cut, cut)], ref.at[n], keep_sems.at[m + 1, n]
            )
            for m, ref in enumerate((oa_ref, ob_ref))
        ]
        copies.append((keep, give, writes))
        keep.start()
    greet()
    for _, give, _ in copies:
        give.start()
    for n, (keep, give, writes) in enumerate(copies):
        keep.wait()
        give.wait_recv()
        kept[n] = (kept[n].astype(f32) + got[n].astype(f32)).astype(bf16)
        for write in writes:
            write.start()
    for _, give, writes in copies:
        give.wait_send()
        for write in writes:
            write.wait()


def chip_add(dense, after=()):
    half = dense.shape[0] // 2
    dims = (half,) + dense.shape[1:]
    cut = dims[:2] + (dims[2] // 2,) + dims[3:]
    dma = pltpu.SemaphoreType.DMA
    return launch(
        chip_add_kernel,
        (dense,),
        [ANY],
        8,
        after,
        collective_id=6,
        out_specs=[ANY] * 2,
        out_shape=[shape(cut, bf16)] * 2,
        scratch_shapes=[pltpu.VMEM(dims, bf16)] * 2 + [dma((2, half)), dma((3, half))],
    )


def near_add_kernel(a_ref, b_ref, vec_ref, o_ref):
    cut = a_ref.shape[2]
    o_ref[0, :cut] = jnp.sum(a_ref[:, 0].astype(f32), axis=0).astype(bf16)
    o_ref[0, cut : 2 * cut] = jnp.sum(b_ref[:, 0].astype(f32), axis=0).astype(bf16)
    vectors = jnp.sum(vec_ref[:, 0], axis=0)
    high = vectors.astype(bf16)
    low = (vectors - high.astype(f32)).astype(bf16)
    lanes = vectors.shape[1]
    o_ref[0, 2 * cut] = jnp.zeros(o_ref.shape[2:], bf16)
    o_ref[0, 2 * cut, :, :lanes] = high
    o_ref[0, 2 * cut, :, lanes : 2 * lanes] = low


def near_add(a, b, vectors, after=()):
    groups, copies, cut = a.shape[:3]
    dims = (2 * cut + 1,) + a.shape[3:]
    spec = pl.BlockSpec((groups, 1) + a.shape[2:], lambda i: (0, i, 0, 0, 0))
    return launch(
        near_add_kernel,
        (a, b, vectors),
        [
            spec,
            spec,
            pl.BlockSpec((vectors.shape[0], 1) + vectors.shape[2:], lambda i: (0, i, 0, 0)),
        ],
        6,
        after,
        grid=(copies,),
        out_specs=pl.BlockSpec((1,) + dims, lambda i: (i, 0, 0, 0)),
        out_shape=shape((copies,) + dims, bf16),
    )


def far_add_kernel(parts_ref, *out_refs):
    for n, ref in enumerate(out_refs):
        ref[...] = jnp.sum(parts_ref[:, n].astype(f32), axis=0)


def far_add(parts, after=()):
    _, count, share, width = parts.shape
    return launch(
        far_add_kernel,
        (parts,),
        [whole(parts)],
        1,
        after,
        out_specs=[pl.BlockSpec((share, width), lambda: (0, 0))] * count,
        out_shape=[shape((share, width), f32)] * count,
    )


def output_kernel(back_ref, place_ref, mid_ref, o_ref):
    combined = nn(row_pick(place_ref[...], back_ref.shape[0]), back_ref[...])
    o_ref[...] = (mid_ref[...] + combined).astype(bf16)


def combine(back, place, middle, block=256, after=()):
    rows, width = middle.shape
    return launch(
        output_kernel,
        (back, place, middle),
        [
            whole(back),
            pl.BlockSpec((8, block), lambda i: (0, i)),
            row_spec(block, width),
        ],
        7,
        after,
        grid=(rows // block,),
        out_specs=row_spec(block, width),
        out_shape=shape((rows, width), bf16),
    )


def body(
    inputs,
    cotangent,
    token_ids,
    lengths,
    hash_table,
    first_gain,
    first_shift,
    w_query,
    w_key,
    w_value,
    w_output,
    second_gain,
    second_shift,
    expert_in,
    expert_out,
):
    seq_count, seq_len, width = inputs.shape
    rows = seq_count * seq_len
    groups = lax.axis_size("exp")
    copies = lax.axis_size("rep")
    place_z = lax.axis_index("rep")
    capacity = rows // groups
    slot_total = groups * capacity
    x = inputs.reshape(rows, width)
    cot = cotangent.reshape(rows, width)
    gain_one, shift_one, gain_two, shift_two = (
        v.reshape(1, width) for v in (first_gain, first_shift, second_gain, second_shift)
    )
    table_rows = -(-hash_table.shape[0] // (8 * 128)) * 8
    table = jnp.pad(hash_table, (0, table_rows * 128 - hash_table.shape[0]))
    table = table.reshape(table_rows, 128)

    place_e = lax.axis_index("exp")

    def exchange(parts, axis="exp"):
        return lax.all_to_all(parts, axis, split_axis=0, concat_axis=0, tiled=True)

    def gather(array):
        return lax.all_gather(array, "rep", axis=0, tiled=False)

    flat = (slot_total, width)
    by_group = (groups, capacity, width)
    w_in, w_out = expert_in[0], expert_out[0]
    first = max(16, capacity // 4)
    place, grad_send, send_first = route(
        lengths, token_ids.reshape(1, rows), table, cot, groups, capacity, first
    )
    firsts = gather(send_first)
    grads = exchange(grad_send)
    normed, q, k, v = project(x, gain_one, shift_one, w_query, w_key, w_value, after=(grad_send,))
    mixed, logs = attend(lengths, q, k, v)
    (grads,) = fence((grads,), (mixed,))
    laters = gather(grads[:, first:])
    middle, send_rows = middle_and_send(
        x, mixed, w_output, gain_two, shift_two, place, slot_total, after=(grads,)
    )
    grad_back, result, sent = expert_main(send_rows.reshape(by_group), grads, w_in, w_out)

    def hops(up, down, start):
        ups = [(z, z + 1) for z in range(start, copies - 1)]
        downs = [(z, z - 1) for z in range(1, copies - start)]
        return lax.ppermute(up, "rep", ups), lax.ppermute(down, "rep", downs)

    sent_u1, sent_d1 = hops(sent, sent, 0)
    returned = exchange(result)
    grad_middle, branch, grad_mixed, grad_second_gain, grad_second_shift = middle_back(
        grad_back.reshape(flat), place, middle, cot, lengths, gain_two, w_output
    )
    gq, gk, gv, firsts = attend_back(lengths, q, k, v, mixed, grad_mixed, logs, firsts)
    parts = weight_grads(mixed, branch, normed, gq, gk, gv, groups, copies)
    chip_a, chip_b = chip_add(parts, after=(returned,))
    sent_u1, sent_d1 = fence((sent_u1, sent_d1), (chip_a,))
    sent_u2, sent_d2 = hops(sent_u1, sent_d1, 1)
    grad_inputs, grad_first_gain, grad_first_shift = input_back(
        gq, gk, gv, w_query, w_key, w_value, x, grad_middle, gain_one, after=(sent_u1,)
    )
    vectors = jnp.concatenate(
        [grad_first_gain, grad_first_shift, grad_second_gain, grad_second_shift], axis=0
    )
    part = width // (groups * copies)
    vectors = vectors.reshape(4, copies, groups, part).transpose(2, 1, 0, 3)
    vectors = jnp.pad(vectors, ((0, 0), (0, 0), (0, part - 4), (0, 128 - part)))
    sums, near_a, vectors = own_grads(
        sent, grads, w_in, w_out, chip_a, vectors
    )
    sent_u2, sent_d2 = fence((sent_u2, sent_d2), (sums,))
    sent_u3, sent_d3 = hops(sent_u2, sent_d2, 2)
    xs = (sent_u1, sent_u2, sent_u3, sent_d1, sent_d2, sent_d3)
    early = (sent_u1, sent_u2, sent_u2, sent_d1, sent_d2, sent_d2)
    sums, near_b = two_grads(early, firsts, laters, w_in, w_out, sums, chip_b)
    near_all = near_add(near_a, near_b, vectors)
    far = exchange(near_all, "rep")
    outputs = combine(returned.reshape(flat), place, middle, after=(near_all,))
    grad_expert_in, grad_expert_out = last_grads(
        xs, firsts, laters, place_z.astype(jnp.int32).reshape(1), w_in, w_out, sums, after=(outputs,)
    )
    dense_output, dense_query, dense_key, dense_value, vectors = far_add(
        far, after=(grad_expert_in,)
    )
    vectors = (vectors[:4, :128] + vectors[:4, 128:256])[:, :part]
    return (
        outputs.reshape(seq_count, seq_len, width),
        grad_inputs.reshape(seq_count, seq_len, width),
        vectors[0],
        vectors[1],
        dense_query,
        dense_key,
        dense_value,
        dense_output,
        vectors[2],
        vectors[3],
        grad_expert_in[None],
        grad_expert_out[None],
    )


def solution(mesh):
    both = ("rep", "exp")
    placed = (
        P(both, None, None),
        P(both, None, None),
        P(both, None),
        P(both),
    ) + (P(),) * 9 + (P("exp", None, None),) * 2
    return jax.shard_map(
        body,
        mesh=mesh,
        in_specs=placed,
        out_specs=(
            P(both, None, None),
            P(both, None, None),
            P(both),
            P(both),
            P(both, None),
            P(both, None),
            P(both, None),
            P(both, None),
            P(both),
            P(both),
            P("exp", "rep", None),
            P("exp", "rep", None),
        ),
        check_vma=False,
    )
```

```python
import functools
import math

import jax
import jax.numpy as jnp
from jax import lax
from jax.experimental import pallas as pl
from jax.experimental.pallas import tpu as pltpu
from jax.sharding import PartitionSpec as P

HEAD_DIM = 64
PAIR = 2 * HEAD_DIM
MASKED = -1e30
epsilon = 1e-05
bf16, f32 = jnp.bfloat16, jnp.float32
MESH = pl.DeviceIdType.MESH
ANY = pl.BlockSpec(memory_space=pl.ANY)
VMEM_BYTES = 56 * 1024 * 1024
PARTS = 4


def params(collective_id=None):
    if collective_id is None:
        return pltpu.CompilerParams(vmem_limit_bytes=VMEM_BYTES)
    return pltpu.CompilerParams(
        vmem_limit_bytes=VMEM_BYTES, collective_id=collective_id, has_side_effects=True
    )


def launch(kernel, operands, in_specs, micros, after=(), collective_id=None, **options):
    count = len(operands)

    def run(*refs):
        kernel(*refs[:count], *refs[count + len(after) :])

    return pl.pallas_call(
        run,
        in_specs=list(in_specs) + [pl.BlockSpec(memory_space=pl.ANY)] * len(after),
        compiler_params=params(collective_id),
        cost_estimate=pl.CostEstimate(
            flops=int(1e9), bytes_accessed=int(1e6), transcendentals=0
        ),
        **options,
    )(*operands, *after)


def at_rep(place):
    return {"rep": place}


def at_exp(place):
    return {"exp": place}


def greet(*axes):
    barrier = pltpu.get_barrier_semaphore()
    count = 0
    for axis in axes or ("exp",):
        size, me = lax.axis_size(axis), lax.axis_index(axis)

        def tell(step, carry, axis=axis, size=size, me=me):
            peer = lax.rem(me + step, size)
            pl.semaphore_signal(barrier, inc=1, device_id={axis: peer}, device_id_type=MESH)
            return carry

        lax.fori_loop(1, size, tell, 0)
        count += size - 1
    pl.semaphore_wait(barrier, count)


def push(source, target, send_sem, recv_sem, device):
    return pltpu.make_async_remote_copy(
        src_ref=source,
        dst_ref=target,
        send_sem=send_sem,
        recv_sem=recv_sem,
        device_id=device,
        device_id_type=MESH,
    )


def remote(source, target, send_sem, recv_sem, peer):
    return push(source, target, send_sem, recv_sem, at_exp(peer))


def start_exchange(send_ref, recv_ref, send_sems, recv_sems, stride=1, axis="exp"):
    groups = send_ref.shape[0]
    me = lax.axis_index(axis)
    mine = me // stride
    pltpu.make_async_copy(send_ref.at[mine], recv_ref.at[mine], recv_sems.at[mine]).start()

    def send(step, carry):
        entry = lax.rem(mine + step, groups)
        peer = entry * stride + lax.rem(me, stride)
        push(
            send_ref.at[entry], recv_ref.at[mine], send_sems.at[entry], recv_sems.at[mine], {axis: peer}
        ).start()
        return carry

    lax.fori_loop(1, groups, send, 0)


def finish_exchange(send_ref, recv_ref, send_sems, recv_sems, stride=1, axis="exp"):
    groups = send_ref.shape[0]
    me = lax.axis_index(axis)
    mine = me // stride
    pltpu.make_async_copy(send_ref.at[mine], recv_ref.at[mine], recv_sems.at[mine]).wait()

    def wait(step, carry):
        entry = lax.rem(mine + step, groups)
        peer = entry * stride + lax.rem(me, stride)
        copy = push(
            send_ref.at[entry], recv_ref.at[entry], send_sems.at[entry], recv_sems.at[entry], {axis: peer}
        )
        copy.wait_send()
        copy.wait_recv()
        return carry

    lax.fori_loop(1, groups, wait, 0)


def remote(source, target, send_sem, recv_sem, peer):
    return push(source, target, send_sem, recv_sem, at_exp(peer))


def exchange_planes(send_ref, recv_ref, send_sems, recv_sems, begin):
    copies, groups = send_ref.shape[:2]
    z, me = lax.axis_index("rep"), lax.axis_index("exp")

    def shift(n, carry):
        plane = lax.rem(z + n + 1, copies)
        own = pltpu.make_async_copy(send_ref.at[plane, me], recv_ref.at[n, me], recv_sems.at[n, me])
        own.start() if begin else own.wait()

        def one(step, inner):
            peer = lax.rem(me + step, groups)
            entry = me if begin else peer
            copy = push(
                send_ref.at[plane, peer], recv_ref.at[n, entry],
                send_sems.at[n, peer], recv_sems.at[n, entry], at_exp(peer),
            )
            if begin:
                copy.start()
            else:
                copy.wait_send()
                copy.wait_recv()
            return inner

        return lax.fori_loop(1, groups, one, carry)

    lax.fori_loop(0, copies - 1, shift, 0)


def exchange_scratch(groups):
    return [pltpu.SemaphoreType.DMA((groups,))] * 2


def shape(dims, kind):
    return jax.ShapeDtypeStruct(dims, kind)


def nn(left, right):
    return lax.dot_general(left, right, (((1,), (0,)), ((), ())), preferred_element_type=f32)


def nt(left, right):
    return lax.dot_general(left, right, (((1,), (1,)), ((), ())), preferred_element_type=f32)


def tn(left, right):
    return lax.dot_general(left, right, (((0,), (0,)), ((), ())), preferred_element_type=f32)


def whole(array):
    return pl.BlockSpec(array.shape, lambda *_: (0,) * array.ndim)


def row_spec(rows, width):
    return pl.BlockSpec((rows, width), lambda i: (i, 0))


def normalize(values):
    average = jnp.mean(values, axis=1, keepdims=True)
    centered = values - average
    spread = jnp.mean(centered * centered, axis=1, keepdims=True)
    inverse = lax.rsqrt(spread + epsilon)
    return centered * inverse, inverse


def norm_backward(grad_out, normal, inverse, gain):
    grad_normal = grad_out * gain
    inner = (
        grad_normal
        - jnp.mean(grad_normal, axis=1, keepdims=True)
        - normal * jnp.mean(grad_normal * normal, axis=1, keepdims=True)
    )
    return inner * inverse


def gelu_parts(hidden):
    share = 0.5 * (1.0 + lax.erf(hidden * (1.0 / math.sqrt(2.0))))
    slope = share + hidden * jnp.exp(-0.5 * hidden * hidden) * (1.0 / math.sqrt(2.0 * math.pi))
    return hidden * share, slope


def route_kernel(
    len_ref, ids_ref, table_ref, cot_ref, place_ref, send_ref, *, groups, capacity
):
    seq_len = ids_ref.shape[1]
    slot_total = groups * capacity
    high_count, low_count = table_ref.shape
    ids = ids_ref[...]
    high, low = ids // low_count, ids % low_count
    high_pick = (
        lax.broadcasted_iota(jnp.int32, (high_count, seq_len), 0) == high
    ).astype(f32).astype(bf16)
    picked = tn(table_ref[...].astype(bf16), high_pick)
    low_pick = lax.broadcasted_iota(jnp.int32, (low_count, seq_len), 0) == low
    expert = jnp.sum(jnp.where(low_pick, picked, 0.0), axis=0, keepdims=True)
    valid = lax.broadcasted_iota(jnp.int32, (1, seq_len), 1) < len_ref[0]
    own = lax.broadcasted_iota(jnp.int32, (groups, seq_len), 0).astype(f32)
    chosen = jnp.where((own == expert) & valid, 1.0, 0.0)
    earlier = (
        lax.broadcasted_iota(jnp.int32, (seq_len, seq_len), 0)
        < lax.broadcasted_iota(jnp.int32, (seq_len, seq_len), 1)
    ).astype(f32).astype(bf16)
    before = nn(chosen.astype(bf16), earlier)
    slot = jnp.sum(before * chosen, axis=0, keepdims=True)
    place = jnp.where(valid & (slot < capacity), expert * capacity + slot, float(slot_total))
    place_ref[...] = jnp.broadcast_to(place, place_ref.shape)
    first = send_ref.shape[1]
    entry = lax.broadcasted_iota(jnp.int32, (groups * first, seq_len), 0)
    slots = (entry // first * capacity + entry % first).astype(f32)
    pick = jnp.where(slots == place, 1.0, 0.0).astype(bf16)
    send_ref[...] = nn(pick, cot_ref[...]).astype(bf16).reshape(send_ref.shape)


def dispatch_kernel(place_ref, cot_ref, send_ref):
    groups, capacity, _ = send_ref.shape
    sent = nn(slot_pick(place_ref[:1], groups * capacity), cot_ref[...])
    send_ref[...] = sent.astype(bf16).reshape(send_ref.shape)


def dispatch(place, cotangent, groups, capacity, after=()):
    dims = (groups, capacity, cotangent.shape[1])
    return launch(
        dispatch_kernel,
        (place, cotangent),
        [whole(place), whole(cotangent)],
        4,
        after,
        out_specs=pl.BlockSpec(dims, lambda: (0, 0, 0)),
        out_shape=shape(dims, bf16),
    )


def slot_pick(place_row, slot_total):
    slots = lax.broadcasted_iota(jnp.int32, (slot_total, place_row.shape[1]), 0).astype(f32)
    return jnp.where(slots == place_row, 1.0, 0.0).astype(bf16)


def row_pick(place_rows, slot_total):
    column = place_rows.T[:, :1]
    slots = lax.broadcasted_iota(jnp.int32, (column.shape[0], slot_total), 1).astype(f32)
    return jnp.where(slots == column, 1.0, 0.0).astype(bf16)


def route(lengths, ids, table, cotangent, groups, capacity, first, after=()):
    rows, width = cotangent.shape
    return launch(
        functools.partial(route_kernel, groups=groups, capacity=capacity),
        (lengths, ids, table, cotangent,),
        [
            pl.BlockSpec(memory_space=pltpu.SMEM),
            whole(ids),
            whole(table),
            whole(cotangent),
        ],
        10,
        after,
        out_specs=[
            pl.BlockSpec((8, rows), lambda: (0, 0)),
            pl.BlockSpec((groups, first, width), lambda: (0, 0, 0)),
        ],
        out_shape=[shape((8, rows), f32), shape((groups, first, width), bf16)],
    )


def project_kernel(x_ref, gain_ref, shift_ref, wq_ref, wk_ref, wv_ref, n_ref, q_ref, k_ref, v_ref):
    normal, _ = normalize(x_ref[...].astype(f32))
    normed = (normal * gain_ref[...] + shift_ref[...]).astype(bf16)
    n_ref[...] = normed
    q_ref[...] = nn(normed, wq_ref[...]).astype(bf16)
    k_ref[...] = nn(normed, wk_ref[...]).astype(bf16)
    v_ref[...] = nn(normed, wv_ref[...]).astype(bf16)


def project(x, gain, shift, wq, wk, wv, block=256, after=()):
    rows, width = x.shape
    return launch(
        project_kernel,
        (x, gain, shift, wq, wk, wv),
        [row_spec(block, width)] + [whole(a) for a in (gain, shift, wq, wk, wv)],
        13,
        after,
        grid=(rows // block,),
        out_specs=[row_spec(block, width)] * 4,
        out_shape=[shape((rows, width), bf16)] * 4,
    )


def head_parts(length, block, seq_len):
    lane = lax.broadcasted_iota(jnp.int32, (1, PAIR), 1)
    position = lax.broadcasted_iota(jnp.int32, (seq_len, 1), 0)
    bias = jnp.where(position < length, 0.0, MASKED).astype(bf16)
    down = lax.broadcasted_iota(jnp.int32, (block, block), 0)
    across = lax.broadcasted_iota(jnp.int32, (block, block), 1)
    return lane // HEAD_DIM, lane % HEAD_DIM == 0, bias, down <= across


def attend_kernel(
    len_ref, q_ref, k_ref, v_ref, o_ref, log_ref, *, block, pairs
):
    seq_len = q_ref.shape[0]
    factor = HEAD_DIM**-0.5 * math.log2(math.e)
    half, first_lane, bias, causal = head_parts(len_ref[0], block, seq_len)
    zero = jnp.zeros_like(bias)
    keys, queries, values = [], [], []
    for pair in range(pairs):
        lanes = slice(pair * PAIR, (pair + 1) * PAIR)
        q, k = q_ref[:, lanes], k_ref[:, lanes]
        value_t = v_ref[:, lanes].T
        for h in range(2):
            spare = jnp.where(first_lane & (half != h), 1.0, 0.0).astype(bf16)
            keys.append(jnp.where(half == h, k, bias * spare))
            queries.append(jnp.where(half == h, q, spare))
            values.append(
                jnp.concatenate(
                    [value_t[h * HEAD_DIM : (h + 1) * HEAD_DIM], jnp.ones((16, seq_len), bf16)],
                    axis=0,
                )
            )
    order = [(h, j) for j in range(seq_len // block) for h in range(2 * pairs)]

    def score(h, j):
        end = (j + 1) * block
        return nt(keys[h][:end], queries[h][j * block : end])

    def soften(scores, j):
        last = jnp.where(causal, scores[j * block :], MASKED)
        scores = last if j == 0 else jnp.concatenate([scores[: j * block], last], axis=0)
        highest = jnp.max(scores, axis=0, keepdims=True) * factor
        return jnp.exp2(scores * factor - highest).astype(bf16), highest

    def finish(powers, highest, h, j):
        rows = slice(j * block, (j + 1) * block)
        total = nn(values[h][:, : (j + 1) * block], powers)
        summed = total[HEAD_DIM : HEAD_DIM + 1]
        mixed = total[:HEAD_DIM] * (1.0 / summed)
        o_ref[rows, h * HEAD_DIM : (h + 1) * HEAD_DIM] = mixed.T.astype(bf16)
        log_ref[h // 2, h % 2 : h % 2 + 1, rows] = highest + jnp.log2(summed)

    ahead = score(*order[0])
    behind = None
    for step, (h, j) in enumerate(order):
        scores = ahead
        if step + 1 < len(order):
            ahead = score(*order[step + 1])
        if behind is not None:
            finish(*behind, *order[step - 1])
        behind = soften(scores, j)
    finish(*behind, *order[-1])


def attend(lengths, q, k, v, block=256, pairs=2, after=()):
    rows, width = q.shape
    lanes = pl.BlockSpec((rows, pairs * PAIR), lambda i: (0, i))
    return launch(
        functools.partial(attend_kernel, block=block, pairs=pairs),
        (lengths, q, k, v),
        [pl.BlockSpec(memory_space=pltpu.SMEM)] + [lanes] * 3,
        18,
        after,
        grid=(width // (pairs * PAIR),),
        out_specs=[lanes, pl.BlockSpec((pairs, 2, rows), lambda i: (i, 0, 0))],
        out_shape=[shape((rows, width), bf16), shape((width // PAIR, 2, rows), f32)],
    )


def attend_back_kernel(
    len_ref, q_ref, k_ref, v_ref, o_ref, g_ref, log_ref, send_ref,
    dq_ref, dk_ref, dv_ref, recv_ref, send_sems, recv_sems, *, block, pairs,
):
    @pl.when(pl.program_id(0) == 0)
    def _():
        greet()
        exchange_planes(send_ref, recv_ref, send_sems, recv_sems, True)

    seq_len = q_ref.shape[0]
    blocks = seq_len // block
    scale = HEAD_DIM**-0.5
    factor = scale * math.log2(math.e)
    half, first_lane, bias, causal = head_parts(len_ref[0], block, seq_len)
    zero = jnp.zeros_like(bias)
    keys, queries, values, keys_t, logs, deltas = [], [], [], [], [], []
    for pair in range(pairs):
        lanes = slice(pair * PAIR, (pair + 1) * PAIR)
        q, k, v = q_ref[:, lanes], k_ref[:, lanes], v_ref[:, lanes]
        key_t = k.T
        product = (g_ref[:, lanes].astype(f32) * o_ref[:, lanes].astype(f32)).T
        for h in range(2):
            rows = slice(h * HEAD_DIM, (h + 1) * HEAD_DIM)
            spare = jnp.where(first_lane & (half != h), 1.0, 0.0).astype(bf16)
            keys.append(jnp.where(half == h, k, bias * spare))
            queries.append(jnp.where(half == h, q, spare))
            values.append(jnp.where(half == h, v, zero))
            keys_t.append(key_t[rows])
            logs.append(log_ref[pair, h : h + 1, :])
            deltas.append(jnp.sum(product[rows], axis=0, keepdims=True))
    order = [(h, i) for i in range(blocks) for h in range(2 * pairs)]
    query_sums = [[None] * blocks for _ in range(2 * pairs)]
    kept = {}

    def lanes_of(h):
        return slice((h // 2) * PAIR, (h // 2 + 1) * PAIR)

    def products(h, i):
        rows = slice(i * block, (i + 1) * block)
        return (
            nt(keys[h][rows], queries[h][i * block :]),
            nt(values[h][rows], g_ref[i * block :, lanes_of(h)]),
        )

    def shares_of(scores, grad_shares, h, i):
        shares = jnp.exp2(scores * factor - logs[h][:, i * block :])
        first = jnp.where(causal, shares[:, :block], 0.0)
        if i + 1 < blocks:
            first = jnp.concatenate([first, shares[:, block:]], axis=1)
        grad_scores = first * (grad_shares - deltas[h][:, i * block :])
        return first.astype(bf16), grad_scores.astype(bf16)

    def finish(shares, grad_scores, h, i):
        rows, lanes = slice(i * block, (i + 1) * block), lanes_of(h)
        grad_v = nn(shares, g_ref[i * block :, lanes])
        grad_k = nn(grad_scores, q_ref[i * block :, lanes])
        part = nn(keys_t[h][:, rows], grad_scores)
        for j in range(i, blocks):
            term = part[:, (j - i) * block : (j - i + 1) * block]
            held = query_sums[h][j]
            query_sums[h][j] = term if held is None else held + term
        dq_ref[rows, h * HEAD_DIM : (h + 1) * HEAD_DIM] = (
            (query_sums[h][i] * scale).T.astype(bf16)
        )
        kept[h] = (grad_k, grad_v)
        if h % 2:
            other_k, other_v = kept[h - 1]
            dk_ref[rows, lanes] = (jnp.where(half == 0, other_k, grad_k) * scale).astype(bf16)
            dv_ref[rows, lanes] = jnp.where(half == 0, other_v, grad_v).astype(bf16)

    ahead = products(*order[0])
    behind = None
    for step, (h, i) in enumerate(order):
        now = ahead
        if step + 1 < len(order):
            ahead = products(*order[step + 1])
        if behind is not None:
            finish(*behind, *order[step - 1])
        behind = shares_of(*now, h, i)
    finish(*behind, *order[-1])

    @pl.when(pl.program_id(0) == pl.num_programs(0) - 1)
    def _():
        exchange_planes(send_ref, recv_ref, send_sems, recv_sems, False)


def attend_back(lengths, q, k, v, mixed, grad_mixed, logs, send, block=256, pairs=2, after=()):
    rows, width = q.shape
    lanes = pl.BlockSpec((rows, pairs * PAIR), lambda i: (0, i))
    return launch(
        functools.partial(attend_back_kernel, block=block, pairs=pairs),
        (lengths, q, k, v, mixed, grad_mixed, logs, send),
        [pl.BlockSpec(memory_space=pltpu.SMEM)]
        + [lanes] * 5
        + [pl.BlockSpec((pairs, 2, rows), lambda i: (i, 0, 0)), ANY],
        31,
        after,
        collective_id=3,
        grid=(width // (pairs * PAIR),),
        out_specs=[lanes] * 3 + [ANY],
        out_shape=[shape((rows, width), bf16)] * 3
        + [shape((send.shape[0] - 1,) + send.shape[1:], bf16)],
        scratch_shapes=[pltpu.SemaphoreType.DMA((send.shape[0] - 1, send.shape[1]))] * 2,
    )


def middle_kernel(x_ref, m_ref, w_ref, gain_ref, shift_ref, place_ref, mid_ref, send_ref, sent):
    step = pl.program_id(0)
    block = x_ref.shape[0]
    middle = x_ref[...].astype(f32) + nn(m_ref[...], w_ref[...])
    mid_ref[...] = middle
    normal, _ = normalize(middle)
    sent[pl.ds(step * block, block)] = (normal * gain_ref[...] + shift_ref[...]).astype(bf16)

    @pl.when(step == pl.num_programs(0) - 1)
    def _():
        pick = slot_pick(place_ref[:1], send_ref.shape[0])
        send_ref[...] = nn(pick, sent[...]).astype(bf16)


def middle_and_send(x, mixed, w_output, gain, shift, place, slot_total, block=256, after=()):
    rows, width = x.shape
    blocked = row_spec(block, width)
    return launch(
        middle_kernel,
        (x, mixed, w_output, gain, shift, place,),
        [blocked, blocked] + [whole(a) for a in (w_output, gain, shift, place)],
        10,
        after,
        grid=(rows // block,),
        out_specs=[blocked, pl.BlockSpec((slot_total, width), lambda i: (0, 0))],
        out_shape=[shape((rows, width), f32), shape((slot_total, width), bf16)],
        scratch_shapes=[pltpu.VMEM((rows, width), bf16)],
    )


def expert_kernel(
    send_ref, g_ref, in_hbm, out_hbm,
    back_ref, result_ref, arrived_ref,
    w_in, w_out, x_all, slots_all, result_all,
    w_sems, send_sems, recv_sems, back_sems, back_recv, keep_sems,
    *, rows, sub,
):
    groups, capacity, width = send_ref.shape
    me = lax.axis_index("exp")
    units = w_in.shape[0]
    sources = rows // capacity
    blocks = groups // sources
    mine = me // sources
    count = units // sub
    loads = []
    for f in range(count):
        part = slice(f * sub, (f + 1) * sub)
        pair = [
            pltpu.make_async_copy(hbm.at[part], vmem.at[part], w_sems.at[n, f])
            for n, (hbm, vmem) in enumerate(((in_hbm, w_in), (out_hbm, w_out)))
        ]
        for load in pair:
            load.start()
        loads.append(pair)
    greet()
    def send_block(j, carry):
        block = lax.rem(mine + blocks - j, blocks)

        def send(i, inner):
            peer = block * sources + i

            @pl.when(peer == me)
            def _():
                pltpu.make_async_copy(send_ref.at[me], x_all.at[me], recv_sems.at[me]).start()

            @pl.when(peer != me)
            def _():
                remote(
                    send_ref.at[peer], x_all.at[me], send_sems.at[peer], recv_sems.at[me], peer
                ).start()

            return inner

        return lax.fori_loop(0, sources, send, carry)

    lax.fori_loop(0, blocks, send_block, 0)

    def work(j, wait_weights):
        first_source = lax.rem(mine + j, blocks) * sources

        def arrive(i, carry):
            source = first_source + i
            remote(
                send_ref.at[source], x_all.at[source], send_sems.at[source], recv_sems.at[source],
                source,
            ).wait_recv()
            return carry

        lax.fori_loop(0, sources, arrive, 0)
        x = x_all[pl.ds(first_source, sources)].reshape(rows, width)
        g = g_ref[pl.ds(first_source, sources)].reshape(rows, width)

        def first(f):
            part = slice(f * sub, (f + 1) * sub)
            if wait_weights:
                for load in loads[f]:
                    load.wait()
            return nt(x, w_in[part]), nt(g, w_out[part])

        def second(hidden, grad_activated):
            activated, slope = gelu_parts(hidden)
            return activated.astype(bf16), (grad_activated * slope).astype(bf16)

        sums = None
        ahead, behind = first(0), None
        for f in range(count + 1):
            now = ahead
            if f + 1 < count:
                ahead = first(f + 1)
            if behind is not None:
                part = slice((f - 1) * sub, f * sub)
                terms = nn(behind[1], w_in[part]), nn(behind[0], w_out[part])
                sums = terms if sums is None else (sums[0] + terms[0], sums[1] + terms[1])
            if f < count:
                behind = second(*now)
        dims = (sources, capacity, width)
        slots_all[pl.ds(first_source, sources)] = sums[0].astype(bf16).reshape(dims)
        result_all[pl.ds(first_source, sources)] = sums[1].astype(bf16).reshape(dims)

        def answer(i, carry):
            peer = first_source + i

            @pl.when(peer == me)
            def _():
                pltpu.make_async_copy(slots_all.at[me], back_ref.at[me], back_recv.at[me]).start()

            @pl.when(peer != me)
            def _():
                remote(
                    slots_all.at[peer], back_ref.at[me], back_sems.at[peer], back_recv.at[me], peer
                ).start()

            return carry

        lax.fori_loop(0, sources, answer, 0)

    work(0, True)

    def later(j, carry):
        work(j, False)
        return carry

    lax.fori_loop(1, blocks, later, 0)
    keeps = [
        pltpu.make_async_copy(result_all, result_ref, keep_sems.at[0]),
        pltpu.make_async_copy(x_all, arrived_ref, keep_sems.at[1]),
    ]
    for keep in keeps:
        keep.start()
    def close(peer, carry):
        @pl.when(peer != me)
        def _():
            remote(
                send_ref.at[peer], x_all.at[peer], send_sems.at[peer], recv_sems.at[peer], peer
            ).wait_send()
            remote(
                slots_all.at[peer], back_ref.at[peer], back_sems.at[peer], back_recv.at[peer], peer
            ).wait_send()

        remote(
            slots_all.at[peer], back_ref.at[peer], back_sems.at[peer], back_recv.at[peer], peer
        ).wait_recv()
        return carry

    lax.fori_loop(0, groups, close, 0)

    for keep in keeps:
        keep.wait()


def expert_main(send, g, w_in, w_out, rows=256, sub=512, after=()):
    groups, capacity, width = send.shape
    units = w_in.shape[0]
    dma = pltpu.SemaphoreType.DMA
    return launch(
        functools.partial(expert_kernel, rows=rows, sub=sub),
        (send, g, w_in, w_out),
        [ANY, whole(g), ANY, ANY],
        60,
        after,
        collective_id=1,
        out_specs=[ANY] * 3,
        out_shape=[shape(send.shape, bf16)] * 3,
        scratch_shapes=[pltpu.VMEM((units, width), bf16)] * 2
        + [pltpu.VMEM(send.shape, bf16)] * 3
        + [dma((2, units // sub))]
        + [dma((groups,))] * 4
        + [dma((2,))],
    )


def grad_steps(held, place, w_in, w_out, total, sub):
    devices, slots, width = held.shape[2:]
    x = held[place, 0].reshape(devices * slots, width)
    g = held[place, 1].reshape(devices * slots, width)
    count = w_in.shape[0] // sub

    def rows(r):
        return slice(r * sub, (r + 1) * sub)

    def first(r):
        return nt(w_in[rows(r)], x), nt(w_out[rows(r)], g)

    def second(hidden, grad_activated):
        activated, slope = gelu_parts(hidden)
        return activated.astype(bf16), (grad_activated * slope).astype(bf16)

    def third(activated, grad_hidden, r):
        total[0, rows(r)] += nn(grad_hidden, x)
        total[1, rows(r)] += nn(activated, g)

    ahead, behind = first(0), None
    for r in range(count):
        now = ahead
        if r + 1 < count:
            ahead = first(r + 1)
        if behind is not None:
            third(*behind, r - 1)
        behind = second(*now)
    third(*behind, count - 1)


def share_copies(in_hbm, out_hbm, w_in, w_out, sems):
    part = pl.ds(lax.axis_index("rep") * w_in.shape[0], w_in.shape[0])
    return [
        pltpu.make_async_copy(in_hbm.at[part], w_in, sems.at[0]),
        pltpu.make_async_copy(out_hbm.at[part], w_out, sems.at[1]),
    ]


def plane_copies(held, sems, place, x_ref, first_ref, later_ref, start):
    devices, slots = held.shape[2:4]
    split = first_ref.shape[1]
    part = pl.ds(start, devices)
    return [
        pltpu.make_async_copy(source, target, sems.at[place, n])
        for n, (source, target) in enumerate(
            (
                (x_ref, held.at[place, 0]),
                (first_ref.at[part], held.at[place, 1, :, pl.ds(0, split)]),
                (later_ref.at[part], held.at[place, 1, :, pl.ds(split, slots - split)]),
            )
        )
    ]


def own_grad_kernel(
    x_ref, g_ref, in_hbm, out_hbm, send_ref, vec_ref, sums_ref, recv_ref, vec_recv,
    held, w_in, w_out, total, sems, w_sems, out_sems, send_sems, recv_sems, vec_sends, vec_recvs, *, sub,
):
    copies = share_copies(in_hbm, out_hbm, w_in, w_out, w_sems)
    for kind, ref in enumerate((x_ref, g_ref)):
        copies.append(pltpu.make_async_copy(ref, held.at[0, kind], sems.at[0, kind]))
    for copy in copies:
        copy.start()
    greet()
    start_exchange(send_ref, recv_ref, send_sems, recv_sems, 2)
    start_exchange(vec_ref, vec_recv, vec_sends, vec_recvs)
    total[...] = jnp.zeros_like(total)
    for copy in copies:
        copy.wait()
    grad_steps(held, 0, w_in, w_out, total, sub)
    copy = pltpu.make_async_copy(total, sums_ref, out_sems.at[0])
    copy.start()
    finish_exchange(send_ref, recv_ref, send_sems, recv_sems, 2)
    finish_exchange(vec_ref, vec_recv, vec_sends, vec_recvs)
    copy.wait()


def grad_scratch(sets, devices, slots, width, share):
    dma = pltpu.SemaphoreType.DMA
    return [
        pltpu.VMEM((sets, 2, devices, slots, width), bf16),
        pltpu.VMEM((share, width), bf16),
        pltpu.VMEM((share, width), bf16),
        pltpu.VMEM((2, share, width), f32),
        dma((max(sets, 2), 3)),
        dma((2,)),
        dma((2,)),
    ]


def own_grads(x, g, w_in, w_out, send, vectors, sub=256, after=()):
    groups, slots, width = g.shape
    share = w_in.shape[0] // lax.axis_size("rep")
    return launch(
        functools.partial(own_grad_kernel, sub=sub),
        (x, g, w_in, w_out, send, vectors),
        [ANY] * 6,
        15,
        after,
        collective_id=7,
        out_specs=[ANY] * 3,
        out_shape=[shape((2, share, width), f32), shape(send.shape, bf16), shape(vectors.shape, f32)],
        scratch_shapes=grad_scratch(1, groups, slots, width, share)
        + exchange_scratch(send.shape[0])
        + exchange_scratch(groups),
    )


HOLDERS = ((3, 0, 3, 0), (4, 3, 0, 1), (5, 4, 1, 2))


def rows_of(order, xs, firsts_ref, laters_ref, held, sems, place, action):
    z, copies = lax.axis_index("rep"), lax.axis_size("rep")
    low = z < 2
    plane = (z + 1 - 2 * lax.rem(z, 2), jnp.where(low, 2, 1), jnp.where(low, 3, 0))[order]
    shift = lax.rem(plane - z + copies, copies) - 1
    first_ref, later_ref = firsts_ref.at[shift], laters_ref.at[plane]
    if action == "wait":
        for copy in plane_copies(held, sems, place, xs[0], first_ref, later_ref, 0):
            copy.wait()
        return
    for at, index in enumerate(HOLDERS[order]):

        @pl.when(z == at)
        def _(index=index):
            for copy in plane_copies(held, sems, place, xs[index], first_ref, later_ref, 0):
                copy.start()


def two_grad_kernel(*refs, sub):
    xs = refs[:6]
    firsts_ref, laters_ref, in_hbm, out_hbm, before_ref, send_ref, sums_ref, recv_ref = refs[6:14]
    held, w_in, w_out, total, sems, w_sems, out_sems, send_sems, recv_sems = refs[14:]
    step = pl.program_id(0)
    weights = share_copies(in_hbm, out_hbm, w_in, w_out, w_sems)
    load = pltpu.make_async_copy(before_ref, total, out_sems.at[0])

    @pl.when(step == 0)
    def _():
        for copy in weights:
            copy.start()
        rows_of(0, xs, firsts_ref, laters_ref, held, sems, 0, "start")
        load.start()
        rows_of(1, xs, firsts_ref, laters_ref, held, sems, 1, "start")
        greet()
        start_exchange(send_ref, recv_ref, send_sems, recv_sems, 2)
        for copy in weights + [load]:
            copy.wait()

    rows_of(0, xs, firsts_ref, laters_ref, held, sems, step, "wait")
    grad_steps(held, step, w_in, w_out, total, sub)

    @pl.when(step == 1)
    def _():
        copy = pltpu.make_async_copy(total, sums_ref, out_sems.at[0])
        copy.start()
        finish_exchange(send_ref, recv_ref, send_sems, recv_sems, 2)
        copy.wait()


def two_grads(xs, firsts, laters, w_in, w_out, before, send, sub=256, after=()):
    groups, capacity, width = xs[0].shape
    share = w_in.shape[0] // lax.axis_size("rep")
    return launch(
        functools.partial(two_grad_kernel, sub=sub),
        (*xs, firsts, laters, w_in, w_out, before, send),
        [ANY] * 12,
        27,
        after,
        grid=(2,),
        collective_id=4,
        out_specs=[ANY] * 2,
        out_shape=[shape((2, share, width), f32), shape(send.shape, bf16)],
        scratch_shapes=grad_scratch(2, groups, capacity, width, share)
        + exchange_scratch(send.shape[0]),
    )


def last_grad_kernel(shard_ref, *refs, parts):
    xs = refs[:6]
    firsts_ref, laters_ref, in_ref, out_ref, before_ref, gin_ref, gout_ref, held, sems = refs[6:]

    @pl.when(pl.program_id(0) == 0)
    def _():
        rows_of(2, xs, firsts_ref, laters_ref, held, sems, 0, "start")
        rows_of(2, xs, firsts_ref, laters_ref, held, sems, 0, "wait")

    devices, slots, width = held.shape[2:]
    count = devices // parts

    def rows(p, kind):
        return held[0, kind, p * count : (p + 1) * count].reshape(count * slots, width)

    def first(p):
        return nt(in_ref[...], rows(p, 0)), nt(out_ref[...], rows(p, 1))

    grad_in, grad_out = before_ref[0], before_ref[1]
    ahead = first(0)
    for p in range(parts):
        hidden, grad_activated = ahead
        if p + 1 < parts:
            ahead = first(p + 1)
        activated, slope = gelu_parts(hidden)
        grad_out += nn(activated.astype(bf16), rows(p, 1))
        grad_in += nn((grad_activated * slope).astype(bf16), rows(p, 0))
    gin_ref[...] = grad_in
    gout_ref[...] = grad_out


def last_grads(xs, firsts, laters, shard, w_in, w_out, before, block=256, parts=2, after=()):
    groups, capacity, width = xs[0].shape
    share = w_in.shape[0] // lax.axis_size("rep")
    steps = share // block
    weights = pl.BlockSpec((block, width), lambda i, shard: (shard[0] * steps + i, 0))
    both = pl.BlockSpec((2, block, width), lambda i, shard: (0, i, 0))
    blocked = pl.BlockSpec((block, width), lambda i, shard: (i, 0))

    def kernel(*refs):
        last_grad_kernel(*refs[:12], *refs[12 + len(after) :], parts=parts)

    return pl.pallas_call(
        kernel,
        grid_spec=pltpu.PrefetchScalarGridSpec(
            num_scalar_prefetch=1,
            grid=(steps,),
            in_specs=[ANY] * 8 + [weights] * 2 + [both] + [ANY] * len(after),
            out_specs=[blocked] * 2,
            scratch_shapes=[
                pltpu.VMEM((1, 2, groups, capacity, width), bf16),
                pltpu.SemaphoreType.DMA((1, 3)),
            ],
        ),
        out_shape=[shape((share, width), f32)] * 2,
        compiler_params=params(),
        cost_estimate=pl.CostEstimate(flops=int(1e9), bytes_accessed=int(1e6), transcendentals=0),
    )(shard, *xs, firsts, laters, w_in, w_out, before, *after)


def fence_kernel(*refs):
    pass


def fence(arrays, after):
    count = len(arrays)
    return launch(
        fence_kernel,
        tuple(arrays),
        [ANY] * count,
        1,
        after,
        out_specs=[ANY] * count,
        out_shape=[shape(a.shape, a.dtype) for a in arrays],
        input_output_aliases={n: n for n in range(count)},
    )


def back_kernel(
    back_ref, place_ref, mid_ref, cot_ref, len_ref, gain_ref, w_ref,
    gmid_ref, branch_ref, gmix_ref, ggain_ref, gshift_ref,
):
    step = pl.program_id(0)
    block = mid_ref.shape[0]
    grad_sent = nn(row_pick(place_ref[...], back_ref.shape[0]), back_ref[...])
    normal, inverse = normalize(mid_ref[...])
    position = step * block + lax.broadcasted_iota(jnp.int32, (block, 1), 0)
    grad_final = jnp.where(position < len_ref[0], cot_ref[...].astype(f32), 0.0)
    grad_middle = grad_final + norm_backward(grad_sent, normal, inverse, gain_ref[...])
    gmid_ref[...] = grad_middle
    branch = grad_middle.astype(bf16)
    branch_ref[...] = branch
    gmix_ref[...] = nt(branch, w_ref[...]).astype(bf16)

    @pl.when(step == 0)
    def _():
        ggain_ref[...] = jnp.zeros_like(ggain_ref)
        gshift_ref[...] = jnp.zeros_like(gshift_ref)

    ggain_ref[...] += jnp.sum(grad_sent * normal, axis=0, keepdims=True)
    gshift_ref[...] += jnp.sum(grad_sent, axis=0, keepdims=True)


def middle_back(back, place, middle, cotangent, lengths, gain, w_output, block=256, after=()):
    rows, width = middle.shape
    blocked = row_spec(block, width)
    vector = pl.BlockSpec((1, width), lambda i: (0, 0))
    return launch(
        back_kernel,
        (back, place, middle, cotangent, lengths, gain, w_output,),
        [
            whole(back),
            pl.BlockSpec((8, block), lambda i: (0, i)),
            blocked,
            blocked,
            pl.BlockSpec(memory_space=pltpu.SMEM),
            whole(gain),
            whole(w_output),
        ],
        12,
        after,
        grid=(rows // block,),
        out_specs=[blocked, blocked, blocked, vector, vector],
        out_shape=[shape((rows, width), f32)]
        + [shape((rows, width), bf16)] * 2
        + [shape((1, width), f32)] * 2,
    )


def weight_grad_kernel(m_ref, branch_ref, n_ref, gq_ref, gk_ref, gv_ref, o_ref):
    groups, _, _, share, width = o_ref.shape

    def put(n, left, right_ref):
        o_ref[:, 0, n] = nn(left, right_ref[...]).reshape(groups, share, width).astype(bf16)

    put(0, m_ref[...].T, branch_ref)
    left = n_ref[...].T
    for n, ref in enumerate((gq_ref, gk_ref, gv_ref)):
        put(n + 1, left, ref)


def weight_grads(mixed, branch, normed, gq, gk, gv, groups, copies, after=()):
    rows, width = mixed.shape
    block = width // copies
    dims = (groups, copies, 4, block // groups, width)
    column = pl.BlockSpec((rows, block), lambda i: (0, i))
    return launch(
        weight_grad_kernel,
        (mixed, branch, normed, gq, gk, gv),
        [column, whole(branch), column] + [whole(a) for a in (gq, gk, gv)],
        16,
        after,
        grid=(copies,),
        out_specs=pl.BlockSpec((groups, 1) + dims[2:], lambda i: (0, i, 0, 0, 0)),
        out_shape=shape(dims, bf16),
    )


def input_back_kernel(
    gq_ref, gk_ref, gv_ref, wq_ref, wk_ref, wv_ref, x_ref, gmid_ref, gain_ref,
    gin_ref, ggain_ref, gshift_ref,
):
    grad_normed = (
        nt(gq_ref[...], wq_ref[...]) + nt(gk_ref[...], wk_ref[...]) + nt(gv_ref[...], wv_ref[...])
    )
    normal, inverse = normalize(x_ref[...].astype(f32))
    gin_ref[...] = gmid_ref[...] + norm_backward(grad_normed, normal, inverse, gain_ref[...])

    @pl.when(pl.program_id(0) == 0)
    def _():
        ggain_ref[...] = jnp.zeros_like(ggain_ref)
        gshift_ref[...] = jnp.zeros_like(gshift_ref)

    ggain_ref[...] += jnp.sum(grad_normed * normal, axis=0, keepdims=True)
    gshift_ref[...] += jnp.sum(grad_normed, axis=0, keepdims=True)


def input_back(gq, gk, gv, wq, wk, wv, x, grad_middle, gain, block=256, after=()):
    rows, width = x.shape
    blocked = row_spec(block, width)
    vector = pl.BlockSpec((1, width), lambda i: (0, 0))
    return launch(
        input_back_kernel,
        (gq, gk, gv, wq, wk, wv, x, grad_middle, gain,),
        [blocked] * 3 + [whole(w) for w in (wq, wk, wv)] + [blocked, blocked, whole(gain)],
        14,
        after,
        grid=(rows // block,),
        out_specs=[blocked, vector, vector],
        out_shape=[shape((rows, width), f32)] + [shape((1, width), f32)] * 2,
    )


def chip_add_kernel(dense_ref, oa_ref, ob_ref, kept, got, sems, keep_sems):
    me = lax.axis_index("exp")
    core = lax.rem(me, 2)
    half = kept.shape[0]
    cut = kept.shape[2] // 2
    sibling = at_exp(me + 1 - 2 * core)
    copies = []
    for n in range(half):
        keep = pltpu.make_async_copy(dense_ref.at[2 * n + core], kept.at[n], keep_sems.at[0, n])
        give = push(dense_ref.at[2 * n + 1 - core], got.at[n], sems.at[0, n], sems.at[1, n], sibling)
        writes = [
            pltpu.make_async_copy(
                kept.at[n, :, pl.ds(m * cut, cut)], ref.at[n], keep_sems.at[m + 1, n]
            )
            for m, ref in enumerate((oa_ref, ob_ref))
        ]
        copies.append((keep, give, writes))
        keep.start()
    greet()
    for _, give, _ in copies:
        give.start()
    for n, (keep, give, writes) in enumerate(copies):
        keep.wait()
        give.wait_recv()
        kept[n] = (kept[n].astype(f32) + got[n].astype(f32)).astype(bf16)
        for write in writes:
            write.start()
    for _, give, writes in copies:
        give.wait_send()
        for write in writes:
            write.wait()


def chip_add(dense, after=()):
    half = dense.shape[0] // 2
    dims = (half,) + dense.shape[1:]
    cut = dims[:2] + (dims[2] // 2,) + dims[3:]
    dma = pltpu.SemaphoreType.DMA
    return launch(
        chip_add_kernel,
        (dense,),
        [ANY],
        8,
        after,
        collective_id=6,
        out_specs=[ANY] * 2,
        out_shape=[shape(cut, bf16)] * 2,
        scratch_shapes=[pltpu.VMEM(dims, bf16)] * 2 + [dma((2, half)), dma((3, half))],
    )


def near_add_kernel(a_ref, b_ref, vec_ref, o_ref):
    cut = a_ref.shape[2]
    o_ref[0, :cut] = jnp.sum(a_ref[:, 0].astype(f32), axis=0).astype(bf16)
    o_ref[0, cut : 2 * cut] = jnp.sum(b_ref[:, 0].astype(f32), axis=0).astype(bf16)
    vectors = jnp.sum(vec_ref[:, 0], axis=0)
    high = vectors.astype(bf16)
    low = (vectors - high.astype(f32)).astype(bf16)
    lanes = vectors.shape[1]
    o_ref[0, 2 * cut] = jnp.zeros(o_ref.shape[2:], bf16)
    o_ref[0, 2 * cut, :, :lanes] = high
    o_ref[0, 2 * cut, :, lanes : 2 * lanes] = low


def near_add(a, b, vectors, after=()):
    groups, copies, cut = a.shape[:3]
    dims = (2 * cut + 1,) + a.shape[3:]
    spec = pl.BlockSpec((groups, 1) + a.shape[2:], lambda i: (0, i, 0, 0, 0))
    return launch(
        near_add_kernel,
        (a, b, vectors),
        [
            spec,
            spec,
            pl.BlockSpec((vectors.shape[0], 1) + vectors.shape[2:], lambda i: (0, i, 0, 0)),
        ],
        6,
        after,
        grid=(copies,),
        out_specs=pl.BlockSpec((1,) + dims, lambda i: (i, 0, 0, 0)),
        out_shape=shape((copies,) + dims, bf16),
    )


def far_add_kernel(parts_ref, *out_refs):
    for n, ref in enumerate(out_refs):
        ref[...] = jnp.sum(parts_ref[:, n].astype(f32), axis=0)


def far_add(parts, after=()):
    _, count, share, width = parts.shape
    return launch(
        far_add_kernel,
        (parts,),
        [whole(parts)],
        1,
        after,
        out_specs=[pl.BlockSpec((share, width), lambda: (0, 0))] * count,
        out_shape=[shape((share, width), f32)] * count,
    )


def output_kernel(back_ref, place_ref, mid_ref, o_ref):
    combined = nn(row_pick(place_ref[...], back_ref.shape[0]), back_ref[...])
    o_ref[...] = (mid_ref[...] + combined).astype(bf16)


def combine(back, place, middle, block=256, after=()):
    rows, width = middle.shape
    return launch(
        output_kernel,
        (back, place, middle),
        [
            whole(back),
            pl.BlockSpec((8, block), lambda i: (0, i)),
            row_spec(block, width),
        ],
        7,
        after,
        grid=(rows // block,),
        out_specs=row_spec(block, width),
        out_shape=shape((rows, width), bf16),
    )


def body(
    inputs,
    cotangent,
    token_ids,
    lengths,
    hash_table,
    first_gain,
    first_shift,
    w_query,
    w_key,
    w_value,
    w_output,
    second_gain,
    second_shift,
    expert_in,
    expert_out,
):
    seq_count, seq_len, width = inputs.shape
    rows = seq_count * seq_len
    groups = lax.axis_size("exp")
    copies = lax.axis_size("rep")
    place_z = lax.axis_index("rep")
    capacity = rows // groups
    slot_total = groups * capacity
    x = inputs.reshape(rows, width)
    cot = cotangent.reshape(rows, width)
    gain_one, shift_one, gain_two, shift_two = (
        v.reshape(1, width) for v in (first_gain, first_shift, second_gain, second_shift)
    )
    table_rows = -(-hash_table.shape[0] // (8 * 128)) * 8
    table = jnp.pad(hash_table, (0, table_rows * 128 - hash_table.shape[0]))
    table = table.reshape(table_rows, 128)

    place_e = lax.axis_index("exp")

    def exchange(parts, axis="exp"):
        return lax.all_to_all(parts, axis, split_axis=0, concat_axis=0, tiled=True)

    def gather(array):
        return lax.all_gather(array, "rep", axis=0, tiled=False)

    flat = (slot_total, width)
    by_group = (groups, capacity, width)
    w_in, w_out = expert_in[0], expert_out[0]
    first = max(16, capacity // 4)
    place, send_first = route(
        lengths, token_ids.reshape(1, rows), table, cot, groups, capacity, first
    )
    firsts = gather(send_first)
    grad_send = dispatch(place, cot, groups, capacity, after=(send_first,))
    grads = exchange(grad_send)
    normed, q, k, v = project(x, gain_one, shift_one, w_query, w_key, w_value, after=(grad_send,))
    mixed, logs = attend(lengths, q, k, v)
    (grads,) = fence((grads,), (mixed,))
    laters = gather(grads[:, first:])
    middle, send_rows = middle_and_send(
        x, mixed, w_output, gain_two, shift_two, place, slot_total, after=(grads,)
    )
    grad_back, result, sent = expert_main(send_rows.reshape(by_group), grads, w_in, w_out)

    def hops(up, down, start):
        ups = [(z, z + 1) for z in range(start, copies - 1)]
        downs = [(z, z - 1) for z in range(1, copies - start)]
        return lax.ppermute(up, "rep", ups), lax.ppermute(down, "rep", downs)

    sent_u1, sent_d1 = hops(sent, sent, 0)
    returned = exchange(result)
    grad_middle, branch, grad_mixed, grad_second_gain, grad_second_shift = middle_back(
        grad_back.reshape(flat), place, middle, cot, lengths, gain_two, w_output
    )
    gq, gk, gv, firsts = attend_back(lengths, q, k, v, mixed, grad_mixed, logs, firsts)
    parts = weight_grads(mixed, branch, normed, gq, gk, gv, groups, copies)
    chip_a, chip_b = chip_add(parts, after=(returned,))
    sent_u1, sent_d1 = fence((sent_u1, sent_d1), (chip_a,))
    sent_u2, sent_d2 = hops(sent_u1, sent_d1, 1)
    grad_inputs, grad_first_gain, grad_first_shift = input_back(
        gq, gk, gv, w_query, w_key, w_value, x, grad_middle, gain_one, after=(sent_u1,)
    )
    vectors = jnp.concatenate(
        [grad_first_gain, grad_first_shift, grad_second_gain, grad_second_shift], axis=0
    )
    part = width // (groups * copies)
    vectors = vectors.reshape(4, copies, groups, part).transpose(2, 1, 0, 3)
    vectors = jnp.pad(vectors, ((0, 0), (0, 0), (0, part - 4), (0, 128 - part)))
    sums, near_a, vectors = own_grads(
        sent, grads, w_in, w_out, chip_a, vectors
    )
    sent_u2, sent_d2 = fence((sent_u2, sent_d2), (sums,))
    sent_u3, sent_d3 = hops(sent_u2, sent_d2, 2)
    xs = (sent_u1, sent_u2, sent_u3, sent_d1, sent_d2, sent_d3)
    early = (sent_u1, sent_u2, sent_u2, sent_d1, sent_d2, sent_d2)
    sums, near_b = two_grads(early, firsts, laters, w_in, w_out, sums, chip_b)
    near_all = near_add(near_a, near_b, vectors)
    far = exchange(near_all, "rep")
    outputs = combine(returned.reshape(flat), place, middle, after=(near_all,))
    grad_expert_in, grad_expert_out = last_grads(
        xs, firsts, laters, place_z.astype(jnp.int32).reshape(1), w_in, w_out, sums, after=(outputs,)
    )
    dense_output, dense_query, dense_key, dense_value, vectors = far_add(
        far, after=(grad_expert_in,)
    )
    vectors = (vectors[:4, :128] + vectors[:4, 128:256])[:, :part]
    return (
        outputs.reshape(seq_count, seq_len, width),
        grad_inputs.reshape(seq_count, seq_len, width),
        vectors[0],
        vectors[1],
        dense_query,
        dense_key,
        dense_value,
        dense_output,
        vectors[2],
        vectors[3],
        grad_expert_in[None],
        grad_expert_out[None],
    )


def solution(mesh):
    both = ("rep", "exp")
    placed = (
        P(both, None, None),
        P(both, None, None),
        P(both, None),
        P(both),
    ) + (P(),) * 9 + (P("exp", None, None),) * 2
    return jax.shard_map(
        body,
        mesh=mesh,
        in_specs=placed,
        out_specs=(
            P(both, None, None),
            P(both, None, None),
            P(both),
            P(both),
            P(both, None),
            P(both, None),
            P(both, None),
            P(both, None),
            P(both),
            P(both),
            P("exp", "rep", None),
            P("exp", "rep", None),
        ),
        check_vma=False,
    )
```

```python
import functools
import math

import jax
import jax.numpy as jnp
from jax import lax
from jax.experimental import pallas as pl
from jax.experimental.pallas import tpu as pltpu
from jax.sharding import PartitionSpec as P

HEAD_DIM = 64
PAIR = 2 * HEAD_DIM
MASKED = -1e30
epsilon = 1e-05
bf16, f32 = jnp.bfloat16, jnp.float32
MESH = pl.DeviceIdType.MESH
ANY = pl.BlockSpec(memory_space=pl.ANY)
VMEM_BYTES = 56 * 1024 * 1024
PARTS = 4


def params(collective_id=None):
    if collective_id is None:
        return pltpu.CompilerParams(vmem_limit_bytes=VMEM_BYTES)
    return pltpu.CompilerParams(
        vmem_limit_bytes=VMEM_BYTES, collective_id=collective_id, has_side_effects=True
    )


def launch(kernel, operands, in_specs, micros, after=(), collective_id=None, **options):
    count = len(operands)

    def run(*refs):
        kernel(*refs[:count], *refs[count + len(after) :])

    return pl.pallas_call(
        run,
        in_specs=list(in_specs) + [pl.BlockSpec(memory_space=pl.ANY)] * len(after),
        compiler_params=params(collective_id),
        cost_estimate=pl.CostEstimate(
            flops=int(1e9), bytes_accessed=int(1e6), transcendentals=0
        ),
        **options,
    )(*operands, *after)


def at_rep(place):
    return {"rep": place}


def at_exp(place):
    return {"exp": place}


def greet(*axes):
    barrier = pltpu.get_barrier_semaphore()
    count = 0
    for axis in axes or ("exp",):
        size, me = lax.axis_size(axis), lax.axis_index(axis)

        def tell(step, carry, axis=axis, size=size, me=me):
            peer = lax.rem(me + step, size)
            pl.semaphore_signal(barrier, inc=1, device_id={axis: peer}, device_id_type=MESH)
            return carry

        lax.fori_loop(1, size, tell, 0)
        count += size - 1
    pl.semaphore_wait(barrier, count)


def push(source, target, send_sem, recv_sem, device):
    return pltpu.make_async_remote_copy(
        src_ref=source,
        dst_ref=target,
        send_sem=send_sem,
        recv_sem=recv_sem,
        device_id=device,
        device_id_type=MESH,
    )


def remote(source, target, send_sem, recv_sem, peer):
    return push(source, target, send_sem, recv_sem, at_exp(peer))


def start_exchange(send_ref, recv_ref, send_sems, recv_sems, stride=1, axis="exp"):
    groups = send_ref.shape[0]
    me = lax.axis_index(axis)
    mine = me // stride
    pltpu.make_async_copy(send_ref.at[mine], recv_ref.at[mine], recv_sems.at[mine]).start()

    def send(step, carry):
        entry = lax.rem(mine + step, groups)
        peer = entry * stride + lax.rem(me, stride)
        push(
            send_ref.at[entry], recv_ref.at[mine], send_sems.at[entry], recv_sems.at[mine], {axis: peer}
        ).start()
        return carry

    lax.fori_loop(1, groups, send, 0)


def finish_exchange(send_ref, recv_ref, send_sems, recv_sems, stride=1, axis="exp"):
    groups = send_ref.shape[0]
    me = lax.axis_index(axis)
    mine = me // stride
    pltpu.make_async_copy(send_ref.at[mine], recv_ref.at[mine], recv_sems.at[mine]).wait()

    def wait(step, carry):
        entry = lax.rem(mine + step, groups)
        peer = entry * stride + lax.rem(me, stride)
        copy = push(
            send_ref.at[entry], recv_ref.at[entry], send_sems.at[entry], recv_sems.at[entry], {axis: peer}
        )
        copy.wait_send()
        copy.wait_recv()
        return carry

    lax.fori_loop(1, groups, wait, 0)


def remote(source, target, send_sem, recv_sem, peer):
    return push(source, target, send_sem, recv_sem, at_exp(peer))


def exchange_planes(send_ref, recv_ref, send_sems, recv_sems, begin):
    copies, groups = send_ref.shape[:2]
    z, me = lax.axis_index("rep"), lax.axis_index("exp")

    def shift(n, carry):
        plane = lax.rem(z + n + 1, copies)
        own = pltpu.make_async_copy(send_ref.at[plane, me], recv_ref.at[n, me], recv_sems.at[n, me])
        own.start() if begin else own.wait()

        def one(step, inner):
            peer = lax.rem(me + step, groups)
            entry = me if begin else peer
            copy = push(
                send_ref.at[plane, peer], recv_ref.at[n, entry],
                send_sems.at[n, peer], recv_sems.at[n, entry], at_exp(peer),
            )
            if begin:
                copy.start()
            else:
                copy.wait_send()
                copy.wait_recv()
            return inner

        return lax.fori_loop(1, groups, one, carry)

    lax.fori_loop(0, copies - 1, shift, 0)


def exchange_scratch(groups):
    return [pltpu.SemaphoreType.DMA((groups,))] * 2


def shape(dims, kind):
    return jax.ShapeDtypeStruct(dims, kind)


def nn(left, right):
    return lax.dot_general(left, right, (((1,), (0,)), ((), ())), preferred_element_type=f32)


def nt(left, right):
    return lax.dot_general(left, right, (((1,), (1,)), ((), ())), preferred_element_type=f32)


def tn(left, right):
    return lax.dot_general(left, right, (((0,), (0,)), ((), ())), preferred_element_type=f32)


def whole(array):
    return pl.BlockSpec(array.shape, lambda *_: (0,) * array.ndim)


def row_spec(rows, width):
    return pl.BlockSpec((rows, width), lambda i: (i, 0))


def normalize(values):
    average = jnp.mean(values, axis=1, keepdims=True)
    centered = values - average
    spread = jnp.mean(centered * centered, axis=1, keepdims=True)
    inverse = lax.rsqrt(spread + epsilon)
    return centered * inverse, inverse


def norm_backward(grad_out, normal, inverse, gain):
    grad_normal = grad_out * gain
    inner = (
        grad_normal
        - jnp.mean(grad_normal, axis=1, keepdims=True)
        - normal * jnp.mean(grad_normal * normal, axis=1, keepdims=True)
    )
    return inner * inverse


def gelu_parts(hidden):
    share = 0.5 * (1.0 + lax.erf(hidden * (1.0 / math.sqrt(2.0))))
    slope = share + hidden * jnp.exp(-0.5 * hidden * hidden) * (1.0 / math.sqrt(2.0 * math.pi))
    return hidden * share, slope


def route_kernel(
    len_ref, ids_ref, table_ref, cot_ref, place_ref, send_ref, *, groups, capacity
):
    seq_len = ids_ref.shape[1]
    slot_total = groups * capacity
    high_count, low_count = table_ref.shape
    ids = ids_ref[...]
    high, low = ids // low_count, ids % low_count
    high_pick = (
        lax.broadcasted_iota(jnp.int32, (high_count, seq_len), 0) == high
    ).astype(f32).astype(bf16)
    picked = tn(table_ref[...].astype(bf16), high_pick)
    low_pick = lax.broadcasted_iota(jnp.int32, (low_count, seq_len), 0) == low
    expert = jnp.sum(jnp.where(low_pick, picked, 0.0), axis=0, keepdims=True)
    valid = lax.broadcasted_iota(jnp.int32, (1, seq_len), 1) < len_ref[0]
    own = lax.broadcasted_iota(jnp.int32, (groups, seq_len), 0).astype(f32)
    chosen = jnp.where((own == expert) & valid, 1.0, 0.0)
    earlier = (
        lax.broadcasted_iota(jnp.int32, (seq_len, seq_len), 0)
        < lax.broadcasted_iota(jnp.int32, (seq_len, seq_len), 1)
    ).astype(f32).astype(bf16)
    before = nn(chosen.astype(bf16), earlier)
    slot = jnp.sum(before * chosen, axis=0, keepdims=True)
    place = jnp.where(valid & (slot < capacity), expert * capacity + slot, float(slot_total))
    place_ref[...] = jnp.broadcast_to(place, place_ref.shape)
    first = send_ref.shape[1]
    entry = lax.broadcasted_iota(jnp.int32, (groups * first, seq_len), 0)
    slots = (entry // first * capacity + entry % first).astype(f32)
    pick = jnp.where(slots == place, 1.0, 0.0).astype(bf16)
    send_ref[...] = nn(pick, cot_ref[...]).astype(bf16).reshape(send_ref.shape)


def dispatch_kernel(place_ref, cot_ref, send_ref):
    groups, capacity, _ = send_ref.shape
    sent = nn(slot_pick(place_ref[:1], groups * capacity), cot_ref[...])
    send_ref[...] = sent.astype(bf16).reshape(send_ref.shape)


def dispatch(place, cotangent, groups, capacity, after=()):
    dims = (groups, capacity, cotangent.shape[1])
    return launch(
        dispatch_kernel,
        (place, cotangent),
        [whole(place), whole(cotangent)],
        4,
        after,
        out_specs=pl.BlockSpec(dims, lambda: (0, 0, 0)),
        out_shape=shape(dims, bf16),
    )


def slot_pick(place_row, slot_total):
    slots = lax.broadcasted_iota(jnp.int32, (slot_total, place_row.shape[1]), 0).astype(f32)
    return jnp.where(slots == place_row, 1.0, 0.0).astype(bf16)


def row_pick(place_rows, slot_total):
    column = place_rows.T[:, :1]
    slots = lax.broadcasted_iota(jnp.int32, (column.shape[0], slot_total), 1).astype(f32)
    return jnp.where(slots == column, 1.0, 0.0).astype(bf16)


def route(lengths, ids, table, cotangent, groups, capacity, first, after=()):
    rows, width = cotangent.shape
    return launch(
        functools.partial(route_kernel, groups=groups, capacity=capacity),
        (lengths, ids, table, cotangent,),
        [
            pl.BlockSpec(memory_space=pltpu.SMEM),
            whole(ids),
            whole(table),
            whole(cotangent),
        ],
        10,
        after,
        out_specs=[
            pl.BlockSpec((8, rows), lambda: (0, 0)),
            pl.BlockSpec((groups, first, width), lambda: (0, 0, 0)),
        ],
        out_shape=[shape((8, rows), f32), shape((groups, first, width), bf16)],
    )


def project_kernel(x_ref, gain_ref, shift_ref, wq_ref, wk_ref, wv_ref, n_ref, q_ref, k_ref, v_ref):
    normal, _ = normalize(x_ref[...].astype(f32))
    normed = (normal * gain_ref[...] + shift_ref[...]).astype(bf16)
    n_ref[...] = normed
    q_ref[...] = nn(normed, wq_ref[...]).astype(bf16)
    k_ref[...] = nn(normed, wk_ref[...]).astype(bf16)
    v_ref[...] = nn(normed, wv_ref[...]).astype(bf16)


def project(x, gain, shift, wq, wk, wv, block=256, after=()):
    rows, width = x.shape
    return launch(
        project_kernel,
        (x, gain, shift, wq, wk, wv),
        [row_spec(block, width)] + [whole(a) for a in (gain, shift, wq, wk, wv)],
        13,
        after,
        grid=(rows // block,),
        out_specs=[row_spec(block, width)] * 4,
        out_shape=[shape((rows, width), bf16)] * 4,
    )


def head_parts(length, block, seq_len):
    lane = lax.broadcasted_iota(jnp.int32, (1, PAIR), 1)
    position = lax.broadcasted_iota(jnp.int32, (seq_len, 1), 0)
    bias = jnp.where(position < length, 0.0, MASKED).astype(bf16)
    down = lax.broadcasted_iota(jnp.int32, (block, block), 0)
    across = lax.broadcasted_iota(jnp.int32, (block, block), 1)
    return lane // HEAD_DIM, lane % HEAD_DIM == 0, bias, down <= across


def attend_kernel(
    len_ref, q_ref, k_ref, v_ref, o_ref, log_ref, *, block, pairs
):
    seq_len = q_ref.shape[0]
    factor = HEAD_DIM**-0.5 * math.log2(math.e)
    half, first_lane, bias, causal = head_parts(len_ref[0], block, seq_len)
    zero = jnp.zeros_like(bias)
    keys, queries, values = [], [], []
    for pair in range(pairs):
        lanes = slice(pair * PAIR, (pair + 1) * PAIR)
        q, k = q_ref[:, lanes], k_ref[:, lanes]
        value_t = v_ref[:, lanes].T
        for h in range(2):
            spare = jnp.where(first_lane & (half != h), 1.0, 0.0).astype(bf16)
            keys.append(jnp.where(half == h, k, bias * spare))
            queries.append(jnp.where(half == h, q, spare))
            values.append(
                jnp.concatenate(
                    [value_t[h * HEAD_DIM : (h + 1) * HEAD_DIM], jnp.ones((16, seq_len), bf16)],
                    axis=0,
                )
            )
    order = [(h, j) for j in range(seq_len // block) for h in range(2 * pairs)]

    def score(h, j):
        end = (j + 1) * block
        return nt(keys[h][:end], queries[h][j * block : end])

    def soften(scores, j):
        last = jnp.where(causal, scores[j * block :], MASKED)
        scores = last if j == 0 else jnp.concatenate([scores[: j * block], last], axis=0)
        highest = jnp.max(scores, axis=0, keepdims=True) * factor
        return jnp.exp2(scores * factor - highest).astype(bf16), highest

    def finish(powers, highest, h, j):
        rows = slice(j * block, (j + 1) * block)
        total = nn(values[h][:, : (j + 1) * block], powers)
        summed = total[HEAD_DIM : HEAD_DIM + 1]
        mixed = total[:HEAD_DIM] * (1.0 / summed)
        o_ref[rows, h * HEAD_DIM : (h + 1) * HEAD_DIM] = mixed.T.astype(bf16)
        log_ref[h // 2, h % 2 : h % 2 + 1, rows] = highest + jnp.log2(summed)

    ahead = score(*order[0])
    behind = None
    for step, (h, j) in enumerate(order):
        scores = ahead
        if step + 1 < len(order):
            ahead = score(*order[step + 1])
        if behind is not None:
            finish(*behind, *order[step - 1])
        behind = soften(scores, j)
    finish(*behind, *order[-1])


def attend(lengths, q, k, v, block=256, pairs=2, after=()):
    rows, width = q.shape
    lanes = pl.BlockSpec((rows, pairs * PAIR), lambda i: (0, i))
    return launch(
        functools.partial(attend_kernel, block=block, pairs=pairs),
        (lengths, q, k, v),
        [pl.BlockSpec(memory_space=pltpu.SMEM)] + [lanes] * 3,
        18,
        after,
        grid=(width // (pairs * PAIR),),
        out_specs=[lanes, pl.BlockSpec((pairs, 2, rows), lambda i: (i, 0, 0))],
        out_shape=[shape((rows, width), bf16), shape((width // PAIR, 2, rows), f32)],
    )


def attend_back_kernel(
    len_ref, q_ref, k_ref, v_ref, o_ref, g_ref, log_ref, send_ref,
    dq_ref, dk_ref, dv_ref, recv_ref, send_sems, recv_sems, *, block, pairs,
):
    @pl.when(pl.program_id(0) == 0)
    def _():
        greet()
        exchange_planes(send_ref, recv_ref, send_sems, recv_sems, True)

    seq_len = q_ref.shape[0]
    blocks = seq_len // block
    scale = HEAD_DIM**-0.5
    factor = scale * math.log2(math.e)
    half, first_lane, bias, causal = head_parts(len_ref[0], block, seq_len)
    zero = jnp.zeros_like(bias)
    keys, queries, values, keys_t, logs, deltas = [], [], [], [], [], []
    for pair in range(pairs):
        lanes = slice(pair * PAIR, (pair + 1) * PAIR)
        q, k, v = q_ref[:, lanes], k_ref[:, lanes], v_ref[:, lanes]
        key_t = k.T
        product = (g_ref[:, lanes].astype(f32) * o_ref[:, lanes].astype(f32)).T
        for h in range(2):
            rows = slice(h * HEAD_DIM, (h + 1) * HEAD_DIM)
            spare = jnp.where(first_lane & (half != h), 1.0, 0.0).astype(bf16)
            keys.append(jnp.where(half == h, k, bias * spare))
            queries.append(jnp.where(half == h, q, spare))
            values.append(jnp.where(half == h, v, zero))
            keys_t.append(key_t[rows])
            logs.append(log_ref[pair, h : h + 1, :])
            deltas.append(jnp.sum(product[rows], axis=0, keepdims=True))
    order = [(h, i) for i in range(blocks) for h in range(2 * pairs)]
    query_sums = [[None] * blocks for _ in range(2 * pairs)]
    kept = {}

    def lanes_of(h):
        return slice((h // 2) * PAIR, (h // 2 + 1) * PAIR)

    def products(h, i):
        rows = slice(i * block, (i + 1) * block)
        return (
            nt(keys[h][rows], queries[h][i * block :]),
            nt(values[h][rows], g_ref[i * block :, lanes_of(h)]),
        )

    def shares_of(scores, grad_shares, h, i):
        shares = jnp.exp2(scores * factor - logs[h][:, i * block :])
        first = jnp.where(causal, shares[:, :block], 0.0)
        if i + 1 < blocks:
            first = jnp.concatenate([first, shares[:, block:]], axis=1)
        grad_scores = first * (grad_shares - deltas[h][:, i * block :])
        return first.astype(bf16), grad_scores.astype(bf16)

    def finish(shares, grad_scores, h, i):
        rows, lanes = slice(i * block, (i + 1) * block), lanes_of(h)
        grad_v = nn(shares, g_ref[i * block :, lanes])
        grad_k = nn(grad_scores, q_ref[i * block :, lanes])
        part = nn(keys_t[h][:, rows], grad_scores)
        for j in range(i, blocks):
            term = part[:, (j - i) * block : (j - i + 1) * block]
            held = query_sums[h][j]
            query_sums[h][j] = term if held is None else held + term
        dq_ref[rows, h * HEAD_DIM : (h + 1) * HEAD_DIM] = (
            (query_sums[h][i] * scale).T.astype(bf16)
        )
        kept[h] = (grad_k, grad_v)
        if h % 2:
            other_k, other_v = kept[h - 1]
            dk_ref[rows, lanes] = (jnp.where(half == 0, other_k, grad_k) * scale).astype(bf16)
            dv_ref[rows, lanes] = jnp.where(half == 0, other_v, grad_v).astype(bf16)

    ahead = products(*order[0])
    behind = None
    for step, (h, i) in enumerate(order):
        now = ahead
        if step + 1 < len(order):
            ahead = products(*order[step + 1])
        if behind is not None:
            finish(*behind, *order[step - 1])
        behind = shares_of(*now, h, i)
    finish(*behind, *order[-1])

    @pl.when(pl.program_id(0) == pl.num_programs(0) - 1)
    def _():
        exchange_planes(send_ref, recv_ref, send_sems, recv_sems, False)


def attend_back(lengths, q, k, v, mixed, grad_mixed, logs, send, block=256, pairs=2, after=()):
    rows, width = q.shape
    lanes = pl.BlockSpec((rows, pairs * PAIR), lambda i: (0, i))
    return launch(
        functools.partial(attend_back_kernel, block=block, pairs=pairs),
        (lengths, q, k, v, mixed, grad_mixed, logs, send),
        [pl.BlockSpec(memory_space=pltpu.SMEM)]
        + [lanes] * 5
        + [pl.BlockSpec((pairs, 2, rows), lambda i: (i, 0, 0)), ANY],
        31,
        after,
        collective_id=3,
        grid=(width // (pairs * PAIR),),
        out_specs=[lanes] * 3 + [ANY],
        out_shape=[shape((rows, width), bf16)] * 3
        + [shape((send.shape[0] - 1,) + send.shape[1:], bf16)],
        scratch_shapes=[pltpu.SemaphoreType.DMA((send.shape[0] - 1, send.shape[1]))] * 2,
    )


def middle_kernel(x_ref, m_ref, w_ref, gain_ref, shift_ref, place_ref, mid_ref, send_ref, sent):
    step = pl.program_id(0)
    block = x_ref.shape[0]
    middle = x_ref[...].astype(f32) + nn(m_ref[...], w_ref[...])
    mid_ref[...] = middle
    normal, _ = normalize(middle)
    sent[pl.ds(step * block, block)] = (normal * gain_ref[...] + shift_ref[...]).astype(bf16)

    @pl.when(step == pl.num_programs(0) - 1)
    def _():
        pick = slot_pick(place_ref[:1], send_ref.shape[0])
        send_ref[...] = nn(pick, sent[...]).astype(bf16)


def middle_and_send(x, mixed, w_output, gain, shift, place, slot_total, block=256, after=()):
    rows, width = x.shape
    blocked = row_spec(block, width)
    return launch(
        middle_kernel,
        (x, mixed, w_output, gain, shift, place,),
        [blocked, blocked] + [whole(a) for a in (w_output, gain, shift, place)],
        10,
        after,
        grid=(rows // block,),
        out_specs=[blocked, pl.BlockSpec((slot_total, width), lambda i: (0, 0))],
        out_shape=[shape((rows, width), f32), shape((slot_total, width), bf16)],
        scratch_shapes=[pltpu.VMEM((rows, width), bf16)],
    )


def expert_kernel(
    send_ref, g_ref, in_hbm, out_hbm,
    back_ref, result_ref, arrived_ref,
    w_in, w_out, x_all, slots_all, result_all,
    w_sems, send_sems, recv_sems, back_sems, back_recv, keep_sems,
    *, rows, sub,
):
    groups, capacity, width = send_ref.shape
    me = lax.axis_index("exp")
    units = w_in.shape[0]
    sources = rows // capacity
    blocks = groups // sources
    mine = me // sources
    count = units // sub
    loads = []
    for f in range(count):
        part = slice(f * sub, (f + 1) * sub)
        pair = [
            pltpu.make_async_copy(hbm.at[part], vmem.at[part], w_sems.at[n, f])
            for n, (hbm, vmem) in enumerate(((in_hbm, w_in), (out_hbm, w_out)))
        ]
        for load in pair:
            load.start()
        loads.append(pair)
    greet()
    def send_block(j, carry):
        block = lax.rem(mine + blocks - j, blocks)

        def send(i, inner):
            peer = block * sources + i

            @pl.when(peer == me)
            def _():
                pltpu.make_async_copy(send_ref.at[me], x_all.at[me], recv_sems.at[me]).start()

            @pl.when(peer != me)
            def _():
                remote(
                    send_ref.at[peer], x_all.at[me], send_sems.at[peer], recv_sems.at[me], peer
                ).start()

            return inner

        return lax.fori_loop(0, sources, send, carry)

    lax.fori_loop(0, blocks, send_block, 0)

    def work(j, wait_weights):
        first_source = lax.rem(mine + j, blocks) * sources

        def arrive(i, carry):
            source = first_source + i
            remote(
                send_ref.at[source], x_all.at[source], send_sems.at[source], recv_sems.at[source],
                source,
            ).wait_recv()
            return carry

        lax.fori_loop(0, sources, arrive, 0)
        x = x_all[pl.ds(first_source, sources)].reshape(rows, width)
        g = g_ref[pl.ds(first_source, sources)].reshape(rows, width)

        def first(f):
            part = slice(f * sub, (f + 1) * sub)
            if wait_weights:
                for load in loads[f]:
                    load.wait()
            return nt(x, w_in[part]), nt(g, w_out[part])

        def second(hidden, grad_activated):
            activated, slope = gelu_parts(hidden)
            return activated.astype(bf16), (grad_activated * slope).astype(bf16)

        sums = None
        ahead, behind = first(0), None
        for f in range(count + 1):
            now = ahead
            if f + 1 < count:
                ahead = first(f + 1)
            if behind is not None:
                part = slice((f - 1) * sub, f * sub)
                terms = nn(behind[1], w_in[part]), nn(behind[0], w_out[part])
                sums = terms if sums is None else (sums[0] + terms[0], sums[1] + terms[1])
            if f < count:
                behind = second(*now)
        dims = (sources, capacity, width)
        slots_all[pl.ds(first_source, sources)] = sums[0].astype(bf16).reshape(dims)
        result_all[pl.ds(first_source, sources)] = sums[1].astype(bf16).reshape(dims)

        def answer(i, carry):
            peer = first_source + i

            @pl.when(peer == me)
            def _():
                pltpu.make_async_copy(slots_all.at[me], back_ref.at[me], back_recv.at[me]).start()

            @pl.when(peer != me)
            def _():
                remote(
                    slots_all.at[peer], back_ref.at[me], back_sems.at[peer], back_recv.at[me], peer
                ).start()

            return carry

        lax.fori_loop(0, sources, answer, 0)

    work(0, True)

    def later(j, carry):
        work(j, False)
        return carry

    lax.fori_loop(1, blocks, later, 0)
    keeps = [
        pltpu.make_async_copy(result_all, result_ref, keep_sems.at[0]),
        pltpu.make_async_copy(x_all, arrived_ref, keep_sems.at[1]),
    ]
    for keep in keeps:
        keep.start()
    def close(peer, carry):
        @pl.when(peer != me)
        def _():
            remote(
                send_ref.at[peer], x_all.at[peer], send_sems.at[peer], recv_sems.at[peer], peer
            ).wait_send()
            remote(
                slots_all.at[peer], back_ref.at[peer], back_sems.at[peer], back_recv.at[peer], peer
            ).wait_send()

        remote(
            slots_all.at[peer], back_ref.at[peer], back_sems.at[peer], back_recv.at[peer], peer
        ).wait_recv()
        return carry

    lax.fori_loop(0, groups, close, 0)

    for keep in keeps:
        keep.wait()


def expert_main(send, g, w_in, w_out, rows=256, sub=512, after=()):
    groups, capacity, width = send.shape
    units = w_in.shape[0]
    dma = pltpu.SemaphoreType.DMA
    return launch(
        functools.partial(expert_kernel, rows=rows, sub=sub),
        (send, g, w_in, w_out),
        [ANY, whole(g), ANY, ANY],
        60,
        after,
        collective_id=1,
        out_specs=[ANY] * 3,
        out_shape=[shape(send.shape, bf16)] * 3,
        scratch_shapes=[pltpu.VMEM((units, width), bf16)] * 2
        + [pltpu.VMEM(send.shape, bf16)] * 3
        + [dma((2, units // sub))]
        + [dma((groups,))] * 4
        + [dma((2,))],
    )


def grad_steps(held, place, w_in, w_out, total, sub):
    devices, slots, width = held.shape[2:]
    x = held[place, 0].reshape(devices * slots, width)
    g = held[place, 1].reshape(devices * slots, width)
    count = w_in.shape[0] // sub

    def rows(r):
        return slice(r * sub, (r + 1) * sub)

    def first(r):
        return nt(w_in[rows(r)], x), nt(w_out[rows(r)], g)

    def second(hidden, grad_activated):
        activated, slope = gelu_parts(hidden)
        return activated.astype(bf16), (grad_activated * slope).astype(bf16)

    def third(activated, grad_hidden, r):
        total[0, rows(r)] += nn(grad_hidden, x)
        total[1, rows(r)] += nn(activated, g)

    ahead, behind = first(0), None
    for r in range(count):
        now = ahead
        if r + 1 < count:
            ahead = first(r + 1)
        if behind is not None:
            third(*behind, r - 1)
        behind = second(*now)
    third(*behind, count - 1)


def share_copies(in_hbm, out_hbm, w_in, w_out, sems):
    part = pl.ds(lax.axis_index("rep") * w_in.shape[0], w_in.shape[0])
    return [
        pltpu.make_async_copy(in_hbm.at[part], w_in, sems.at[0]),
        pltpu.make_async_copy(out_hbm.at[part], w_out, sems.at[1]),
    ]


def plane_copies(held, sems, place, x_ref, first_ref, later_ref, start):
    devices, slots = held.shape[2:4]
    split = first_ref.shape[1]
    part = pl.ds(start, devices)
    return [
        pltpu.make_async_copy(source, target, sems.at[place, n])
        for n, (source, target) in enumerate(
            (
                (x_ref, held.at[place, 0]),
                (first_ref.at[part], held.at[place, 1, :, pl.ds(0, split)]),
                (later_ref.at[part], held.at[place, 1, :, pl.ds(split, slots - split)]),
            )
        )
    ]


def own_grad_kernel(*refs, sub):
    x_ref, g_ref, *xs = refs[:8]
    firsts_ref, laters_ref, in_hbm, out_hbm, send_ref, vec_ref, sums_ref, recv_ref, vec_recv = refs[8:17]
    held, w_in, w_out, total, sems, w_sems, out_sems, send_sems, recv_sems, vec_sends, vec_recvs = refs[17:]
    copies = share_copies(in_hbm, out_hbm, w_in, w_out, w_sems)
    for kind, ref in enumerate((x_ref, g_ref)):
        copies.append(pltpu.make_async_copy(ref, held.at[0, kind], sems.at[0, kind]))
    for copy in copies:
        copy.start()
    rows_of(0, xs, firsts_ref, laters_ref, held, sems, 1, "start")
    greet()
    start_exchange(send_ref, recv_ref, send_sems, recv_sems, 2)
    start_exchange(vec_ref, vec_recv, vec_sends, vec_recvs)
    total[...] = jnp.zeros_like(total)
    for copy in copies:
        copy.wait()
    grad_steps(held, 0, w_in, w_out, total, sub)
    rows_of(0, xs, firsts_ref, laters_ref, held, sems, 1, "wait")
    grad_steps(held, 1, w_in, w_out, total, sub)
    copy = pltpu.make_async_copy(total, sums_ref, out_sems.at[0])
    copy.start()
    finish_exchange(send_ref, recv_ref, send_sems, recv_sems, 2)
    finish_exchange(vec_ref, vec_recv, vec_sends, vec_recvs)
    copy.wait()


def grad_scratch(sets, devices, slots, width, share):
    dma = pltpu.SemaphoreType.DMA
    return [
        pltpu.VMEM((sets, 2, devices, slots, width), bf16),
        pltpu.VMEM((share, width), bf16),
        pltpu.VMEM((share, width), bf16),
        pltpu.VMEM((2, share, width), f32),
        dma((max(sets, 2), 3)),
        dma((2,)),
        dma((2,)),
    ]


def own_grads(x, g, xs, firsts, laters, w_in, w_out, send, vectors, sub=256, after=()):
    groups, slots, width = g.shape
    share = w_in.shape[0] // lax.axis_size("rep")
    return launch(
        functools.partial(own_grad_kernel, sub=sub),
        (x, g, *xs, firsts, laters, w_in, w_out, send, vectors),
        [ANY] * 14,
        15,
        after,
        collective_id=7,
        out_specs=[ANY] * 3,
        out_shape=[shape((2, share, width), f32), shape(send.shape, bf16), shape(vectors.shape, f32)],
        scratch_shapes=grad_scratch(2, groups, slots, width, share)
        + exchange_scratch(send.shape[0])
        + exchange_scratch(groups),
    )


HOLDERS = ((3, 0, 3, 0), (4, 3, 0, 1), (5, 4, 1, 2))


def rows_of(order, xs, firsts_ref, laters_ref, held, sems, place, action):
    z, copies = lax.axis_index("rep"), lax.axis_size("rep")
    low = z < 2
    plane = (z + 1 - 2 * lax.rem(z, 2), jnp.where(low, 2, 1), jnp.where(low, 3, 0))[order]
    shift = lax.rem(plane - z + copies, copies) - 1
    first_ref, later_ref = firsts_ref.at[shift], laters_ref.at[plane]
    if action == "wait":
        for copy in plane_copies(held, sems, place, xs[0], first_ref, later_ref, 0):
            copy.wait()
        return
    for at, index in enumerate(HOLDERS[order]):

        @pl.when(z == at)
        def _(index=index):
            for copy in plane_copies(held, sems, place, xs[index], first_ref, later_ref, 0):
                copy.start()


def second_grad_kernel(*refs, sub):
    xs = refs[:6]
    firsts_ref, laters_ref, in_hbm, out_hbm, before_ref, send_ref, sums_ref, recv_ref = refs[6:14]
    held, w_in, w_out, total, sems, w_sems, out_sems, send_sems, recv_sems = refs[14:]
    copies = share_copies(in_hbm, out_hbm, w_in, w_out, w_sems)
    copies.append(pltpu.make_async_copy(before_ref, total, out_sems.at[0]))
    for copy in copies:
        copy.start()
    rows_of(1, xs, firsts_ref, laters_ref, held, sems, 0, "start")
    greet()
    start_exchange(send_ref, recv_ref, send_sems, recv_sems, 2)
    for copy in copies:
        copy.wait()
    rows_of(1, xs, firsts_ref, laters_ref, held, sems, 0, "wait")
    grad_steps(held, 0, w_in, w_out, total, sub)
    copy = pltpu.make_async_copy(total, sums_ref, out_sems.at[0])
    copy.start()
    finish_exchange(send_ref, recv_ref, send_sems, recv_sems, 2)
    copy.wait()


def second_grads(xs, firsts, laters, w_in, w_out, before, send, sub=256, after=()):
    groups, capacity, width = xs[0].shape
    share = w_in.shape[0] // lax.axis_size("rep")
    return launch(
        functools.partial(second_grad_kernel, sub=sub),
        (*xs, firsts, laters, w_in, w_out, before, send),
        [ANY] * 12,
        27,
        after,
        collective_id=4,
        out_specs=[ANY] * 2,
        out_shape=[shape((2, share, width), f32), shape(send.shape, bf16)],
        scratch_shapes=grad_scratch(1, groups, capacity, width, share)
        + exchange_scratch(send.shape[0]),
    )


def last_grad_kernel(shard_ref, *refs, parts):
    xs = refs[:6]
    firsts_ref, laters_ref, in_ref, out_ref, before_ref, gin_ref, gout_ref, held, sems = refs[6:]

    @pl.when(pl.program_id(0) == 0)
    def _():
        rows_of(2, xs, firsts_ref, laters_ref, held, sems, 0, "start")
        rows_of(2, xs, firsts_ref, laters_ref, held, sems, 0, "wait")

    devices, slots, width = held.shape[2:]
    count = devices // parts

    def rows(p, kind):
        return held[0, kind, p * count : (p + 1) * count].reshape(count * slots, width)

    def first(p):
        return nt(in_ref[...], rows(p, 0)), nt(out_ref[...], rows(p, 1))

    grad_in, grad_out = before_ref[0], before_ref[1]
    ahead = first(0)
    for p in range(parts):
        hidden, grad_activated = ahead
        if p + 1 < parts:
            ahead = first(p + 1)
        activated, slope = gelu_parts(hidden)
        grad_out += nn(activated.astype(bf16), rows(p, 1))
        grad_in += nn((grad_activated * slope).astype(bf16), rows(p, 0))
    gin_ref[...] = grad_in
    gout_ref[...] = grad_out


def last_grads(xs, firsts, laters, shard, w_in, w_out, before, block=256, parts=2, after=()):
    groups, capacity, width = xs[0].shape
    share = w_in.shape[0] // lax.axis_size("rep")
    steps = share // block
    weights = pl.BlockSpec((block, width), lambda i, shard: (shard[0] * steps + i, 0))
    both = pl.BlockSpec((2, block, width), lambda i, shard: (0, i, 0))
    blocked = pl.BlockSpec((block, width), lambda i, shard: (i, 0))

    def kernel(*refs):
        last_grad_kernel(*refs[:12], *refs[12 + len(after) :], parts=parts)

    return pl.pallas_call(
        kernel,
        grid_spec=pltpu.PrefetchScalarGridSpec(
            num_scalar_prefetch=1,
            grid=(steps,),
            in_specs=[ANY] * 8 + [weights] * 2 + [both] + [ANY] * len(after),
            out_specs=[blocked] * 2,
            scratch_shapes=[
                pltpu.VMEM((1, 2, groups, capacity, width), bf16),
                pltpu.SemaphoreType.DMA((1, 3)),
            ],
        ),
        out_shape=[shape((share, width), f32)] * 2,
        compiler_params=params(),
        cost_estimate=pl.CostEstimate(flops=int(1e9), bytes_accessed=int(1e6), transcendentals=0),
    )(shard, *xs, firsts, laters, w_in, w_out, before, *after)


def fence_kernel(*refs):
    pass


def fence(arrays, after):
    count = len(arrays)
    return launch(
        fence_kernel,
        tuple(arrays),
        [ANY] * count,
        1,
        after,
        out_specs=[ANY] * count,
        out_shape=[shape(a.shape, a.dtype) for a in arrays],
        input_output_aliases={n: n for n in range(count)},
    )


def back_kernel(
    back_ref, place_ref, mid_ref, cot_ref, len_ref, gain_ref, w_ref,
    gmid_ref, branch_ref, gmix_ref, ggain_ref, gshift_ref,
):
    step = pl.program_id(0)
    block = mid_ref.shape[0]
    grad_sent = nn(row_pick(place_ref[...], back_ref.shape[0]), back_ref[...])
    normal, inverse = normalize(mid_ref[...])
    position = step * block + lax.broadcasted_iota(jnp.int32, (block, 1), 0)
    grad_final = jnp.where(position < len_ref[0], cot_ref[...].astype(f32), 0.0)
    grad_middle = grad_final + norm_backward(grad_sent, normal, inverse, gain_ref[...])
    gmid_ref[...] = grad_middle
    branch = grad_middle.astype(bf16)
    branch_ref[...] = branch
    gmix_ref[...] = nt(branch, w_ref[...]).astype(bf16)

    @pl.when(step == 0)
    def _():
        ggain_ref[...] = jnp.zeros_like(ggain_ref)
        gshift_ref[...] = jnp.zeros_like(gshift_ref)

    ggain_ref[...] += jnp.sum(grad_sent * normal, axis=0, keepdims=True)
    gshift_ref[...] += jnp.sum(grad_sent, axis=0, keepdims=True)


def middle_back(back, place, middle, cotangent, lengths, gain, w_output, block=256, after=()):
    rows, width = middle.shape
    blocked = row_spec(block, width)
    vector = pl.BlockSpec((1, width), lambda i: (0, 0))
    return launch(
        back_kernel,
        (back, place, middle, cotangent, lengths, gain, w_output,),
        [
            whole(back),
            pl.BlockSpec((8, block), lambda i: (0, i)),
            blocked,
            blocked,
            pl.BlockSpec(memory_space=pltpu.SMEM),
            whole(gain),
            whole(w_output),
        ],
        12,
        after,
        grid=(rows // block,),
        out_specs=[blocked, blocked, blocked, vector, vector],
        out_shape=[shape((rows, width), f32)]
        + [shape((rows, width), bf16)] * 2
        + [shape((1, width), f32)] * 2,
    )


def weight_grad_kernel(m_ref, branch_ref, n_ref, gq_ref, gk_ref, gv_ref, o_ref):
    groups, _, _, share, width = o_ref.shape

    def put(n, left, right_ref):
        o_ref[:, 0, n] = nn(left, right_ref[...]).reshape(groups, share, width).astype(bf16)

    put(0, m_ref[...].T, branch_ref)
    left = n_ref[...].T
    for n, ref in enumerate((gq_ref, gk_ref, gv_ref)):
        put(n + 1, left, ref)


def weight_grads(mixed, branch, normed, gq, gk, gv, groups, copies, after=()):
    rows, width = mixed.shape
    block = width // copies
    dims = (groups, copies, 4, block // groups, width)
    column = pl.BlockSpec((rows, block), lambda i: (0, i))
    return launch(
        weight_grad_kernel,
        (mixed, branch, normed, gq, gk, gv),
        [column, whole(branch), column] + [whole(a) for a in (gq, gk, gv)],
        16,
        after,
        grid=(copies,),
        out_specs=pl.BlockSpec((groups, 1) + dims[2:], lambda i: (0, i, 0, 0, 0)),
        out_shape=shape(dims, bf16),
    )


def input_back_kernel(
    gq_ref, gk_ref, gv_ref, wq_ref, wk_ref, wv_ref, x_ref, gmid_ref, gain_ref,
    gin_ref, ggain_ref, gshift_ref,
):
    grad_normed = (
        nt(gq_ref[...], wq_ref[...]) + nt(gk_ref[...], wk_ref[...]) + nt(gv_ref[...], wv_ref[...])
    )
    normal, inverse = normalize(x_ref[...].astype(f32))
    gin_ref[...] = gmid_ref[...] + norm_backward(grad_normed, normal, inverse, gain_ref[...])

    @pl.when(pl.program_id(0) == 0)
    def _():
        ggain_ref[...] = jnp.zeros_like(ggain_ref)
        gshift_ref[...] = jnp.zeros_like(gshift_ref)

    ggain_ref[...] += jnp.sum(grad_normed * normal, axis=0, keepdims=True)
    gshift_ref[...] += jnp.sum(grad_normed, axis=0, keepdims=True)


def input_back(gq, gk, gv, wq, wk, wv, x, grad_middle, gain, block=256, after=()):
    rows, width = x.shape
    blocked = row_spec(block, width)
    vector = pl.BlockSpec((1, width), lambda i: (0, 0))
    return launch(
        input_back_kernel,
        (gq, gk, gv, wq, wk, wv, x, grad_middle, gain,),
        [blocked] * 3 + [whole(w) for w in (wq, wk, wv)] + [blocked, blocked, whole(gain)],
        14,
        after,
        grid=(rows // block,),
        out_specs=[blocked, vector, vector],
        out_shape=[shape((rows, width), f32)] + [shape((1, width), f32)] * 2,
    )


def chip_add_kernel(dense_ref, oa_ref, ob_ref, kept, got, sems, keep_sems):
    me = lax.axis_index("exp")
    core = lax.rem(me, 2)
    half = kept.shape[0]
    cut = kept.shape[2] // 2
    sibling = at_exp(me + 1 - 2 * core)
    copies = []
    for n in range(half):
        keep = pltpu.make_async_copy(dense_ref.at[2 * n + core], kept.at[n], keep_sems.at[0, n])
        give = push(dense_ref.at[2 * n + 1 - core], got.at[n], sems.at[0, n], sems.at[1, n], sibling)
        writes = [
            pltpu.make_async_copy(
                kept.at[n, :, pl.ds(m * cut, cut)], ref.at[n], keep_sems.at[m + 1, n]
            )
            for m, ref in enumerate((oa_ref, ob_ref))
        ]
        copies.append((keep, give, writes))
        keep.start()
    greet()
    for _, give, _ in copies:
        give.start()
    for n, (keep, give, writes) in enumerate(copies):
        keep.wait()
        give.wait_recv()
        kept[n] = (kept[n].astype(f32) + got[n].astype(f32)).astype(bf16)
        for write in writes:
            write.start()
    for _, give, writes in copies:
        give.wait_send()
        for write in writes:
            write.wait()


def chip_add(dense, after=()):
    half = dense.shape[0] // 2
    dims = (half,) + dense.shape[1:]
    cut = dims[:2] + (dims[2] // 2,) + dims[3:]
    dma = pltpu.SemaphoreType.DMA
    return launch(
        chip_add_kernel,
        (dense,),
        [ANY],
        8,
        after,
        collective_id=6,
        out_specs=[ANY] * 2,
        out_shape=[shape(cut, bf16)] * 2,
        scratch_shapes=[pltpu.VMEM(dims, bf16)] * 2 + [dma((2, half)), dma((3, half))],
    )


def near_add_kernel(a_ref, b_ref, vec_ref, o_ref):
    cut = a_ref.shape[2]
    o_ref[0, :cut] = jnp.sum(a_ref[:, 0].astype(f32), axis=0).astype(bf16)
    o_ref[0, cut : 2 * cut] = jnp.sum(b_ref[:, 0].astype(f32), axis=0).astype(bf16)
    vectors = jnp.sum(vec_ref[:, 0], axis=0)
    high = vectors.astype(bf16)
    low = (vectors - high.astype(f32)).astype(bf16)
    lanes = vectors.shape[1]
    o_ref[0, 2 * cut] = jnp.zeros(o_ref.shape[2:], bf16)
    o_ref[0, 2 * cut, :, :lanes] = high
    o_ref[0, 2 * cut, :, lanes : 2 * lanes] = low


def near_add(a, b, vectors, after=()):
    groups, copies, cut = a.shape[:3]
    dims = (2 * cut + 1,) + a.shape[3:]
    spec = pl.BlockSpec((groups, 1) + a.shape[2:], lambda i: (0, i, 0, 0, 0))
    return launch(
        near_add_kernel,
        (a, b, vectors),
        [
            spec,
            spec,
            pl.BlockSpec((vectors.shape[0], 1) + vectors.shape[2:], lambda i: (0, i, 0, 0)),
        ],
        6,
        after,
        grid=(copies,),
        out_specs=pl.BlockSpec((1,) + dims, lambda i: (i, 0, 0, 0)),
        out_shape=shape((copies,) + dims, bf16),
    )


def far_add_kernel(parts_ref, *out_refs):
    for n, ref in enumerate(out_refs):
        ref[...] = jnp.sum(parts_ref[:, n].astype(f32), axis=0)


def far_add(parts, after=()):
    _, count, share, width = parts.shape
    return launch(
        far_add_kernel,
        (parts,),
        [whole(parts)],
        1,
        after,
        out_specs=[pl.BlockSpec((share, width), lambda: (0, 0))] * count,
        out_shape=[shape((share, width), f32)] * count,
    )


def output_kernel(back_ref, place_ref, mid_ref, o_ref):
    combined = nn(row_pick(place_ref[...], back_ref.shape[0]), back_ref[...])
    o_ref[...] = (mid_ref[...] + combined).astype(bf16)


def combine(back, place, middle, block=256, after=()):
    rows, width = middle.shape
    return launch(
        output_kernel,
        (back, place, middle),
        [
            whole(back),
            pl.BlockSpec((8, block), lambda i: (0, i)),
            row_spec(block, width),
        ],
        7,
        after,
        grid=(rows // block,),
        out_specs=row_spec(block, width),
        out_shape=shape((rows, width), bf16),
    )


def body(
    inputs,
    cotangent,
    token_ids,
    lengths,
    hash_table,
    first_gain,
    first_shift,
    w_query,
    w_key,
    w_value,
    w_output,
    second_gain,
    second_shift,
    expert_in,
    expert_out,
):
    seq_count, seq_len, width = inputs.shape
    rows = seq_count * seq_len
    groups = lax.axis_size("exp")
    copies = lax.axis_size("rep")
    place_z = lax.axis_index("rep")
    capacity = rows // groups
    slot_total = groups * capacity
    x = inputs.reshape(rows, width)
    cot = cotangent.reshape(rows, width)
    gain_one, shift_one, gain_two, shift_two = (
        v.reshape(1, width) for v in (first_gain, first_shift, second_gain, second_shift)
    )
    table_rows = -(-hash_table.shape[0] // (8 * 128)) * 8
    table = jnp.pad(hash_table, (0, table_rows * 128 - hash_table.shape[0]))
    table = table.reshape(table_rows, 128)

    place_e = lax.axis_index("exp")

    def exchange(parts, axis="exp"):
        return lax.all_to_all(parts, axis, split_axis=0, concat_axis=0, tiled=True)

    def gather(array):
        return lax.all_gather(array, "rep", axis=0, tiled=False)

    flat = (slot_total, width)
    by_group = (groups, capacity, width)
    w_in, w_out = expert_in[0], expert_out[0]
    first = max(16, capacity // 4)
    place, send_first = route(
        lengths, token_ids.reshape(1, rows), table, cot, groups, capacity, first
    )
    firsts = gather(send_first)
    grad_send = dispatch(place, cot, groups, capacity, after=(send_first,))
    grads = exchange(grad_send)
    normed, q, k, v = project(x, gain_one, shift_one, w_query, w_key, w_value, after=(grad_send,))
    mixed, logs = attend(lengths, q, k, v)
    (grads,) = fence((grads,), (mixed,))
    laters = gather(grads[:, first:])
    middle, send_rows = middle_and_send(
        x, mixed, w_output, gain_two, shift_two, place, slot_total, after=(grads,)
    )
    grad_back, result, sent = expert_main(send_rows.reshape(by_group), grads, w_in, w_out)

    def hops(up, down, start):
        ups = [(z, z + 1) for z in range(start, copies - 1)]
        downs = [(z, z - 1) for z in range(1, copies - start)]
        return lax.ppermute(up, "rep", ups), lax.ppermute(down, "rep", downs)

    sent_u1, sent_d1 = hops(sent, sent, 0)
    returned = exchange(result)
    grad_middle, branch, grad_mixed, grad_second_gain, grad_second_shift = middle_back(
        grad_back.reshape(flat), place, middle, cot, lengths, gain_two, w_output
    )
    gq, gk, gv, firsts = attend_back(lengths, q, k, v, mixed, grad_mixed, logs, firsts)
    parts = weight_grads(mixed, branch, normed, gq, gk, gv, groups, copies)
    chip_a, chip_b = chip_add(parts, after=(returned,))
    sent_u1, sent_d1 = fence((sent_u1, sent_d1), (chip_a,))
    sent_u2, sent_d2 = hops(sent_u1, sent_d1, 1)
    grad_inputs, grad_first_gain, grad_first_shift = input_back(
        gq, gk, gv, w_query, w_key, w_value, x, grad_middle, gain_one, after=(sent_u1,)
    )
    vectors = jnp.concatenate(
        [grad_first_gain, grad_first_shift, grad_second_gain, grad_second_shift], axis=0
    )
    part = width // (groups * copies)
    vectors = vectors.reshape(4, copies, groups, part).transpose(2, 1, 0, 3)
    vectors = jnp.pad(vectors, ((0, 0), (0, 0), (0, part - 4), (0, 128 - part)))
    sums, near_a, vectors = own_grads(
        sent, grads, (sent_u1,) * 3 + (sent_d1,) * 3, firsts, laters, w_in, w_out, chip_a, vectors
    )
    sent_u2, sent_d2 = fence((sent_u2, sent_d2), (sums,))
    sent_u3, sent_d3 = hops(sent_u2, sent_d2, 2)
    xs = (sent_u1, sent_u2, sent_u3, sent_d1, sent_d2, sent_d3)
    early = (sent_u1, sent_u2, sent_u2, sent_d1, sent_d2, sent_d2)
    sums, near_b = second_grads(early, firsts, laters, w_in, w_out, sums, chip_b)
    near_all = near_add(near_a, near_b, vectors)
    far = exchange(near_all, "rep")
    outputs = combine(returned.reshape(flat), place, middle, after=(near_all,))
    grad_expert_in, grad_expert_out = last_grads(
        xs, firsts, laters, place_z.astype(jnp.int32).reshape(1), w_in, w_out, sums, after=(outputs,)
    )
    dense_output, dense_query, dense_key, dense_value, vectors = far_add(
        far, after=(grad_expert_in,)
    )
    vectors = (vectors[:4, :128] + vectors[:4, 128:256])[:, :part]
    return (
        outputs.reshape(seq_count, seq_len, width),
        grad_inputs.reshape(seq_count, seq_len, width),
        vectors[0],
        vectors[1],
        dense_query,
        dense_key,
        dense_value,
        dense_output,
        vectors[2],
        vectors[3],
        grad_expert_in[None],
        grad_expert_out[None],
    )


def solution(mesh):
    both = ("rep", "exp")
    placed = (
        P(both, None, None),
        P(both, None, None),
        P(both, None),
        P(both),
    ) + (P(),) * 9 + (P("exp", None, None),) * 2
    return jax.shard_map(
        body,
        mesh=mesh,
        in_specs=placed,
        out_specs=(
            P(both, None, None),
            P(both, None, None),
            P(both),
            P(both),
            P(both, None),
            P(both, None),
            P(both, None),
            P(both, None),
            P(both),
            P(both),
            P("exp", "rep", None),
            P("exp", "rep", None),
        ),
        check_vma=False,
    )
```
